32 devices in a mesh: grp: 2 (over y), gene: 4 (over z), cell: 4 (over x, core).
Axes of the slice: x: 2, y: 2, z: 4, core: 2. Of those that a mesh axis runs over, the one named last changes fastest.
Arguments:
- expression: bfloat16 [4096, 32768], P(('grp', 'cell'), 'gene'), parts along dimension 0, may hold values from -6 to 6
- gene_mask: int32 [4096, 32768], P(('grp', 'cell'), 'gene'), parts along dimension 0, may hold values 0 or 1
- mask_value: bfloat16 [32768], P('gene'), may hold values from -4 to 4
- w_qkv: bfloat16 [32768, 3072], P('gene'), may hold values from -0.03125 to 0.03125
- w_out: bfloat16 [1024, 32768], P(None, 'gene'), may hold values from -1.5 to 1.5
- w_first: bfloat16 [128, 256, 256], P('gene'), may hold values from -0.375 to 0.375
- w_second: bfloat16 [128, 256, 256], P('gene'), may hold values from -0.375 to 0.375
- cotangent: bfloat16 [4096, 32768], P(('grp', 'cell'), 'gene'), parts along dimension 0, may hold values from -6 to 6
Outputs:
- denoised: bfloat16 [4096, 32768], P(('grp', 'cell'), 'gene'), parts along dimension 0
- grad_first: float32 [256, 256, 256], P(('grp', 'gene'), 'cell'), parts along dimension 0
- grad_second: float32 [256, 256, 256], P(('grp', 'gene'), 'cell'), parts along dimension 0
The draws below stay inside these ranges and needn't reach their ends.
There are 2 independent parts, one for each index of `grp`. The reference program is written for one: setup_inputs(seed, part) draws one part's arguments, and reference() takes and returns one part's arrays. A program takes and returns all parts, laid end to end along the dimension named above; an argument that names none is the same for every part. Nothing has to cross between parts.
All inputs are finite; a program needn't handle non-finite values. No bound on the sum of `gene_mask` on one device may be relied on, other than what follows from the above.
Results may differ from the reference program's by a relative error of at most 0.02.
Values may be sent and summed in bfloat16 or wider, within the bound.
No kernel may reach another device: no remote copies, remote signals or barrier semaphores. Data moves between devices by JAX's collectives and lax.ppermute only.
A program may use at most 256 MiB of HBM per device.

```python
import jax
import jax.numpy as jnp
from jax import lax

NB = 128
BS = 256
HEADS = 16
HEAD_DIM = 64
G = 32768
WIDTH = 1024
CELLS = 2048


def plant(entries, stream_key, least, high):
    longest = entries.shape.index(max(entries.shape))
    spots = []
    for shift in (0, 1):
        where = [jax.random.randint(jax.random.fold_in(stream_key, axis), (), 0, length) for axis, length in enumerate(entries.shape)]
        where[longest] = (where[longest] + shift) % entries.shape[longest]
        spots.append(tuple(where))
    return entries.at[spots[0]].set(least).at[spots[1]].set(high)


def shard_levels(stream_key, dims, shards, smallest, largest):
    def one(dim, parts):
        heights = jax.random.uniform(jax.random.fold_in(jax.random.fold_in(stream_key, 6), dim), (parts,), jnp.float32, smallest / len(shards), largest / len(shards))
        return jnp.repeat(jnp.exp(heights), dims[dim] // parts).reshape((-1,) + (1,) * (len(dims) - dim - 1))

    gain = one(*shards[0])
    for cut in shards[1:]:
        gain = gain * one(*cut)
    return gain


def bell_draw(stream_key, shape, width, reach, split=(), kind=jnp.bfloat16):
    result = width * jax.random.normal(stream_key, shape, jnp.float32)
    if split:
        result = result * shard_levels(stream_key, shape, split, -0.22, 0.18)
    return jnp.clip(result, -reach, reach).astype(kind)


def setup_inputs(seed: int = 0, part: int = 0) -> dict:
    streams_of = jax.random.split(jax.random.key(seed), 9)
    part_keys = jax.random.split(jax.random.fold_in(streams_of[8], part), 9)
    return {
        "expression": bell_draw(part_keys[0], (CELLS, G), 1.0, 6.0, ((0, 4), (1, 4))),
        "gene_mask": plant((jax.random.randint(part_keys[1], (CELLS, G), 0, 4) < 1).astype(jnp.int32), jax.random.fold_in(part_keys[1], 1), 0, 1),
        "mask_value": bell_draw(streams_of[2], (G,), 1.0, 4.0, ((0, 4),)),
        "w_qkv": bell_draw(streams_of[3], (G, 3 * WIDTH), G ** -0.5, 0.03125, ((0, 4),)),
        "w_out": bell_draw(streams_of[4], (WIDTH, G), (WIDTH // 64) ** -0.5, 1.5, ((1, 4),)),
        "w_first": bell_draw(streams_of[5], (NB, BS, BS), BS ** -0.5, 0.375, ((0, 4),)),
        "w_second": bell_draw(streams_of[6], (NB, BS, BS), BS ** -0.5, 0.375, ((0, 4),)),
        "cotangent": bell_draw(part_keys[7], (CELLS, G), 1.0, 6.0, ((0, 4), (1, 4))),
    }


def normalize(part, count):
    shaped = part.reshape(count, HEADS, HEAD_DIM)
    meansq = lax.optimization_barrier(jnp.mean(shaped * shaped, axis=-1, keepdims=True))
    return (shaped * lax.rsqrt(meansq + 1e-06)).astype(jnp.bfloat16)

def reference(expression, gene_mask, mask_value, w_qkv, w_out, w_first, w_second, cotangent):
    count = expression.shape[0]
    masked_in = jnp.where(gene_mask == 1, mask_value[None, :], expression)
    qkv = jnp.dot(masked_in, w_qkv, preferred_element_type=jnp.float32)
    queries = normalize(qkv[:, :WIDTH], count)
    keys_normed = normalize(qkv[:, WIDTH:2 * WIDTH], count)
    values_b = qkv[:, 2 * WIDTH:].reshape(count, HEADS, HEAD_DIM).astype(jnp.bfloat16)
    scores = jnp.einsum('qhd,khd->hqk', queries.astype(jnp.float32), keys_normed.astype(jnp.float32)) * HEAD_DIM ** (-0.5)
    expw = jnp.exp(scores).astype(jnp.bfloat16)
    denom = lax.optimization_barrier(jnp.sum(expw.astype(jnp.float32), axis=2))
    numer = jnp.einsum('hqk,khd->qhd', expw.astype(jnp.float32), values_b.astype(jnp.float32))
    attended = (numer / denom.T[:, :, None]).astype(jnp.bfloat16).reshape(count, WIDTH)
    added = jnp.dot(attended, w_out, preferred_element_type=jnp.float32)
    hidden = (masked_in.astype(jnp.float32) + added).astype(jnp.bfloat16)
    blocks = hidden.reshape(count, NB, BS)
    first = jnp.einsum('cbi,bio->cbo', blocks.astype(jnp.float32), w_first.astype(jnp.float32)).astype(jnp.bfloat16)
    permuted = jnp.swapaxes(first, 1, 2).reshape(count, NB, BS)
    mixed = jnp.einsum('cjk,jko->cjo', permuted.astype(jnp.float32), w_second.astype(jnp.float32))
    denoised = (blocks.astype(jnp.float32) + mixed).astype(jnp.bfloat16).reshape(count, NB * BS)
    cot_blocks = cotangent.reshape(count, NB, BS).astype(jnp.float32)
    grad_second = jnp.einsum('cjk,cjo->jko', permuted.astype(jnp.float32), cot_blocks)
    back_perm = jnp.einsum('cjo,jko->cjk', cot_blocks, w_second.astype(jnp.float32)).astype(jnp.bfloat16)
    back_first = jnp.swapaxes(back_perm.reshape(count, BS, NB), 1, 2)
    grad_first = jnp.einsum('cbi,cbo->bio', blocks.astype(jnp.float32), back_first.astype(jnp.float32))
    return (denoised, grad_first, grad_second)
```

```python
import jax
import jax.numpy as jnp
from jax import lax
from jax.experimental import pallas as pl
from jax.experimental.pallas import tpu as pltpu
from jax.sharding import PartitionSpec as P

HEADS = 16
HEAD_DIM = 64
TILE = 16
BF16 = jnp.bfloat16
F32 = jnp.float32


def normalize(part):
    count, columns = part.shape
    shaped = part.reshape(count, columns // HEAD_DIM, HEAD_DIM)
    meansq = jnp.mean(shaped * shaped, axis=-1, keepdims=True)
    return (shaped * lax.rsqrt(meansq + 1e-06)).astype(BF16).reshape(count, columns)


def attend(queries, key_piece, value_piece):
    query_count, columns = queries.shape
    key_count = key_piece.shape[0]
    heads = columns // HEAD_DIM
    query_heads = queries.reshape(query_count, heads, HEAD_DIM)
    key_heads = key_piece.reshape(key_count, heads, HEAD_DIM)
    value_heads = value_piece.reshape(key_count, heads, HEAD_DIM)
    scores = jnp.einsum(
        "qhd,khd->hqk", query_heads, key_heads, preferred_element_type=F32
    ) * HEAD_DIM ** (-0.5)
    expw = jnp.exp(scores).astype(BF16)
    denom = jnp.sum(expw, axis=2, dtype=F32)
    numer = jnp.einsum("hqk,khd->qhd", expw, value_heads, preferred_element_type=F32)
    return (numer / denom.T[:, :, None]).astype(BF16).reshape(query_count, columns)


def on_device_general(
    expression, gene_mask, mask_value, w_qkv, w_out, w_first, w_second, cotangent
):
    groups = lax.axis_size("gene")
    local_blocks = w_first.shape[0]
    block_size = w_first.shape[1]
    block_total = local_blocks * groups
    cell_rows = expression.shape[0]
    masked_in = jnp.where(gene_mask == 1, mask_value[None, :], expression)
    qkv_part = jnp.dot(masked_in, w_qkv, preferred_element_type=F32)
    qkv_full = lax.psum(qkv_part.astype(BF16), "gene").astype(F32)
    columns = qkv_full.shape[1] // 3
    queries = normalize(qkv_full[:, :columns])
    keys_normed = normalize(qkv_full[:, columns : 2 * columns])
    values_b = qkv_full[:, 2 * columns :].astype(BF16)
    attended = attend(
        queries,
        lax.all_gather(keys_normed, "cell", axis=0, tiled=True),
        lax.all_gather(values_b, "cell", axis=0, tiled=True),
    )
    added = jnp.dot(attended, w_out, preferred_element_type=F32)
    hidden = (masked_in.astype(F32) + added).astype(BF16)
    blocks = hidden.reshape(cell_rows, local_blocks, block_size)
    first = jnp.einsum("cbi,bio->cbo", blocks, w_first, preferred_element_type=F32).astype(BF16)
    cot_blocks = cotangent.reshape(cell_rows, local_blocks, block_size)
    back_perm = jnp.einsum(
        "cjo,jko->cjk", cot_blocks, w_second, preferred_element_type=F32
    ).astype(BF16)
    back_send = back_perm.reshape(cell_rows, block_size // groups, block_total)
    received = lax.all_to_all(first, "gene", split_axis=2, concat_axis=1, tiled=True)
    permuted = jnp.swapaxes(received, 1, 2).reshape(cell_rows, local_blocks, block_size)
    mixed = jnp.einsum("cjk,jko->cjo", permuted, w_second, preferred_element_type=F32)
    denoised = (
        (blocks.astype(F32) + mixed).astype(BF16).reshape(cell_rows, local_blocks * block_size)
    )
    grad_second = jnp.einsum("cjk,cjo->jko", permuted, cot_blocks, preferred_element_type=F32)
    back_recv = lax.all_to_all(back_send, "gene", split_axis=2, concat_axis=1, tiled=True)
    back_first = jnp.swapaxes(back_recv, 1, 2)
    grad_first = jnp.einsum("cbi,cbo->bio", blocks, back_first, preferred_element_type=F32)
    first_share, second_share = (
        lax.psum_scatter(
            grad_first.astype(BF16), "cell", scatter_dimension=1, tiled=True
        ).astype(F32),
        lax.psum_scatter(
            grad_second.astype(BF16), "cell", scatter_dimension=1, tiled=True
        ).astype(F32),
    )
    return (denoised, first_share, second_share)


def after(value, *earlier):
    return lax.optimization_barrier((value, *earlier))[0]


def flip(value, axis, bit):
    pairs = [(i, i ^ bit) for i in range(lax.axis_size(axis))]
    return lax.ppermute(value, axis, pairs)


def call(body, me, args, in_specs, outs, out_specs, grid=(1,), scratch=(), aliases=None):
    return pl.pallas_call(
        body,
        out_shape=outs,
        grid_spec=pltpu.PrefetchScalarGridSpec(
            num_scalar_prefetch=1,
            grid=grid,
            in_specs=in_specs,
            out_specs=out_specs,
            scratch_shapes=list(scratch),
        ),
        input_output_aliases=aliases or {},
        compiler_params=pltpu.CompilerParams(vmem_limit_bytes=52 * 2**20),
        cost_estimate=pl.CostEstimate(flops=1, bytes_accessed=1, transcendentals=0),
    )(me, *args)


def spec(shape, place):
    return pl.BlockSpec(shape, place)


def whole(shape):
    return pl.BlockSpec(shape, lambda *_: (0,) * len(shape))


def array(shape, dtype):
    return jax.ShapeDtypeStruct(shape, dtype)


def grid_turn():
    rows = lax.broadcasted_iota(jnp.int32, (TILE * TILE, TILE * TILE), 0)
    columns = lax.broadcasted_iota(jnp.int32, (TILE * TILE, TILE * TILE), 1)
    return ((rows % TILE) * TILE + rows // TILE == columns).astype(BF16)


def turn(matrix, tile):
    rows = tile.shape[-1]
    flat = tile.reshape(TILE * TILE, rows)
    return jnp.dot(matrix, flat, preferred_element_type=F32).astype(BF16).reshape(TILE, TILE, rows)


def back_kernel(me_ref, turn_ref, second_ref, cot_ref, *refs):
    outs, held = refs[:4], refs[4]
    blocks, rows = held.shape[2], held.shape[3]
    pair = held.shape[0] // (TILE // 2)
    at = pl.program_id(0) % (TILE // pair)
    back = lax.dot_general(
        second_ref[0], cot_ref[...], (((1,), (1,)), ((), ())), preferred_element_type=F32
    ).astype(BF16)
    held[pl.ds(at * pair, pair)] = back.reshape(pair, 4, blocks, rows)

    @pl.when(at == TILE // pair - 1)
    def _():
        for bits in range(4):
            there = me_ref[0] ^ bits
            for low in range(0, blocks, TILE):
                outs[bits][low : low + TILE] = turn(
                    turn_ref[...], held[:, there, low : low + TILE, :]
                )


def back_call(me, matrix, w_second, cotangent, part, parts):
    blocks, size, _ = w_second.shape
    rows = cotangent.shape[0]
    pair = size // (4 * blocks)
    count = blocks // parts
    per = TILE // pair
    first = part * count
    piece = array((blocks, count * pair, rows), BF16)
    return call(
        back_kernel,
        me,
        (matrix, w_second, cotangent),
        [
            whole(matrix.shape),
            spec((1, size, size), lambda j, _: (first + j, 0, 0)),
            spec((rows, size), lambda j, _: (0, first + j)),
        ],
        [piece] * 4,
        [spec((blocks, TILE, rows), lambda j, _: (0, j // per, 0))] * 4,
        grid=(count,),
        scratch=[pltpu.VMEM((TILE, 4, blocks, rows), BF16)],
    )


def project_kernel(me_ref, value_ref, mask_ref, fill_ref, *refs):
    weights, (masked_ref, send_ref, keep_ref), sums = refs[:3], refs[3:6], refs[6:]
    step = pl.program_id(0)
    masked = jnp.where(
        mask_ref[...] == 1, fill_ref[...].astype(F32), value_ref[...].astype(F32)
    ).astype(BF16)
    masked_ref[...] = masked

    @pl.when(step == 0)
    def _():
        for total in sums:
            total[...] = jnp.zeros_like(total)

    for weight, total in zip(weights, sums):
        total[...] += jnp.dot(masked, weight[...], preferred_element_type=F32)

    @pl.when(step == pl.num_programs(0) - 1)
    def _():
        share = sums[0].shape[1] // 4
        for out, flips in ((send_ref, (1, 3)), (keep_ref, (0, 2))):
            for slot, bits in enumerate(flips):
                columns = pl.ds(pl.multiple_of((me_ref[0] ^ bits) * share, share), share)
                for kind, total in enumerate(sums):
                    out[slot, :, kind * share : (kind + 1) * share] = total[:, columns].astype(
                        out.dtype
                    )


def project_call(me, expression, gene_mask, mask_value, w_qkv):
    rows, genes = expression.shape
    width = w_qkv.shape[1] // 3
    depth = min(genes, 512)
    wide = spec((rows, depth), lambda i, _: (0, i))
    shape = (2, rows, 3 * width // 4)
    return call(
        project_kernel,
        me,
        (expression, gene_mask, mask_value.reshape(1, genes), w_qkv, w_qkv, w_qkv),
        [
            wide,
            wide,
            spec((1, depth), lambda i, _: (0, i)),
            spec((depth, width), lambda i, _: (i, 0)),
            spec((depth, width), lambda i, _: (i, 1)),
            spec((depth, width), lambda i, _: (i, 2)),
        ],
        [array((rows, genes), BF16), array(shape, BF16), array(shape, F32)],
        [wide, whole(shape), whole(shape)],
        grid=(genes // depth,),
        scratch=[pltpu.VMEM((rows, width), F32)] * 3,
    )


def add_kernel(_, keep_ref, came_ref, mine_ref, other_ref):
    mine_ref[...] = keep_ref[0] + came_ref[0].astype(F32)
    other_ref[...] = (keep_ref[1] + came_ref[1].astype(F32)).astype(BF16)


def add_call(me, keep, came):
    shape = keep.shape
    return call(
        add_kernel,
        me,
        (keep, came),
        [whole(shape), whole(shape)],
        [array(shape[1:], F32), array(shape[1:], BF16)],
        [whole(shape[1:])] * 2,
    )


def normalize_heads(part):
    columns = part.shape[1]
    heads = [lax.broadcasted_iota(jnp.int32, (columns, columns), d) // HEAD_DIM for d in (0, 1)]
    same = (heads[0] == heads[1]).astype(F32)
    sums = jnp.dot(
        part * part, same, precision=lax.Precision.HIGHEST, preferred_element_type=F32
    )
    return (part * lax.rsqrt(sums * (1.0 / HEAD_DIM) + 1e-06)).astype(BF16)


def split_kernel(_, mine_ref, came_ref, query_ref, out_ref):
    total = mine_ref[...] + came_ref[...].astype(F32)
    share = total.shape[1] // 3
    query_ref[...] = normalize_heads(total[:, :share])
    out_ref[:, :share] = normalize_heads(total[:, share : 2 * share])
    out_ref[:, share:] = total[:, 2 * share :].astype(BF16)


def split_call(me, mine, came):
    rows, columns = mine.shape
    shapes = ((rows, columns // 3), (rows, 2 * columns // 3))
    return call(
        split_kernel,
        me,
        (mine, came),
        [whole(mine.shape)] * 2,
        [array(shape, BF16) for shape in shapes],
        [whole(shape) for shape in shapes],
    )


def attend_kernel(_, query_ref, *refs):
    pieces, out_ref = refs[:-1], refs[-1]
    queries = query_ref[...]
    rows, share = queries.shape
    head_of = lax.broadcasted_iota(jnp.int32, (rows, share), 1) // HEAD_DIM
    out = jnp.zeros((rows, share), F32)
    for head in range(share // HEAD_DIM):
        query = jnp.where(head_of == head, queries.astype(F32) * HEAD_DIM**-0.5, 0.0).astype(BF16)
        numer = jnp.zeros((rows, share), F32)
        denom = jnp.zeros((rows, 1), F32)
        for piece in pieces:
            scores = lax.dot_general(
                query, piece[:, :share], (((1,), (1,)), ((), ())), preferred_element_type=F32
            )
            expw = jnp.exp(scores).astype(BF16)
            denom += jnp.sum(expw.astype(F32), axis=1, keepdims=True)
            numer += jnp.dot(expw, piece[:, share:], preferred_element_type=F32)
        out = jnp.where(head_of == head, numer / denom, out)
    out_ref[...] = out.astype(BF16)


def attend_call(me, queries, pieces):
    rows, share = queries.shape
    some = rows // 2
    part = spec((some, share), lambda i, _: (i, 0))
    return call(
        attend_kernel,
        me,
        (queries, *pieces),
        [part] + [whole(piece.shape) for piece in pieces],
        array((rows, share), BF16),
        part,
        grid=(2,),
    )


def first_kernel(me_ref, turn_ref, own, near, far, rest, w_out_ref, masked_ref, wf_ref, *refs):
    hidden_ref, outs, gathered, held = refs[0], refs[1:-2], refs[-2], refs[-1]
    block = pl.program_id(0)
    share = own.shape[1]

    @pl.when(block == 0)
    def _():
        for bits, piece in enumerate((own, near, far, rest)):
            place = pl.multiple_of((me_ref[0] ^ bits) * share, share)
            gathered[:, pl.ds(place, share)] = piece[...]

    added = jnp.dot(gathered[...], w_out_ref[...], preferred_element_type=F32)
    hidden = (masked_ref[...].astype(F32) + added).astype(BF16)
    hidden_ref[...] = hidden
    held[block % TILE] = lax.dot_general(
        wf_ref[0], hidden, (((1,), (1,)), ((), ())), preferred_element_type=F32
    ).astype(BF16)

    @pl.when(block % TILE == TILE - 1)
    def _():
        deeps = [out.shape[0] for out in outs[: len(outs) // 4]]
        deep = sum(deeps)
        for bits in range(4):
            there = me_ref[0] ^ bits
            for low in range(0, deep, TILE):
                start = pl.multiple_of(there * deep + low, TILE)
                tile = turn(turn_ref[...], held[:, pl.ds(start, TILE), :])
                for chunk, count in enumerate(deeps):
                    begin = sum(deeps[:chunk])
                    least, most = max(begin, low), min(begin + count, low + TILE)
                    if least < most:
                        outs[bits * len(deeps) + chunk][least - begin : most - begin] = tile[
                            least - low : most - low
                        ]


def first_call(me, matrix, attended, w_out, masked, w_first_t, deeps):
    blocks, size, _ = w_first_t.shape
    rows, genes = masked.shape
    width = w_out.shape[0]
    wide = spec((rows, size), lambda b, _: (0, b))
    chunks = len(deeps)
    got = call(
        first_kernel,
        me,
        (matrix, *attended, w_out, masked, w_first_t),
        [whole(matrix.shape)]
        + [whole(part.shape) for part in attended]
        + [
            spec((width, size), lambda b, _: (0, b)),
            wide,
            spec((1, size, size), lambda b, _: (b, 0, 0)),
        ],
        [array((rows, genes), BF16)] + [array((deep, blocks, rows), BF16) for deep in deeps] * 4,
        [wide] + [spec((deep, TILE, rows), lambda b, _: (0, b // TILE, 0)) for deep in deeps] * 4,
        grid=(blocks,),
        scratch=[pltpu.VMEM((rows, width), BF16), pltpu.VMEM((TILE, size, rows), BF16)],
    )
    return got[0], [[got[1 + s * chunks + t] for s in range(4)] for t in range(chunks)]


def second_kernel(me_ref, *refs):
    pieces = refs[:4]
    w_ref, cot_ref, hidden_ref = refs[4:7]
    out_ref, grad_ref, held = refs[-3:]
    for bits, piece in enumerate(pieces):
        held[:, me_ref[0] ^ bits] = piece[...]
    size = w_ref.shape[1]
    permuted = held[...].reshape(size, held.shape[3])
    grad_ref[0] = jnp.dot(permuted, cot_ref[...], preferred_element_type=F32).astype(BF16)
    mixed = lax.dot_general(
        permuted, w_ref[0], (((0,), (0,)), ((), ())), preferred_element_type=F32
    )
    out_ref[...] = (hidden_ref[...].astype(F32) + mixed).astype(BF16)


def second_call(me, pieces, w_second, cotangent, hidden, denoised, start):
    blocks, size, _ = w_second.shape
    deep, _, rows = pieces[0].shape
    pair = size // (4 * blocks)
    count = deep // pair
    wide = spec((rows, size), lambda j, _: (0, start + j))
    square = spec((1, size, size), lambda j, _: (start + j, 0, 0))
    args = [*pieces, w_second, cotangent, hidden]
    in_specs = [spec((pair, blocks, rows), lambda j, _: (j, 0, 0))] * 4 + [square, wide, wide]
    aliases = {}
    if denoised is not None:
        args.append(denoised)
        in_specs.append(pl.BlockSpec(memory_space=pl.ANY))
        aliases = {len(args): 0}
    return call(
        second_kernel,
        me,
        args,
        in_specs,
        [array(hidden.shape, BF16), array((count, size, size), BF16)],
        [wide, spec((1, size, size), lambda j, _: (j, 0, 0))],
        grid=(count,),
        scratch=[pltpu.VMEM((pair, 4, blocks, rows), BF16)],
        aliases=aliases,
    )


def grad_first_kernel(me_ref, *refs):
    pieces, hidden_ref, out_ref, held = refs[:-3], refs[-3], refs[-2], refs[-1]
    for half in range(len(pieces) // 4):
        for bits in range(4):
            held[me_ref[0] ^ bits, half] = pieces[half * 4 + bits][0]
    back = held[...].reshape(-1, held.shape[3])
    grad = jnp.dot(back, hidden_ref[...], preferred_element_type=F32)
    out_ref[0] = grad.T.astype(BF16)


def grad_first_call(me, pieces, hidden, size):
    blocks, deep, rows = pieces[0].shape
    return call(
        grad_first_kernel,
        me,
        (*pieces, hidden),
        [spec((1, deep, rows), lambda b, _: (b, 0, 0))] * len(pieces)
        + [spec((rows, size), lambda b, _: (0, b))],
        array((blocks, size, size), BF16),
        spec((1, size, size), lambda b, _: (b, 0, 0)),
        grid=(blocks,),
        scratch=[pltpu.VMEM((4, len(pieces) // 4, deep, rows), BF16)],
    )


def scatter_cells(grad):
    return lax.psum_scatter(grad, "cell", scatter_dimension=1, tiled=True)


def scatter_cells_halving(grad):
    me = lax.axis_index("cell")
    count, size, columns = grad.shape
    rows = grad.reshape(count, 4, size // 4, columns)

    def part(bits):
        return lax.dynamic_index_in_dim(rows, me ^ bits, 1, keepdims=False)

    came = flip(jnp.stack([part(1), part(3)]), "cell", 1).astype(F32)
    other = (part(2).astype(F32) + came[1]).astype(BF16)
    return part(0).astype(F32) + came[0] + flip(other, "cell", 2).astype(F32)


def on_device_four(expression, gene_mask, mask_value, w_qkv, w_out, w_first, w_second, cotangent):
    me = lax.axis_index("gene").astype(jnp.int32).reshape(1)
    blocks, size, _ = w_first.shape
    parts = 4
    deep = size // 4
    deeps = [deep // 4] * 3 + [deep // 8] * 2
    matrix = grid_turn()
    sends, back = [None] * parts, [[None] * 4 for _ in range(parts)]

    def prepare(part, *earlier):
        sends[part] = back_call(me, matrix, w_second, after(cotangent, *earlier), part, parts)
        back[part][0] = sends[part][0]

    def begin(part, bits, *earlier):
        back[part][bits] = flip(after(sends[part][bits], *earlier), "gene", bits)
        return back[part][bits]

    prepare(0)
    first_part = [begin(0, bits) for bits in (3, 2, 1)]
    masked, send, keep = project_call(
        me, after(expression, sends[0][0]), gene_mask, mask_value, w_qkv
    )
    came = flip(after(send, *first_part), "gene", 1)
    prepare(1, send)
    beside_sum = [begin(1, 2), begin(1, 3)]
    mine, other = add_call(me, keep, after(came, *beside_sum))
    last = flip(other, "gene", 2)
    prepare(2, other)
    prepare(3, sends[2][0])
    w_first_t = jnp.swapaxes(after(w_first, other), 1, 2)
    beside_sum = [begin(1, 1, other)]
    queries, key_value = split_call(
        me, mine, after(last, *beside_sum, sends[3][0], w_first_t)
    )
    across = flip(key_value, "cell", 2)
    beside = flip(key_value, "cell", 1)
    corner = flip(across, "cell", 1)
    beside_keys = [begin(2, 2, key_value)]
    queries = after(queries, *beside_keys, beside, across, corner)
    attended = attend_call(me, queries, (key_value, beside, across, corner))
    attended = after(attended, begin(2, 3, queries))
    far = flip(attended, "gene", 2)
    near = flip(attended, "gene", 1)
    rest = flip(far, "gene", 1)
    beside_heads = [begin(2, 1, attended), begin(3, 1, attended)]
    hidden, first = first_call(
        me,
        matrix,
        (attended, near, far, after(rest, *beside_heads)),
        w_out,
        masked,
        w_first_t,
        deeps,
    )
    for bits in (2, 3):
        begin(3, bits, rest)

    got = []
    for t in range(len(deeps)):
        earlier = got[-1] if t else back[3]
        got.append(first[t][:1])
        for bits in (1, 2, 3):
            ready = (earlier[bits],) if t else earlier
            got[t].append(flip(after(first[t][bits], *ready), "gene", bits))
    grad_first = grad_first_call(me, sum(back, []), hidden, size)
    first_share = scatter_cells(grad_first)

    denoised, shares = None, []
    for t in range(len(deeps)):
        pieces = [after(got[t][0], grad_first), *got[t][1:]]
        start = sum(deeps[:t]) * blocks // deep
        denoised, grad = second_call(me, pieces, w_second, cotangent, hidden, denoised, start)
        if deeps[t] * 4 < deep:
            shares.append(scatter_cells_halving(grad))
        else:
            shares.append(scatter_cells(grad).astype(F32))
    return (denoised, first_share.astype(F32), jnp.concatenate(shares, axis=0))


def solution(mesh):
    placed = (
        P(("grp", "cell"), "gene"),
        P(("grp", "cell"), "gene"),
        P("gene"),
        P("gene", None),
        P(None, "gene"),
        P("gene", None, None),
        P("gene", None, None),
        P(("grp", "cell"), "gene"),
    )
    four = mesh.shape["gene"] == 4 and mesh.shape["cell"] == 4
    return jax.shard_map(
        on_device_four if four else on_device_general,
        mesh=mesh,
        in_specs=placed,
        out_specs=(
            P(("grp", "cell"), "gene"),
            P(("grp", "gene"), "cell", None),
            P(("grp", "gene"), "cell", None),
        ),
        check_vma=False,
    )
```

```python
import math

import jax
import jax.numpy as jnp
from jax import lax
from jax.experimental import pallas as pl
from jax.experimental.pallas import tpu as pltpu
from jax.sharding import PartitionSpec as P

HEADS = 16
HEAD_DIM = 64
TILE = 16
BF16 = jnp.bfloat16
F32 = jnp.float32


def normalize(part):
    count, columns = part.shape
    shaped = part.reshape(count, columns // HEAD_DIM, HEAD_DIM)
    meansq = jnp.mean(shaped * shaped, axis=-1, keepdims=True)
    return (shaped * lax.rsqrt(meansq + 1e-06)).astype(BF16).reshape(count, columns)


def attend(queries, key_piece, value_piece):
    query_count, columns = queries.shape
    key_count = key_piece.shape[0]
    heads = columns // HEAD_DIM
    query_heads = queries.reshape(query_count, heads, HEAD_DIM)
    key_heads = key_piece.reshape(key_count, heads, HEAD_DIM)
    value_heads = value_piece.reshape(key_count, heads, HEAD_DIM)
    scores = jnp.einsum(
        "qhd,khd->hqk", query_heads, key_heads, preferred_element_type=F32
    ) * HEAD_DIM ** (-0.5)
    expw = jnp.exp(scores).astype(BF16)
    denom = jnp.sum(expw, axis=2, dtype=F32)
    numer = jnp.einsum("hqk,khd->qhd", expw, value_heads, preferred_element_type=F32)
    return (numer / denom.T[:, :, None]).astype(BF16).reshape(query_count, columns)


def on_device_general(
    expression, gene_mask, mask_value, w_qkv, w_out, w_first, w_second, cotangent
):
    groups = lax.axis_size("gene")
    local_blocks = w_first.shape[0]
    block_size = w_first.shape[1]
    block_total = local_blocks * groups
    cell_rows = expression.shape[0]
    masked_in = jnp.where(gene_mask == 1, mask_value[None, :], expression)
    qkv_part = jnp.dot(masked_in, w_qkv, preferred_element_type=F32)
    qkv_full = lax.psum(qkv_part.astype(BF16), "gene").astype(F32)
    columns = qkv_full.shape[1] // 3
    queries = normalize(qkv_full[:, :columns])
    keys_normed = normalize(qkv_full[:, columns : 2 * columns])
    values_b = qkv_full[:, 2 * columns :].astype(BF16)
    attended = attend(
        queries,
        lax.all_gather(keys_normed, "cell", axis=0, tiled=True),
        lax.all_gather(values_b, "cell", axis=0, tiled=True),
    )
    added = jnp.dot(attended, w_out, preferred_element_type=F32)
    hidden = (masked_in.astype(F32) + added).astype(BF16)
    blocks = hidden.reshape(cell_rows, local_blocks, block_size)
    first = jnp.einsum("cbi,bio->cbo", blocks, w_first, preferred_element_type=F32).astype(BF16)
    cot_blocks = cotangent.reshape(cell_rows, local_blocks, block_size)
    back_perm = jnp.einsum(
        "cjo,jko->cjk", cot_blocks, w_second, preferred_element_type=F32
    ).astype(BF16)
    back_send = back_perm.reshape(cell_rows, block_size // groups, block_total)
    received = lax.all_to_all(first, "gene", split_axis=2, concat_axis=1, tiled=True)
    permuted = jnp.swapaxes(received, 1, 2).reshape(cell_rows, local_blocks, block_size)
    mixed = jnp.einsum("cjk,jko->cjo", permuted, w_second, preferred_element_type=F32)
    denoised = (
        (blocks.astype(F32) + mixed).astype(BF16).reshape(cell_rows, local_blocks * block_size)
    )
    grad_second = jnp.einsum("cjk,cjo->jko", permuted, cot_blocks, preferred_element_type=F32)
    back_recv = lax.all_to_all(back_send, "gene", split_axis=2, concat_axis=1, tiled=True)
    back_first = jnp.swapaxes(back_recv, 1, 2)
    grad_first = jnp.einsum("cbi,cbo->bio", blocks, back_first, preferred_element_type=F32)
    first_share, second_share = (
        lax.psum_scatter(
            grad_first.astype(BF16), "cell", scatter_dimension=1, tiled=True
        ).astype(F32),
        lax.psum_scatter(
            grad_second.astype(BF16), "cell", scatter_dimension=1, tiled=True
        ).astype(F32),
    )
    return (denoised, first_share, second_share)


def after(value, *earlier):
    return lax.optimization_barrier((value, *earlier))[0]


def flip(value, axis, bit):
    pairs = [(i, i ^ bit) for i in range(lax.axis_size(axis))]
    return lax.ppermute(value, axis, pairs)


def call(body, me, args, in_specs, outs, out_specs, grid=(1,), scratch=(), aliases=None):
    return pl.pallas_call(
        body,
        out_shape=outs,
        grid_spec=pltpu.PrefetchScalarGridSpec(
            num_scalar_prefetch=1,
            grid=grid,
            in_specs=in_specs,
            out_specs=out_specs,
            scratch_shapes=list(scratch),
        ),
        input_output_aliases=aliases or {},
        compiler_params=pltpu.CompilerParams(vmem_limit_bytes=52 * 2**20),
        cost_estimate=pl.CostEstimate(flops=1, bytes_accessed=1, transcendentals=0),
    )(me, *args)


def spec(shape, place):
    return pl.BlockSpec(shape, place)


def whole(shape):
    return pl.BlockSpec(shape, lambda *_: (0,) * len(shape))


def array(shape, dtype):
    return jax.ShapeDtypeStruct(shape, dtype)


def grid_turn():
    rows = lax.broadcasted_iota(jnp.int32, (TILE * TILE, TILE * TILE), 0)
    columns = lax.broadcasted_iota(jnp.int32, (TILE * TILE, TILE * TILE), 1)
    return ((rows % TILE) * TILE + rows // TILE == columns).astype(BF16)


def turn(matrix, tile):
    rows = tile.shape[-1]
    flat = tile.reshape(TILE * TILE, rows)
    return jnp.dot(matrix, flat, preferred_element_type=F32).astype(BF16).reshape(TILE, TILE, rows)


def back_kernel(me_ref, turn_ref, second_ref, cot_ref, *refs):
    outs, held = refs[:4], refs[4]
    blocks, rows = held.shape[2], held.shape[3]
    pair = held.shape[0] // (TILE // 2)
    at = pl.program_id(0) % (TILE // pair)
    back = lax.dot_general(
        second_ref[0], cot_ref[...], (((1,), (1,)), ((), ())), preferred_element_type=F32
    ).astype(BF16)
    held[pl.ds(at * pair, pair)] = back.reshape(pair, 4, blocks, rows)

    @pl.when(at == TILE // pair - 1)
    def _():
        for bits in range(4):
            there = me_ref[0] ^ bits
            for low in range(0, blocks, TILE):
                outs[bits][low : low + TILE] = turn(
                    turn_ref[...], held[:, there, low : low + TILE, :]
                )


def back_call(me, matrix, w_second, cotangent, part, parts):
    blocks, size, _ = w_second.shape
    rows = cotangent.shape[0]
    pair = size // (4 * blocks)
    count = blocks // parts
    per = TILE // pair
    first = part * count
    piece = array((blocks, count * pair, rows), BF16)
    return call(
        back_kernel,
        me,
        (matrix, w_second, cotangent),
        [
            whole(matrix.shape),
            spec((1, size, size), lambda j, _: (first + j, 0, 0)),
            spec((rows, size), lambda j, _: (0, first + j)),
        ],
        [piece] * 4,
        [spec((blocks, TILE, rows), lambda j, _: (0, j // per, 0))] * 4,
        grid=(count,),
        scratch=[pltpu.VMEM((TILE, 4, blocks, rows), BF16)],
    )


def project_kernel(me_ref, value_ref, mask_ref, fill_ref, *refs):
    weights, (masked_ref, send_ref, keep_ref), sums = refs[:3], refs[3:6], refs[6:]
    step = pl.program_id(0)
    masked = jnp.where(
        mask_ref[...] == 1, fill_ref[...].astype(F32), value_ref[...].astype(F32)
    ).astype(BF16)
    masked_ref[...] = masked

    @pl.when(step == 0)
    def _():
        for total in sums:
            total[...] = jnp.zeros_like(total)

    for weight, total in zip(weights, sums):
        total[...] += jnp.dot(masked, weight[...], preferred_element_type=F32)

    @pl.when(step == pl.num_programs(0) - 1)
    def _():
        share = sums[0].shape[1] // 4
        for out, flips in ((send_ref, (1, 3)), (keep_ref, (0, 2))):
            for slot, bits in enumerate(flips):
                columns = pl.ds(pl.multiple_of((me_ref[0] ^ bits) * share, share), share)
                for kind, total in enumerate(sums):
                    out[slot, :, kind * share : (kind + 1) * share] = total[:, columns].astype(
                        out.dtype
                    )


def project_call(me, expression, gene_mask, mask_value, w_qkv):
    rows, genes = expression.shape
    width = w_qkv.shape[1] // 3
    depth = min(genes, 512)
    wide = spec((rows, depth), lambda i, _: (0, i))
    shape = (2, rows, 3 * width // 4)
    return call(
        project_kernel,
        me,
        (expression, gene_mask, mask_value.reshape(1, genes), w_qkv, w_qkv, w_qkv),
        [
            wide,
            wide,
            spec((1, depth), lambda i, _: (0, i)),
            spec((depth, width), lambda i, _: (i, 0)),
            spec((depth, width), lambda i, _: (i, 1)),
            spec((depth, width), lambda i, _: (i, 2)),
        ],
        [array((rows, genes), BF16), array(shape, BF16), array(shape, F32)],
        [wide, whole(shape), whole(shape)],
        grid=(genes // depth,),
        scratch=[pltpu.VMEM((rows, width), F32)] * 3,
    )


def store_quarters(me, held, send_ref, keep_ref):
    quarter = held.shape[0] // 4
    for out, flips in ((send_ref, (1, 3)), (keep_ref, (0, 2))):
        for slot, bits in enumerate(flips):
            start = pl.multiple_of((me ^ bits) * quarter, quarter)
            out[slot, 0] = held[pl.ds(start, quarter), :].astype(out.dtype)


def quarter_outs(count, size):
    shape = (2, count, size // 4, size)
    place = spec((2, 1, size // 4, size), lambda j, _: (0, j, 0, 0))
    return [array(shape, BF16), array(shape, F32)], [place, place]


def add_kernel(_, keep_ref, came_ref, mine_ref, other_ref):
    mine_ref[...] = keep_ref[0] + came_ref[0].astype(F32)
    other_ref[...] = (keep_ref[1] + came_ref[1].astype(F32)).astype(BF16)


def add_call(me, keep, came):
    shape = keep.shape
    return call(
        add_kernel,
        me,
        (keep, came),
        [whole(shape), whole(shape)],
        [array(shape[1:], F32), array(shape[1:], BF16)],
        [whole(shape[1:])] * 2,
    )


def normalize_heads(part):
    columns = part.shape[1]
    heads = [lax.broadcasted_iota(jnp.int32, (columns, columns), d) // HEAD_DIM for d in (0, 1)]
    same = (heads[0] == heads[1]).astype(F32)
    sums = jnp.dot(
        part * part, same, precision=lax.Precision.HIGHEST, preferred_element_type=F32
    )
    return (part * lax.rsqrt(sums * (1.0 / HEAD_DIM) + 1e-06)).astype(BF16)


def finish_kernel(_, mine_ref, came_ref, *refs):
    refs[-1][...] = mine_ref[...] + came_ref[...].astype(F32)


def finish_call(me, mine, came, total, start, blocks):
    count, quarter, size = mine.shape
    step = math.gcd(count, start) if start else count
    args = [mine, came]
    in_specs = [spec((step, quarter, size), lambda i, _: (i, 0, 0))] * 2
    aliases = {}
    if total is not None:
        args.append(total)
        in_specs.append(pl.BlockSpec(memory_space=pl.ANY))
        aliases = {len(args): 0}
    return call(
        finish_kernel,
        me,
        args,
        in_specs,
        array((blocks, quarter, size), F32),
        spec((step, quarter, size), lambda i, _: (start // step + i, 0, 0)),
        grid=(count // step,),
        aliases=aliases,
    )


def split_kernel(_, mine_ref, came_ref, query_ref, out_ref):
    total = mine_ref[...] + came_ref[...].astype(F32)
    share = total.shape[1] // 3
    query_ref[...] = normalize_heads(total[:, :share])
    out_ref[:, :share] = normalize_heads(total[:, share : 2 * share])
    out_ref[:, share:] = total[:, 2 * share :].astype(BF16)


def split_call(me, mine, came):
    rows, columns = mine.shape
    shapes = ((rows, columns // 3), (rows, 2 * columns // 3))
    return call(
        split_kernel,
        me,
        (mine, came),
        [whole(mine.shape)] * 2,
        [array(shape, BF16) for shape in shapes],
        [whole(shape) for shape in shapes],
    )


def attend_kernel(_, query_ref, *refs):
    pieces, out_ref = refs[:-1], refs[-1]
    queries = query_ref[...]
    rows, share = queries.shape
    head_of = lax.broadcasted_iota(jnp.int32, (rows, share), 1) // HEAD_DIM
    out = jnp.zeros((rows, share), F32)
    for head in range(share // HEAD_DIM):
        query = jnp.where(head_of == head, queries.astype(F32) * HEAD_DIM**-0.5, 0.0).astype(BF16)
        numer = jnp.zeros((rows, share), F32)
        denom = jnp.zeros((rows, 1), F32)
        for piece in pieces:
            scores = lax.dot_general(
                query, piece[:, :share], (((1,), (1,)), ((), ())), preferred_element_type=F32
            )
            expw = jnp.exp(scores).astype(BF16)
            denom += jnp.sum(expw.astype(F32), axis=1, keepdims=True)
            numer += jnp.dot(expw, piece[:, share:], preferred_element_type=F32)
        out = jnp.where(head_of == head, numer / denom, out)
    out_ref[...] = out.astype(BF16)


def attend_call(me, queries, pieces):
    rows, share = queries.shape
    some = rows // 2
    part = spec((some, share), lambda i, _: (i, 0))
    return call(
        attend_kernel,
        me,
        (queries, *pieces),
        [part] + [whole(piece.shape) for piece in pieces],
        array((rows, share), BF16),
        part,
        grid=(2,),
    )


def first_kernel(me_ref, turn_ref, own, near, far, rest, w_out_ref, masked_ref, wf_ref, *refs):
    hidden_ref, outs, gathered, held = refs[0], refs[1:-2], refs[-2], refs[-1]
    block = pl.program_id(0)
    share = own.shape[1]

    @pl.when(block == 0)
    def _():
        for bits, piece in enumerate((own, near, far, rest)):
            place = pl.multiple_of((me_ref[0] ^ bits) * share, share)
            gathered[:, pl.ds(place, share)] = piece[...]

    added = jnp.dot(gathered[...], w_out_ref[...], preferred_element_type=F32)
    hidden = (masked_ref[...].astype(F32) + added).astype(BF16)
    hidden_ref[...] = hidden
    held[block % TILE] = lax.dot_general(
        wf_ref[0], hidden, (((1,), (1,)), ((), ())), preferred_element_type=F32
    ).astype(BF16)

    @pl.when(block % TILE == TILE - 1)
    def _():
        deeps = [out.shape[0] for out in outs[: len(outs) // 4]]
        deep = sum(deeps)
        for bits in range(4):
            there = me_ref[0] ^ bits
            for low in range(0, deep, TILE):
                start = pl.multiple_of(there * deep + low, TILE)
                tile = turn(turn_ref[...], held[:, pl.ds(start, TILE), :])
                for chunk, count in enumerate(deeps):
                    begin = sum(deeps[:chunk])
                    least, most = max(begin, low), min(begin + count, low + TILE)
                    if least < most:
                        outs[bits * len(deeps) + chunk][least - begin : most - begin] = tile[
                            least - low : most - low
                        ]


def first_call(me, matrix, attended, w_out, masked, w_first_t, deeps):
    blocks, size, _ = w_first_t.shape
    rows, genes = masked.shape
    width = w_out.shape[0]
    wide = spec((rows, size), lambda b, _: (0, b))
    chunks = len(deeps)
    got = call(
        first_kernel,
        me,
        (matrix, *attended, w_out, masked, w_first_t),
        [whole(matrix.shape)]
        + [whole(part.shape) for part in attended]
        + [
            spec((width, size), lambda b, _: (0, b)),
            wide,
            spec((1, size, size), lambda b, _: (b, 0, 0)),
        ],
        [array((rows, genes), BF16)] + [array((deep, blocks, rows), BF16) for deep in deeps] * 4,
        [wide] + [spec((deep, TILE, rows), lambda b, _: (0, b // TILE, 0)) for deep in deeps] * 4,
        grid=(blocks,),
        scratch=[pltpu.VMEM((rows, width), BF16), pltpu.VMEM((TILE, size, rows), BF16)],
    )
    return got[0], [[got[1 + s * chunks + t] for s in range(4)] for t in range(chunks)]


def second_kernel(me_ref, *refs):
    pieces = refs[:4]
    w_ref, cot_ref, hidden_ref = refs[4:7]
    out_ref, send_ref, keep_ref, held, square = refs[-5:]
    for bits, piece in enumerate(pieces):
        held[:, me_ref[0] ^ bits] = piece[...]
    size = w_ref.shape[1]
    permuted = held[...].reshape(size, held.shape[3])
    square[...] = jnp.dot(permuted, cot_ref[...], preferred_element_type=F32)
    store_quarters(me_ref[1], square, send_ref, keep_ref)
    mixed = lax.dot_general(
        permuted, w_ref[0], (((0,), (0,)), ((), ())), preferred_element_type=F32
    )
    out_ref[...] = (hidden_ref[...].astype(F32) + mixed).astype(BF16)


def second_call(me, pieces, w_second, cotangent, hidden, denoised, start):
    blocks, size, _ = w_second.shape
    deep, _, rows = pieces[0].shape
    pair = size // (4 * blocks)
    count = deep // pair
    wide = spec((rows, size), lambda j, _: (0, start + j))
    square = spec((1, size, size), lambda j, _: (start + j, 0, 0))
    args = [*pieces, w_second, cotangent, hidden]
    in_specs = [spec((pair, blocks, rows), lambda j, _: (j, 0, 0))] * 4 + [square, wide, wide]
    quarters = quarter_outs(count, size)
    aliases = {}
    if denoised is not None:
        args.append(denoised)
        in_specs.append(pl.BlockSpec(memory_space=pl.ANY))
        aliases = {len(args): 0}
    return call(
        second_kernel,
        me,
        args,
        in_specs,
        [array(hidden.shape, BF16), *quarters[0]],
        [wide, *quarters[1]],
        grid=(count,),
        scratch=[pltpu.VMEM((pair, 4, blocks, rows), BF16), pltpu.VMEM((size, size), F32)],
        aliases=aliases,
    )


def grad_first_kernel(me_ref, *refs):
    pieces, (hidden_ref, send_ref, keep_ref, held, square) = refs[:-5], refs[-5:]
    for half in range(len(pieces) // 4):
        for bits in range(4):
            held[me_ref[0] ^ bits, half] = pieces[half * 4 + bits][0]
    back = held[...].reshape(-1, held.shape[3])
    square[...] = jnp.dot(back, hidden_ref[...], preferred_element_type=F32).T
    store_quarters(me_ref[1], square, send_ref, keep_ref)


def grad_first_call(me, pieces, hidden, size):
    blocks, deep, rows = pieces[0].shape
    return call(
        grad_first_kernel,
        me,
        (*pieces, hidden),
        [spec((1, deep, rows), lambda b, _: (b, 0, 0))] * len(pieces)
        + [spec((rows, size), lambda b, _: (0, b))],
        *quarter_outs(blocks, size),
        grid=(blocks,),
        scratch=[
            pltpu.VMEM((4, len(pieces) // 4, deep, rows), BF16),
            pltpu.VMEM((size, size), F32),
        ],
    )


def on_device_four(expression, gene_mask, mask_value, w_qkv, w_out, w_first, w_second, cotangent):
    me = jnp.stack([lax.axis_index("gene"), lax.axis_index("cell")]).astype(jnp.int32)
    blocks, size, _ = w_first.shape
    parts = 4
    deep = size // 4
    deeps = [deep // 4] * 3 + [3 * deep // 16, deep // 16]
    matrix = grid_turn()
    sends, back = [None] * parts, [[None] * 4 for _ in range(parts)]

    def prepare(part, *earlier):
        sends[part] = back_call(me, matrix, w_second, after(cotangent, *earlier), part, parts)
        back[part][0] = sends[part][0]

    def begin(part, bits, *earlier):
        back[part][bits] = flip(after(sends[part][bits], *earlier), "gene", bits)
        return back[part][bits]

    prepare(0)
    first_part = [begin(0, bits) for bits in (3, 2, 1)]
    masked, send, keep = project_call(
        me, after(expression, sends[0][0]), gene_mask, mask_value, w_qkv
    )
    came = flip(after(send, *first_part), "gene", 1)
    prepare(1, send)
    beside_sum = [begin(1, 2), begin(1, 3)]
    mine, other = add_call(me, keep, after(came, *beside_sum))
    last = flip(other, "gene", 2)
    prepare(2, other)
    prepare(3, sends[2][0])
    w_first_t = jnp.swapaxes(after(w_first, other), 1, 2)
    beside_sum = [begin(1, 1, other)]
    queries, key_value = split_call(
        me, mine, after(last, *beside_sum, sends[3][0], w_first_t)
    )
    across = flip(key_value, "cell", 2)
    beside = flip(key_value, "cell", 1)
    corner = flip(across, "cell", 1)
    beside_keys = [begin(2, 2, key_value)]
    queries = after(queries, *beside_keys, beside, across, corner)
    attended = attend_call(me, queries, (key_value, beside, across, corner))
    attended = after(attended, begin(2, 3, queries))
    near = flip(attended, "gene", 1)
    far = flip(attended, "gene", 2)
    rest = flip(after(far, near), "gene", 1)
    hidden, first = first_call(
        me, matrix, (attended, near, far, rest), w_out, masked, w_first_t, deeps
    )
    for part, bits in ((3, 2), (3, 3), (2, 1), (3, 1)):
        begin(part, bits, rest)

    got = []
    for t in range(len(deeps)):
        earlier = got[-1] if t else [back[2][1], *back[3][1:]]
        got.append(first[t][:1])
        for bits in (1, 2, 3):
            ready = (earlier[bits],) if t else earlier
            got[t].append(flip(after(first[t][bits], *ready), "gene", bits))

    send, keep = grad_first_call(me, sum(back, []), hidden, size)
    mine, other = add_call(me, keep, flip(send, "cell", 1))
    first_share = finish_call(me, mine, flip(other, "cell", 2), None, 0, blocks)

    denoised, share, pins = None, None, (send,)
    for t in range(len(deeps)):
        if t < len(deeps) - 2:
            pins += tuple(got[t + 1])
        pieces = [after(got[t][0], *pins), *got[t][1:]]
        start = sum(deeps[:t]) * blocks // deep
        denoised, send, keep = second_call(
            me, pieces, w_second, cotangent, hidden, denoised, start
        )
        pins = (first_share,) if share is None else (share,)
        mine, other = add_call(me, keep, flip(send, "cell", 1))
        pins += (other,)
        share = finish_call(me, mine, flip(other, "cell", 2), share, start, blocks)
    return (denoised, first_share, share)


def solution(mesh):
    placed = (
        P(("grp", "cell"), "gene"),
        P(("grp", "cell"), "gene"),
        P("gene"),
        P("gene", None),
        P(None, "gene"),
        P("gene", None, None),
        P("gene", None, None),
        P(("grp", "cell"), "gene"),
    )
    four = mesh.shape["gene"] == 4 and mesh.shape["cell"] == 4
    return jax.shard_map(
        on_device_four if four else on_device_general,
        mesh=mesh,
        in_specs=placed,
        out_specs=(
            P(("grp", "cell"), "gene"),
            P(("grp", "gene"), "cell", None),
            P(("grp", "gene"), "cell", None),
        ),
        check_vma=False,
    )
```

```python
import math

import jax
import jax.numpy as jnp
from jax import lax
from jax.experimental import pallas as pl
from jax.experimental.pallas import tpu as pltpu
from jax.sharding import PartitionSpec as P

HEADS = 16
HEAD_DIM = 64
TILE = 16
BF16 = jnp.bfloat16
F32 = jnp.float32


def normalize(part):
    count, columns = part.shape
    shaped = part.reshape(count, columns // HEAD_DIM, HEAD_DIM)
    meansq = jnp.mean(shaped * shaped, axis=-1, keepdims=True)
    return (shaped * lax.rsqrt(meansq + 1e-06)).astype(BF16).reshape(count, columns)


def attend(queries, key_piece, value_piece):
    query_count, columns = queries.shape
    key_count = key_piece.shape[0]
    heads = columns // HEAD_DIM
    query_heads = queries.reshape(query_count, heads, HEAD_DIM)
    key_heads = key_piece.reshape(key_count, heads, HEAD_DIM)
    value_heads = value_piece.reshape(key_count, heads, HEAD_DIM)
    scores = jnp.einsum(
        "qhd,khd->hqk", query_heads, key_heads, preferred_element_type=F32
    ) * HEAD_DIM ** (-0.5)
    expw = jnp.exp(scores).astype(BF16)
    denom = jnp.sum(expw, axis=2, dtype=F32)
    numer = jnp.einsum("hqk,khd->qhd", expw, value_heads, preferred_element_type=F32)
    return (numer / denom.T[:, :, None]).astype(BF16).reshape(query_count, columns)


def on_device_general(
    expression, gene_mask, mask_value, w_qkv, w_out, w_first, w_second, cotangent
):
    groups = lax.axis_size("gene")
    local_blocks = w_first.shape[0]
    block_size = w_first.shape[1]
    block_total = local_blocks * groups
    cell_rows = expression.shape[0]
    masked_in = jnp.where(gene_mask == 1, mask_value[None, :], expression)
    qkv_part = jnp.dot(masked_in, w_qkv, preferred_element_type=F32)
    qkv_full = lax.psum(qkv_part.astype(BF16), "gene").astype(F32)
    columns = qkv_full.shape[1] // 3
    queries = normalize(qkv_full[:, :columns])
    keys_normed = normalize(qkv_full[:, columns : 2 * columns])
    values_b = qkv_full[:, 2 * columns :].astype(BF16)
    attended = attend(
        queries,
        lax.all_gather(keys_normed, "cell", axis=0, tiled=True),
        lax.all_gather(values_b, "cell", axis=0, tiled=True),
    )
    added = jnp.dot(attended, w_out, preferred_element_type=F32)
    hidden = (masked_in.astype(F32) + added).astype(BF16)
    blocks = hidden.reshape(cell_rows, local_blocks, block_size)
    first = jnp.einsum("cbi,bio->cbo", blocks, w_first, preferred_element_type=F32).astype(BF16)
    cot_blocks = cotangent.reshape(cell_rows, local_blocks, block_size)
    back_perm = jnp.einsum(
        "cjo,jko->cjk", cot_blocks, w_second, preferred_element_type=F32
    ).astype(BF16)
    back_send = back_perm.reshape(cell_rows, block_size // groups, block_total)
    received = lax.all_to_all(first, "gene", split_axis=2, concat_axis=1, tiled=True)
    permuted = jnp.swapaxes(received, 1, 2).reshape(cell_rows, local_blocks, block_size)
    mixed = jnp.einsum("cjk,jko->cjo", permuted, w_second, preferred_element_type=F32)
    denoised = (
        (blocks.astype(F32) + mixed).astype(BF16).reshape(cell_rows, local_blocks * block_size)
    )
    grad_second = jnp.einsum("cjk,cjo->jko", permuted, cot_blocks, preferred_element_type=F32)
    back_recv = lax.all_to_all(back_send, "gene", split_axis=2, concat_axis=1, tiled=True)
    back_first = jnp.swapaxes(back_recv, 1, 2)
    grad_first = jnp.einsum("cbi,cbo->bio", blocks, back_first, preferred_element_type=F32)
    first_share, second_share = (
        lax.psum_scatter(
            grad_first.astype(BF16), "cell", scatter_dimension=1, tiled=True
        ).astype(F32),
        lax.psum_scatter(
            grad_second.astype(BF16), "cell", scatter_dimension=1, tiled=True
        ).astype(F32),
    )
    return (denoised, first_share, second_share)


def after(value, *earlier):
    return lax.optimization_barrier((value, *earlier))[0]


def flip(value, axis, bit):
    pairs = [(i, i ^ bit) for i in range(lax.axis_size(axis))]
    return lax.ppermute(value, axis, pairs)


def call(body, me, args, in_specs, outs, out_specs, grid=(1,), scratch=(), aliases=None):
    return pl.pallas_call(
        body,
        out_shape=outs,
        grid_spec=pltpu.PrefetchScalarGridSpec(
            num_scalar_prefetch=1,
            grid=grid,
            in_specs=in_specs,
            out_specs=out_specs,
            scratch_shapes=list(scratch),
        ),
        input_output_aliases=aliases or {},
        compiler_params=pltpu.CompilerParams(vmem_limit_bytes=52 * 2**20),
        cost_estimate=pl.CostEstimate(flops=1, bytes_accessed=1, transcendentals=0),
    )(me, *args)


def spec(shape, place):
    return pl.BlockSpec(shape, place)


def whole(shape):
    return pl.BlockSpec(shape, lambda *_: (0,) * len(shape))


def array(shape, dtype):
    return jax.ShapeDtypeStruct(shape, dtype)


def grid_turn():
    rows = lax.broadcasted_iota(jnp.int32, (TILE * TILE, TILE * TILE), 0)
    columns = lax.broadcasted_iota(jnp.int32, (TILE * TILE, TILE * TILE), 1)
    return ((rows % TILE) * TILE + rows // TILE == columns).astype(BF16)


def turn(matrix, tile):
    rows = tile.shape[-1]
    flat = tile.reshape(TILE * TILE, rows)
    return jnp.dot(matrix, flat, preferred_element_type=F32).astype(BF16).reshape(TILE, TILE, rows)


def back_kernel(me_ref, turn_ref, second_ref, cot_ref, *refs):
    outs, held = refs[:4], refs[4]
    blocks, rows = held.shape[2], held.shape[3]
    pair = held.shape[0] // (TILE // 2)
    at = pl.program_id(0) % (TILE // pair)
    back = lax.dot_general(
        second_ref[0], cot_ref[...], (((1,), (1,)), ((), ())), preferred_element_type=F32
    ).astype(BF16)
    held[pl.ds(at * pair, pair)] = back.reshape(pair, 4, blocks, rows)

    @pl.when(at == TILE // pair - 1)
    def _():
        for bits in range(4):
            there = me_ref[0] ^ bits
            for low in range(0, blocks, TILE):
                outs[bits][low : low + TILE] = turn(
                    turn_ref[...], held[:, there, low : low + TILE, :]
                )


def back_call(me, matrix, w_second, cotangent, part, parts):
    blocks, size, _ = w_second.shape
    rows = cotangent.shape[0]
    pair = size // (4 * blocks)
    count = blocks // parts
    per = TILE // pair
    first = part * count
    piece = array((blocks, count * pair, rows), BF16)
    return call(
        back_kernel,
        me,
        (matrix, w_second, cotangent),
        [
            whole(matrix.shape),
            spec((1, size, size), lambda j, _: (first + j, 0, 0)),
            spec((rows, size), lambda j, _: (0, first + j)),
        ],
        [piece] * 4,
        [spec((blocks, TILE, rows), lambda j, _: (0, j // per, 0))] * 4,
        grid=(count,),
        scratch=[pltpu.VMEM((TILE, 4, blocks, rows), BF16)],
    )


def project_kernel(me_ref, value_ref, mask_ref, fill_ref, *refs):
    weights, (masked_ref, send_ref, keep_ref), sums = refs[:3], refs[3:6], refs[6:]
    step = pl.program_id(0)
    masked = jnp.where(
        mask_ref[...] == 1, fill_ref[...].astype(F32), value_ref[...].astype(F32)
    ).astype(BF16)
    masked_ref[...] = masked

    @pl.when(step == 0)
    def _():
        for total in sums:
            total[...] = jnp.zeros_like(total)

    for weight, total in zip(weights, sums):
        total[...] += jnp.dot(masked, weight[...], preferred_element_type=F32)

    @pl.when(step == pl.num_programs(0) - 1)
    def _():
        share = sums[0].shape[1] // 4
        for out, flips in ((send_ref, (1, 3)), (keep_ref, (0, 2))):
            for slot, bits in enumerate(flips):
                columns = pl.ds(pl.multiple_of((me_ref[0] ^ bits) * share, share), share)
                for kind, total in enumerate(sums):
                    out[slot, :, kind * share : (kind + 1) * share] = total[:, columns].astype(
                        out.dtype
                    )


def project_call(me, expression, gene_mask, mask_value, w_qkv):
    rows, genes = expression.shape
    width = w_qkv.shape[1] // 3
    depth = min(genes, 512)
    wide = spec((rows, depth), lambda i, _: (0, i))
    shape = (2, rows, 3 * width // 4)
    return call(
        project_kernel,
        me,
        (expression, gene_mask, mask_value.reshape(1, genes), w_qkv, w_qkv, w_qkv),
        [
            wide,
            wide,
            spec((1, depth), lambda i, _: (0, i)),
            spec((depth, width), lambda i, _: (i, 0)),
            spec((depth, width), lambda i, _: (i, 1)),
            spec((depth, width), lambda i, _: (i, 2)),
        ],
        [array((rows, genes), BF16), array(shape, BF16), array(shape, F32)],
        [wide, whole(shape), whole(shape)],
        grid=(genes // depth,),
        scratch=[pltpu.VMEM((rows, width), F32)] * 3,
    )


def store_quarters(me, held, send_ref, keep_ref):
    quarter = held.shape[0] // 4
    for bits in range(4):
        start = pl.multiple_of((me ^ bits) * quarter, quarter)
        part = held[pl.ds(start, quarter), :]
        if bits % 2:
            send_ref[bits // 2][0] = part.astype(BF16)
        else:
            keep_ref[bits // 2, 0] = part


def quarter_outs(count, size):
    shape = (count, size // 4, size)
    one = spec((1, *shape[1:]), lambda j, _: (j, 0, 0))
    two = spec((2, 1, *shape[1:]), lambda j, _: (0, j, 0, 0))
    return [array(shape, BF16)] * 2 + [array((2, *shape), F32)], [one, one, two]


def add_kernel(_, keep_ref, came_ref, mine_ref, other_ref):
    mine_ref[...] = keep_ref[0] + came_ref[0].astype(F32)
    other_ref[...] = (keep_ref[1] + came_ref[1].astype(F32)).astype(BF16)


def add_call(me, keep, came):
    shape = keep.shape
    return call(
        add_kernel,
        me,
        (keep, came),
        [whole(shape), whole(shape)],
        [array(shape[1:], F32), array(shape[1:], BF16)],
        [whole(shape[1:])] * 2,
    )


def normalize_heads(part):
    columns = part.shape[1]
    heads = [lax.broadcasted_iota(jnp.int32, (columns, columns), d) // HEAD_DIM for d in (0, 1)]
    same = (heads[0] == heads[1]).astype(F32)
    sums = jnp.dot(
        part * part, same, precision=lax.Precision.HIGHEST, preferred_element_type=F32
    )
    return (part * lax.rsqrt(sums * (1.0 / HEAD_DIM) + 1e-06)).astype(BF16)


def pair_kernel(_, keep_ref, came_ref, next_ref, mine_ref, other_ref):
    mine_ref[...] = keep_ref[0] + came_ref[...].astype(F32)
    other_ref[...] = (keep_ref[1] + next_ref[...].astype(F32)).astype(BF16)


def pair_call(me, keep, came):
    shape = keep.shape[1:]
    return call(
        pair_kernel,
        me,
        (keep, *came),
        [whole(keep.shape), whole(shape), whole(shape)],
        [array(shape, F32), array(shape, BF16)],
        [whole(shape)] * 2,
    )


def finish_kernel(_, mine_ref, came_ref, *refs):
    refs[-1][...] = mine_ref[...] + came_ref[...].astype(F32)


def finish_call(me, mine, came, total, start, blocks):
    count, quarter, size = mine.shape
    step = math.gcd(count, start) if start else count
    args = [mine, came]
    in_specs = [spec((step, quarter, size), lambda i, _: (i, 0, 0))] * 2
    aliases = {}
    if total is not None:
        args.append(total)
        in_specs.append(pl.BlockSpec(memory_space=pl.ANY))
        aliases = {len(args): 0}
    return call(
        finish_kernel,
        me,
        args,
        in_specs,
        array((blocks, quarter, size), F32),
        spec((step, quarter, size), lambda i, _: (start // step + i, 0, 0)),
        grid=(count // step,),
        aliases=aliases,
    )


def split_kernel(_, mine_ref, came_ref, query_ref, out_ref):
    total = mine_ref[...] + came_ref[...].astype(F32)
    share = total.shape[1] // 3
    query_ref[...] = normalize_heads(total[:, :share])
    out_ref[:, :share] = normalize_heads(total[:, share : 2 * share])
    out_ref[:, share:] = total[:, 2 * share :].astype(BF16)


def split_call(me, mine, came):
    rows, columns = mine.shape
    shapes = ((rows, columns // 3), (rows, 2 * columns // 3))
    return call(
        split_kernel,
        me,
        (mine, came),
        [whole(mine.shape)] * 2,
        [array(shape, BF16) for shape in shapes],
        [whole(shape) for shape in shapes],
    )


def attend_kernel(_, query_ref, *refs):
    pieces, out_ref = refs[:-1], refs[-1]
    queries = query_ref[...]
    rows, share = queries.shape
    head_of = lax.broadcasted_iota(jnp.int32, (rows, share), 1) // HEAD_DIM
    out = jnp.zeros((rows, share), F32)
    for head in range(share // HEAD_DIM):
        query = jnp.where(head_of == head, queries.astype(F32) * HEAD_DIM**-0.5, 0.0).astype(BF16)
        numer = jnp.zeros((rows, share), F32)
        denom = jnp.zeros((rows, 1), F32)
        for piece in pieces:
            scores = lax.dot_general(
                query, piece[:, :share], (((1,), (1,)), ((), ())), preferred_element_type=F32
            )
            expw = jnp.exp(scores).astype(BF16)
            denom += jnp.sum(expw.astype(F32), axis=1, keepdims=True)
            numer += jnp.dot(expw, piece[:, share:], preferred_element_type=F32)
        out = jnp.where(head_of == head, numer / denom, out)
    out_ref[...] = out.astype(BF16)


def attend_call(me, queries, pieces):
    rows, share = queries.shape
    some = rows // 2
    part = spec((some, share), lambda i, _: (i, 0))
    return call(
        attend_kernel,
        me,
        (queries, *pieces),
        [part] + [whole(piece.shape) for piece in pieces],
        array((rows, share), BF16),
        part,
        grid=(2,),
    )


def first_kernel(me_ref, turn_ref, own, near, far, rest, w_out_ref, masked_ref, wf_ref, *refs):
    hidden_ref, outs, gathered, held = refs[0], refs[1:-2], refs[-2], refs[-1]
    block = pl.program_id(0)
    share = own.shape[1]

    @pl.when(block == 0)
    def _():
        for bits, piece in enumerate((own, near, far, rest)):
            place = pl.multiple_of((me_ref[0] ^ bits) * share, share)
            gathered[:, pl.ds(place, share)] = piece[...]

    added = jnp.dot(gathered[...], w_out_ref[...], preferred_element_type=F32)
    hidden = (masked_ref[...].astype(F32) + added).astype(BF16)
    hidden_ref[...] = hidden
    held[block % TILE] = lax.dot_general(
        wf_ref[0], hidden, (((1,), (1,)), ((), ())), preferred_element_type=F32
    ).astype(BF16)

    @pl.when(block % TILE == TILE - 1)
    def _():
        deeps = [out.shape[1] for out in outs]
        deep = sum(deeps)
        for there in range(4):
            for low in range(0, deep, TILE):
                start = there * deep + low
                tile = turn(turn_ref[...], held[:, start : start + TILE, :])
                for chunk, count in enumerate(deeps):
                    begin = sum(deeps[:chunk])
                    least, most = max(begin, low), min(begin + count, low + TILE)
                    if least < most:
                        outs[chunk][there, least - begin : most - begin] = tile[
                            least - low : most - low
                        ]


def first_call(me, matrix, attended, w_out, masked, w_first_t, deeps):
    blocks, size, _ = w_first_t.shape
    rows, genes = masked.shape
    width = w_out.shape[0]
    wide = spec((rows, size), lambda b, _: (0, b))
    hidden, *first = call(
        first_kernel,
        me,
        (matrix, *attended, w_out, masked, w_first_t),
        [whole(matrix.shape)]
        + [whole(part.shape) for part in attended]
        + [
            spec((width, size), lambda b, _: (0, b)),
            wide,
            spec((1, size, size), lambda b, _: (b, 0, 0)),
        ],
        [array((rows, genes), BF16)] + [array((4, deep, blocks, rows), BF16) for deep in deeps],
        [wide] + [spec((4, deep, TILE, rows), lambda b, _: (0, 0, b // TILE, 0)) for deep in deeps],
        grid=(blocks,),
        scratch=[pltpu.VMEM((rows, width), BF16), pltpu.VMEM((TILE, size, rows), BF16)],
    )
    return hidden, first


def second_kernel(me_ref, *refs):
    piece, w_ref, cot_ref, hidden_ref = refs[:4]
    out_ref, *send_ref, keep_ref, held, square = refs[-6:]
    for source in range(4):
        held[:, source] = piece[source]
    size = w_ref.shape[1]
    permuted = held[...].reshape(size, held.shape[3])
    square[...] = jnp.dot(permuted, cot_ref[...], preferred_element_type=F32)
    store_quarters(me_ref[1], square, send_ref, keep_ref)
    mixed = lax.dot_general(
        permuted, w_ref[0], (((0,), (0,)), ((), ())), preferred_element_type=F32
    )
    out_ref[...] = (hidden_ref[...].astype(F32) + mixed).astype(BF16)


def second_call(me, piece, w_second, cotangent, hidden, denoised, start):
    blocks, size, _ = w_second.shape
    _, deep, _, rows = piece.shape
    pair = size // (4 * blocks)
    count = deep // pair
    wide = spec((rows, size), lambda j, _: (0, start + j))
    square = spec((1, size, size), lambda j, _: (start + j, 0, 0))
    args = [piece, w_second, cotangent, hidden]
    in_specs = [spec((4, pair, blocks, rows), lambda j, _: (0, j, 0, 0)), square, wide, wide]
    quarters = quarter_outs(count, size)
    aliases = {}
    if denoised is not None:
        args.append(denoised)
        in_specs.append(pl.BlockSpec(memory_space=pl.ANY))
        aliases = {len(args): 0}
    return call(
        second_kernel,
        me,
        args,
        in_specs,
        [array(hidden.shape, BF16), *quarters[0]],
        [wide, *quarters[1]],
        grid=(count,),
        scratch=[pltpu.VMEM((pair, 4, blocks, rows), BF16), pltpu.VMEM((size, size), F32)],
        aliases=aliases,
    )


def grad_first_kernel(me_ref, *refs):
    pieces, (hidden_ref, *send_ref, keep_ref, held, square) = refs[:-6], refs[-6:]
    for half in range(len(pieces) // 4):
        for bits in range(4):
            held[me_ref[0] ^ bits, half] = pieces[half * 4 + bits][0]
    back = held[...].reshape(-1, held.shape[3])
    square[...] = jnp.dot(back, hidden_ref[...], preferred_element_type=F32).T
    store_quarters(me_ref[1], square, send_ref, keep_ref)


def grad_first_call(me, pieces, hidden, size, start, count):
    _, deep, rows = pieces[0].shape
    return call(
        grad_first_kernel,
        me,
        (*pieces, hidden),
        [spec((1, deep, rows), lambda b, _: (start + b, 0, 0))] * len(pieces)
        + [spec((rows, size), lambda b, _: (0, start + b))],
        *quarter_outs(count, size),
        grid=(count,),
        scratch=[
            pltpu.VMEM((4, len(pieces) // 4, deep, rows), BF16),
            pltpu.VMEM((size, size), F32),
        ],
    )


def on_device_four(expression, gene_mask, mask_value, w_qkv, w_out, w_first, w_second, cotangent):
    me = jnp.stack([lax.axis_index("gene"), lax.axis_index("cell")]).astype(jnp.int32)
    blocks, size, _ = w_first.shape
    parts = 4
    deep = size // 4
    deeps = [deep // 4] * 3 + [3 * deep // 16, deep // 16]
    matrix = grid_turn()
    sends, back = [None] * parts, [[None] * 4 for _ in range(parts)]

    def prepare(part, *earlier):
        sends[part] = back_call(me, matrix, w_second, after(cotangent, *earlier), part, parts)
        back[part][0] = sends[part][0]

    def begin(part, bits, *earlier):
        back[part][bits] = flip(after(sends[part][bits], *earlier), "gene", bits)
        return back[part][bits]

    prepare(0)
    first_part = [begin(0, bits) for bits in (3, 2, 1)]
    masked, send, keep = project_call(
        me, after(expression, sends[0][0]), gene_mask, mask_value, w_qkv
    )
    came = flip(after(send, *first_part), "gene", 1)
    prepare(1, send)
    beside_sum = [begin(1, 2), begin(1, 3)]
    mine, other = add_call(me, keep, after(came, *beside_sum))
    last = flip(other, "gene", 2)
    prepare(2, other)
    prepare(3, sends[2][0])
    w_first_t = jnp.swapaxes(after(w_first, other), 1, 2)
    beside_sum = [begin(1, 1, other)]
    queries, key_value = split_call(
        me, mine, after(last, *beside_sum, sends[3][0], w_first_t)
    )
    across = flip(key_value, "cell", 2)
    beside = flip(key_value, "cell", 1)
    corner = flip(across, "cell", 1)
    beside_keys = [begin(2, 2, key_value)]
    queries = after(queries, *beside_keys, beside, across, corner)
    attended = attend_call(me, queries, (key_value, beside, across, corner))
    attended = after(attended, begin(2, 3, queries))
    near = flip(attended, "gene", 1)
    far = flip(attended, "gene", 2)
    rest = flip(after(far, near), "gene", 1)
    hidden, first = first_call(
        me, matrix, (attended, near, far, rest), w_out, masked, w_first_t, deeps
    )
    for part, bits in ((3, 2), (3, 3), (2, 1), (3, 1)):
        begin(part, bits, rest)

    got = []

    def launch(t, *earlier):
        piece = after(first[t], *earlier)
        got.append(lax.all_to_all(piece, "gene", split_axis=0, concat_axis=0, tiled=True))

    launch(0, back[2][1], *back[3][1:])
    denoised, shares, made, added = None, [None, None], [], []
    some = blocks // 2
    back = sum(back, [])

    def make_first(part, *earlier):
        *send, keep = grad_first_call(
            me, after(back, *earlier), hidden, size, part * some, some
        )
        made.append((0, part * some, [flip(piece, "cell", 1) for piece in send], keep))

    def settle(*earlier):
        pins = []
        for which, start, mine, last in added:
            shares[which] = finish_call(
                me, mine, after(last, *earlier), shares[which], start, blocks
            )
        pins += [shares[which] for which in {entry[0]: 0 for entry in added}]
        added.clear()
        for which, start, came, keep in made:
            mine, other = pair_call(me, keep, after(came, *earlier))
            added.append((which, start, mine, flip(other, "cell", 2)))
            pins.append(mine)
        made.clear()
        return pins

    make_first(0)
    make_first(1)
    pins = []
    for t in range(len(deeps)):
        if t + 1 < len(deeps):
            launch(t + 1, got[t], *pins)
        pins = settle(got[t])
        start = sum(deeps[:t]) * blocks // deep
        denoised, *send, keep = second_call(
            me, got[t], w_second, cotangent, hidden, denoised, start
        )
        made.append((1, start, [flip(piece, "cell", 1) for piece in send], keep))
    settle()
    settle()
    return (denoised, *shares)


def solution(mesh):
    placed = (
        P(("grp", "cell"), "gene"),
        P(("grp", "cell"), "gene"),
        P("gene"),
        P("gene", None),
        P(None, "gene"),
        P("gene", None, None),
        P("gene", None, None),
        P(("grp", "cell"), "gene"),
    )
    four = mesh.shape["gene"] == 4 and mesh.shape["cell"] == 4
    return jax.shard_map(
        on_device_four if four else on_device_general,
        mesh=mesh,
        in_specs=placed,
        out_specs=(
            P(("grp", "cell"), "gene"),
            P(("grp", "gene"), "cell", None),
            P(("grp", "gene"), "cell", None),
        ),
        check_vma=False,
    )
```

```python
import math

import jax
import jax.numpy as jnp
from jax import lax
from jax.experimental import pallas as pl
from jax.experimental.pallas import tpu as pltpu
from jax.sharding import PartitionSpec as P

HEADS = 16
HEAD_DIM = 64
TILE = 16
BF16 = jnp.bfloat16
F32 = jnp.float32


def normalize(part):
    count, columns = part.shape
    shaped = part.reshape(count, columns // HEAD_DIM, HEAD_DIM)
    meansq = jnp.mean(shaped * shaped, axis=-1, keepdims=True)
    return (shaped * lax.rsqrt(meansq + 1e-06)).astype(BF16).reshape(count, columns)


def attend(queries, key_piece, value_piece):
    query_count, columns = queries.shape
    key_count = key_piece.shape[0]
    heads = columns // HEAD_DIM
    query_heads = queries.reshape(query_count, heads, HEAD_DIM)
    key_heads = key_piece.reshape(key_count, heads, HEAD_DIM)
    value_heads = value_piece.reshape(key_count, heads, HEAD_DIM)
    scores = jnp.einsum(
        "qhd,khd->hqk", query_heads, key_heads, preferred_element_type=F32
    ) * HEAD_DIM ** (-0.5)
    expw = jnp.exp(scores).astype(BF16)
    denom = jnp.sum(expw, axis=2, dtype=F32)
    numer = jnp.einsum("hqk,khd->qhd", expw, value_heads, preferred_element_type=F32)
    return (numer / denom.T[:, :, None]).astype(BF16).reshape(query_count, columns)


def on_device_general(
    expression, gene_mask, mask_value, w_qkv, w_out, w_first, w_second, cotangent
):
    groups = lax.axis_size("gene")
    local_blocks = w_first.shape[0]
    block_size = w_first.shape[1]
    block_total = local_blocks * groups
    cell_rows = expression.shape[0]
    masked_in = jnp.where(gene_mask == 1, mask_value[None, :], expression)
    qkv_part = jnp.dot(masked_in, w_qkv, preferred_element_type=F32)
    qkv_full = lax.psum(qkv_part.astype(BF16), "gene").astype(F32)
    columns = qkv_full.shape[1] // 3
    queries = normalize(qkv_full[:, :columns])
    keys_normed = normalize(qkv_full[:, columns : 2 * columns])
    values_b = qkv_full[:, 2 * columns :].astype(BF16)
    attended = attend(
        queries,
        lax.all_gather(keys_normed, "cell", axis=0, tiled=True),
        lax.all_gather(values_b, "cell", axis=0, tiled=True),
    )
    added = jnp.dot(attended, w_out, preferred_element_type=F32)
    hidden = (masked_in.astype(F32) + added).astype(BF16)
    blocks = hidden.reshape(cell_rows, local_blocks, block_size)
    first = jnp.einsum("cbi,bio->cbo", blocks, w_first, preferred_element_type=F32).astype(BF16)
    cot_blocks = cotangent.reshape(cell_rows, local_blocks, block_size)
    back_perm = jnp.einsum(
        "cjo,jko->cjk", cot_blocks, w_second, preferred_element_type=F32
    ).astype(BF16)
    back_send = back_perm.reshape(cell_rows, block_size // groups, block_total)
    received = lax.all_to_all(first, "gene", split_axis=2, concat_axis=1, tiled=True)
    permuted = jnp.swapaxes(received, 1, 2).reshape(cell_rows, local_blocks, block_size)
    mixed = jnp.einsum("cjk,jko->cjo", permuted, w_second, preferred_element_type=F32)
    denoised = (
        (blocks.astype(F32) + mixed).astype(BF16).reshape(cell_rows, local_blocks * block_size)
    )
    grad_second = jnp.einsum("cjk,cjo->jko", permuted, cot_blocks, preferred_element_type=F32)
    back_recv = lax.all_to_all(back_send, "gene", split_axis=2, concat_axis=1, tiled=True)
    back_first = jnp.swapaxes(back_recv, 1, 2)
    grad_first = jnp.einsum("cbi,cbo->bio", blocks, back_first, preferred_element_type=F32)
    first_share, second_share = (
        lax.psum_scatter(
            grad_first.astype(BF16), "cell", scatter_dimension=1, tiled=True
        ).astype(F32),
        lax.psum_scatter(
            grad_second.astype(BF16), "cell", scatter_dimension=1, tiled=True
        ).astype(F32),
    )
    return (denoised, first_share, second_share)


def after(value, *earlier):
    return lax.optimization_barrier((value, *earlier))[0]


def flip(value, axis, bit):
    pairs = [(i, i ^ bit) for i in range(lax.axis_size(axis))]
    return lax.ppermute(value, axis, pairs)


def call(body, me, args, in_specs, outs, out_specs, grid=(1,), scratch=(), aliases=None):
    return pl.pallas_call(
        body,
        out_shape=outs,
        grid_spec=pltpu.PrefetchScalarGridSpec(
            num_scalar_prefetch=1,
            grid=grid,
            in_specs=in_specs,
            out_specs=out_specs,
            scratch_shapes=list(scratch),
        ),
        input_output_aliases=aliases or {},
        compiler_params=pltpu.CompilerParams(vmem_limit_bytes=52 * 2**20),
        cost_estimate=pl.CostEstimate(flops=1, bytes_accessed=1, transcendentals=0),
    )(me, *args)


def spec(shape, place):
    return pl.BlockSpec(shape, place)


def whole(shape):
    return pl.BlockSpec(shape, lambda *_: (0,) * len(shape))


def several(count):
    return next(group for group in (4, 2, 1) if count % group == 0)


def array(shape, dtype):
    return jax.ShapeDtypeStruct(shape, dtype)


def grid_turn():
    rows = lax.broadcasted_iota(jnp.int32, (TILE * TILE, TILE * TILE), 0)
    columns = lax.broadcasted_iota(jnp.int32, (TILE * TILE, TILE * TILE), 1)
    return ((rows % TILE) * TILE + rows // TILE == columns).astype(BF16)


def turn(matrix, tile):
    rows = tile.shape[-1]
    flat = tile.reshape(TILE * TILE, rows)
    return jnp.dot(matrix, flat, preferred_element_type=F32).astype(BF16).reshape(TILE, TILE, rows)


def back_kernel(me_ref, turn_ref, second_ref, cot_ref, *refs):
    outs, held = refs[:4], refs[4]
    blocks, rows = held.shape[2], held.shape[3]
    group, size, _ = second_ref.shape
    pair = size // (4 * blocks)
    steps = TILE // (pair * group)
    at = pl.program_id(0) % steps
    for g in range(group):
        back = lax.dot_general(
            second_ref[g],
            cot_ref[:, g * size : (g + 1) * size],
            (((1,), (1,)), ((), ())),
            preferred_element_type=F32,
        ).astype(BF16)
        held[pl.ds((at * group + g) * pair, pair)] = back.reshape(pair, 4, blocks, rows)

    @pl.when(at == steps - 1)
    def _():
        for bits in range(4):
            there = me_ref[0] ^ bits
            for low in range(0, blocks, TILE):
                outs[bits][low : low + TILE] = turn(
                    turn_ref[...], held[:, there, low : low + TILE, :]
                )


def back_call(me, matrix, w_second, cotangent, part, parts):
    blocks, size, _ = w_second.shape
    rows = cotangent.shape[0]
    pair = size // (4 * blocks)
    count = blocks // parts
    group = several(math.gcd(count, TILE // pair))
    steps = TILE // (pair * group)
    first = part * count // group
    piece = array((blocks, count * pair, rows), BF16)
    return call(
        back_kernel,
        me,
        (matrix, w_second, cotangent),
        [
            whole(matrix.shape),
            spec((group, size, size), lambda j, _: (first + j, 0, 0)),
            spec((rows, group * size), lambda j, _: (0, first + j)),
        ],
        [piece] * 4,
        [spec((blocks, TILE, rows), lambda j, _: (0, j // steps, 0))] * 4,
        grid=(count // group,),
        scratch=[pltpu.VMEM((TILE, 4, blocks, rows), BF16)],
    )


def project_kernel(me_ref, value_ref, mask_ref, fill_ref, weight_ref, *refs):
    masked_ref, send_ref, keep_ref, total = refs
    step = pl.program_id(0)
    masked = jnp.where(
        mask_ref[...] == 1, fill_ref[...].astype(F32), value_ref[...].astype(F32)
    ).astype(BF16)
    masked_ref[...] = masked
    width = total.shape[1] // 3

    @pl.when(step == 0)
    def _():
        total[...] = jnp.dot(masked, weight_ref[...], preferred_element_type=F32)

    @pl.when(step > 0)
    def _():
        total[...] += jnp.dot(masked, weight_ref[...], preferred_element_type=F32)

    @pl.when(step == pl.num_programs(0) - 1)
    def _():
        share = width // 4
        for out, flips in ((send_ref, (1, 3)), (keep_ref, (0, 2))):
            for slot, bits in enumerate(flips):
                for kind in range(3):
                    place = pl.multiple_of(kind * width + (me_ref[0] ^ bits) * share, share)
                    out[slot, :, kind * share : (kind + 1) * share] = total[
                        :, pl.ds(place, share)
                    ].astype(out.dtype)


def project_call(me, expression, gene_mask, mask_value, w_qkv):
    rows, genes = expression.shape
    width = w_qkv.shape[1]
    depth = min(genes, 1024)
    wide = spec((rows, depth), lambda i, _: (0, i))
    shape = (2, rows, width // 4)
    return call(
        project_kernel,
        me,
        (expression, gene_mask, mask_value.reshape(1, genes), w_qkv),
        [
            wide,
            wide,
            spec((1, depth), lambda i, _: (0, i)),
            spec((depth, width), lambda i, _: (i, 0)),
        ],
        [array((rows, genes), BF16), array(shape, BF16), array(shape, F32)],
        [wide, whole(shape), whole(shape)],
        grid=(genes // depth,),
        scratch=[pltpu.VMEM((rows, width), F32)],
    )


def store_quarters(me, at, held, send_ref, keep_ref):
    quarter = held.shape[0] // 4
    for bits in range(4):
        start = pl.multiple_of((me ^ bits) * quarter, quarter)
        part = held[pl.ds(start, quarter), :]
        if bits % 2:
            send_ref[bits // 2][at] = part.astype(BF16)
        else:
            keep_ref[bits // 2, at] = part


def quarter_outs(count, group, size):
    shape = (count, size // 4, size)
    one = spec((group, *shape[1:]), lambda j, _: (j, 0, 0))
    two = spec((2, group, *shape[1:]), lambda j, _: (0, j, 0, 0))
    return [array(shape, BF16)] * 2 + [array((2, *shape), F32)], [one, one, two]


def add_kernel(_, keep_ref, came_ref, mine_ref, other_ref):
    mine_ref[...] = keep_ref[0] + came_ref[0].astype(F32)
    other_ref[...] = (keep_ref[1] + came_ref[1].astype(F32)).astype(BF16)


def add_call(me, keep, came):
    shape = keep.shape
    return call(
        add_kernel,
        me,
        (keep, came),
        [whole(shape), whole(shape)],
        [array(shape[1:], F32), array(shape[1:], BF16)],
        [whole(shape[1:])] * 2,
    )


def normalize_heads(part):
    columns = part.shape[1]
    heads = [lax.broadcasted_iota(jnp.int32, (columns, columns), d) // HEAD_DIM for d in (0, 1)]
    same = (heads[0] == heads[1]).astype(F32)
    sums = jnp.dot(
        part * part, same, precision=lax.Precision.HIGHEST, preferred_element_type=F32
    )
    return (part * lax.rsqrt(sums * (1.0 / HEAD_DIM) + 1e-06)).astype(BF16)


def pair_kernel(_, keep_ref, came_ref, next_ref, mine_ref, other_ref):
    mine_ref[...] = keep_ref[0] + came_ref[...].astype(F32)
    other_ref[...] = (keep_ref[1] + next_ref[...].astype(F32)).astype(BF16)


def pair_call(me, keep, came):
    shape = keep.shape[1:]
    return call(
        pair_kernel,
        me,
        (keep, *came),
        [whole(keep.shape), whole(shape), whole(shape)],
        [array(shape, F32), array(shape, BF16)],
        [whole(shape)] * 2,
    )


def finish_kernel(_, mine_ref, came_ref, *refs):
    refs[-1][...] = mine_ref[...] + came_ref[...].astype(F32)


def finish_call(me, mine, came, total, start, blocks):
    count, quarter, size = mine.shape
    step = math.gcd(count, start) if start else count
    args = [mine, came]
    in_specs = [spec((step, quarter, size), lambda i, _: (i, 0, 0))] * 2
    aliases = {}
    if total is not None:
        args.append(total)
        in_specs.append(pl.BlockSpec(memory_space=pl.ANY))
        aliases = {len(args): 0}
    return call(
        finish_kernel,
        me,
        args,
        in_specs,
        array((blocks, quarter, size), F32),
        spec((step, quarter, size), lambda i, _: (start // step + i, 0, 0)),
        grid=(count // step,),
        aliases=aliases,
    )


def split_kernel(_, mine_ref, came_ref, query_ref, out_ref):
    total = mine_ref[...] + came_ref[...].astype(F32)
    share = total.shape[1] // 3
    query_ref[...] = normalize_heads(total[:, :share])
    out_ref[:, :share] = normalize_heads(total[:, share : 2 * share])
    out_ref[:, share:] = total[:, 2 * share :].astype(BF16)


def split_call(me, mine, came):
    rows, columns = mine.shape
    shapes = ((rows, columns // 3), (rows, 2 * columns // 3))
    return call(
        split_kernel,
        me,
        (mine, came),
        [whole(mine.shape)] * 2,
        [array(shape, BF16) for shape in shapes],
        [whole(shape) for shape in shapes],
    )


def attend_kernel(_, query_ref, *refs):
    pieces, out_ref = refs[:-1], refs[-1]
    queries = query_ref[...]
    rows, share = queries.shape
    head_of = lax.broadcasted_iota(jnp.int32, (rows, share), 1) // HEAD_DIM
    out = jnp.zeros((rows, share), F32)
    for head in range(share // HEAD_DIM):
        query = jnp.where(head_of == head, queries.astype(F32) * HEAD_DIM**-0.5, 0.0).astype(BF16)
        numer = jnp.zeros((rows, share), F32)
        denom = jnp.zeros((rows, 1), F32)
        for piece in pieces:
            scores = lax.dot_general(
                query, piece[:, :share], (((1,), (1,)), ((), ())), preferred_element_type=F32
            )
            expw = jnp.exp(scores).astype(BF16)
            denom += jnp.sum(expw.astype(F32), axis=1, keepdims=True)
            numer += jnp.dot(expw, piece[:, share:], preferred_element_type=F32)
        out = jnp.where(head_of == head, numer / denom, out)
    out_ref[...] = out.astype(BF16)


def attend_call(me, queries, pieces):
    rows, share = queries.shape
    some = rows // 2
    part = spec((some, share), lambda i, _: (i, 0))
    return call(
        attend_kernel,
        me,
        (queries, *pieces),
        [part] + [whole(piece.shape) for piece in pieces],
        array((rows, share), BF16),
        part,
        grid=(2,),
    )


def first_kernel(me_ref, turn_ref, own, near, far, rest, w_out_ref, masked_ref, wf_ref, *refs):
    hidden_ref, outs, gathered, held = refs[0], refs[1:-2], refs[-2], refs[-1]
    step = pl.program_id(0)
    share = own.shape[1]
    group, size, _ = wf_ref.shape
    steps = TILE // group

    @pl.when(step == 0)
    def _():
        for bits, piece in enumerate((own, near, far, rest)):
            place = pl.multiple_of((me_ref[0] ^ bits) * share, share)
            gathered[:, pl.ds(place, share)] = piece[...]

    added = jnp.dot(gathered[...], w_out_ref[...], preferred_element_type=F32)
    hidden = (masked_ref[...].astype(F32) + added).astype(BF16)
    hidden_ref[...] = hidden
    for g in range(group):
        held[step % steps * group + g] = lax.dot_general(
            wf_ref[g],
            hidden[:, g * size : (g + 1) * size],
            (((1,), (1,)), ((), ())),
            preferred_element_type=F32,
        ).astype(BF16)

    @pl.when(step % steps == steps - 1)
    def _():
        deeps = [out.shape[1] for out in outs]
        deep = sum(deeps)
        for there in range(4):
            for low in range(0, deep, TILE):
                start = there * deep + low
                tile = turn(turn_ref[...], held[:, start : start + TILE, :])
                for chunk, count in enumerate(deeps):
                    begin = sum(deeps[:chunk])
                    least, most = max(begin, low), min(begin + count, low + TILE)
                    if least < most:
                        outs[chunk][there, least - begin : most - begin] = tile[
                            least - low : most - low
                        ]


def first_call(me, matrix, attended, w_out, masked, w_first_t, deeps):
    blocks, size, _ = w_first_t.shape
    rows, genes = masked.shape
    width = w_out.shape[0]
    group = several(TILE)
    steps = TILE // group
    wide = spec((rows, group * size), lambda b, _: (0, b))
    hidden, *first = call(
        first_kernel,
        me,
        (matrix, *attended, w_out, masked, w_first_t),
        [whole(matrix.shape)]
        + [whole(part.shape) for part in attended]
        + [
            spec((width, group * size), lambda b, _: (0, b)),
            wide,
            spec((group, size, size), lambda b, _: (b, 0, 0)),
        ],
        [array((rows, genes), BF16)] + [array((4, deep, blocks, rows), BF16) for deep in deeps],
        [wide]
        + [spec((4, deep, TILE, rows), lambda b, _: (0, 0, b // steps, 0)) for deep in deeps],
        grid=(blocks // group,),
        scratch=[pltpu.VMEM((rows, width), BF16), pltpu.VMEM((TILE, size, rows), BF16)],
    )
    return hidden, first


def second_kernel(me_ref, *refs):
    piece, w_ref, cot_ref, hidden_ref = refs[:4]
    out_ref, *send_ref, keep_ref, square = refs[-5:]
    group, size, _ = w_ref.shape
    pair = piece.shape[1] // group
    for g in range(group):
        at = slice(g * size, (g + 1) * size)
        permuted = jnp.concatenate(
            [piece[s, g * pair + o] for o in range(pair) for s in range(4)], axis=0
        )
        square[g] = jnp.dot(permuted, cot_ref[:, at], preferred_element_type=F32)
        store_quarters(me_ref[1], g, square.at[g], send_ref, keep_ref)
        mixed = lax.dot_general(
            permuted, w_ref[g], (((0,), (0,)), ((), ())), preferred_element_type=F32
        )
        out_ref[:, at] = (hidden_ref[:, at].astype(F32) + mixed).astype(BF16)


def second_call(me, piece, w_second, cotangent, hidden, denoised, start):
    blocks, size, _ = w_second.shape
    _, deep, _, rows = piece.shape
    pair = size // (4 * blocks)
    count = deep // pair
    group = several(math.gcd(count, start) if start else count)
    begin = start // group
    wide = spec((rows, group * size), lambda j, _: (0, begin + j))
    square = spec((group, size, size), lambda j, _: (begin + j, 0, 0))
    args = [piece, w_second, cotangent, hidden]
    in_specs = [
        spec((4, group * pair, blocks, rows), lambda j, _: (0, j, 0, 0)),
        square,
        wide,
        wide,
    ]
    quarters = quarter_outs(count, group, size)
    aliases = {}
    if denoised is not None:
        args.append(denoised)
        in_specs.append(pl.BlockSpec(memory_space=pl.ANY))
        aliases = {len(args): 0}
    return call(
        second_kernel,
        me,
        args,
        in_specs,
        [array(hidden.shape, BF16), *quarters[0]],
        [wide, *quarters[1]],
        grid=(count // group,),
        scratch=[pltpu.VMEM((group, size, size), F32)],
        aliases=aliases,
    )


def grad_first_kernel(me_ref, *refs):
    pieces, (hidden_ref, *send_ref, keep_ref, held, square) = refs[:-6], refs[-6:]
    group, size, _ = square.shape
    for g in range(group):
        for part in range(len(pieces) // 4):
            for bits in range(4):
                held[g, me_ref[0] ^ bits, part] = pieces[part * 4 + bits][g]
        back = held[g].reshape(size, held.shape[4])
        hidden = hidden_ref[:, g * size : (g + 1) * size]
        square[g] = jnp.dot(back, hidden, preferred_element_type=F32).T
        store_quarters(me_ref[1], g, square.at[g], send_ref, keep_ref)


def grad_first_call(me, pieces, hidden, size, start, count):
    _, deep, rows = pieces[0].shape
    group = several(math.gcd(count, start) if start else count)
    begin = start // group
    return call(
        grad_first_kernel,
        me,
        (*pieces, hidden),
        [spec((group, deep, rows), lambda b, _: (begin + b, 0, 0))] * len(pieces)
        + [spec((rows, group * size), lambda b, _: (0, begin + b))],
        *quarter_outs(count, group, size),
        grid=(count // group,),
        scratch=[
            pltpu.VMEM((group, 4, len(pieces) // 4, deep, rows), BF16),
            pltpu.VMEM((group, size, size), F32),
        ],
    )


def on_device_four(expression, gene_mask, mask_value, w_qkv, w_out, w_first, w_second, cotangent):
    me = jnp.stack([lax.axis_index("gene"), lax.axis_index("cell")]).astype(jnp.int32)
    blocks, size, _ = w_first.shape
    parts = 4
    deep = size // 4
    deeps = [deep // 2, 3 * deep // 8, deep // 8]
    matrix = grid_turn()
    sends, back = [None] * parts, [[None] * 4 for _ in range(parts)]

    def prepare(part, *earlier):
        sends[part] = back_call(me, matrix, w_second, after(cotangent, *earlier), part, parts)
        back[part][0] = sends[part][0]

    def begin(part, bits, *earlier):
        back[part][bits] = flip(after(sends[part][bits], *earlier), "gene", bits)
        return back[part][bits]

    prepare(0)
    first_part = [begin(0, bits) for bits in (3, 2, 1)]
    masked, send, keep = project_call(
        me, after(expression, sends[0][0]), gene_mask, mask_value, w_qkv
    )
    came = flip(after(send, *first_part), "gene", 1)
    prepare(1, send)
    beside_sum = [begin(1, 2), begin(1, 3)]
    mine, other = add_call(me, keep, after(came, *beside_sum))
    last = flip(other, "gene", 2)
    prepare(2, other)
    prepare(3, sends[2][0])
    w_first_t = jnp.swapaxes(after(w_first, other), 1, 2)
    beside_sum = [begin(1, 1, other)]
    queries, key_value = split_call(
        me, mine, after(last, *beside_sum, sends[3][0], w_first_t)
    )
    across = flip(key_value, "cell", 2)
    beside = flip(key_value, "cell", 1)
    corner = flip(across, "cell", 1)
    beside_keys = [begin(2, 2, last), begin(2, 1, last)]
    queries = after(queries, *beside_keys, beside, across, corner)
    attended = attend_call(me, queries, (key_value, beside, across, corner))
    attended = after(attended, begin(2, 3, queries), begin(3, 1, queries))
    near = flip(attended, "gene", 1)
    far = flip(attended, "gene", 2)
    rest = flip(after(far, near), "gene", 1)
    rest = after(rest, begin(3, 2, attended))
    hidden, first = first_call(
        me, matrix, (attended, near, far, rest), w_out, masked, w_first_t, deeps
    )
    begin(3, 3, rest)

    got = []

    def launch(t, *earlier):
        piece = after(first[t], *earlier)
        got.append(lax.all_to_all(piece, "gene", split_axis=0, concat_axis=0, tiled=True))

    launch(0, back[3][3])
    denoised, shares = None, [None, None]
    back = sum(back, [])

    def sum_cells(which, start, send, keep):
        came = [flip(piece, "cell", 1) for piece in send]
        mine, other = pair_call(me, keep, came)
        last = flip(other, "cell", 2)
        shares[which] = finish_call(me, mine, last, shares[which], start, blocks)

    *send, keep = grad_first_call(me, back, hidden, size, 0, blocks // 2)
    *send_next, keep_next = grad_first_call(me, back, hidden, size, blocks // 2, blocks // 2)
    sum_cells(0, 0, send, keep)
    sum_cells(0, blocks // 2, send_next, keep_next)
    pin = shares[0]
    for t in range(len(deeps)):
        if t + 1 < len(deeps):
            launch(t + 1, got[t], pin)
        start = sum(deeps[:t]) * blocks // deep
        denoised, *send, keep = second_call(
            me, got[t], w_second, cotangent, hidden, denoised, start
        )
        sum_cells(1, start, send, keep)
        pin = shares[1]
    return (denoised, *shares)


def solution(mesh):
    placed = (
        P(("grp", "cell"), "gene"),
        P(("grp", "cell"), "gene"),
        P("gene"),
        P("gene", None),
        P(None, "gene"),
        P("gene", None, None),
        P("gene", None, None),
        P(("grp", "cell"), "gene"),
    )
    four = mesh.shape["gene"] == 4 and mesh.shape["cell"] == 4
    return jax.shard_map(
        on_device_four if four else on_device_general,
        mesh=mesh,
        in_specs=placed,
        out_specs=(
            P(("grp", "cell"), "gene"),
            P(("grp", "gene"), "cell", None),
            P(("grp", "gene"), "cell", None),
        ),
        check_vma=False,
    )
```

```python
import math

import jax
import jax.numpy as jnp
from jax import lax
from jax.experimental import pallas as pl
from jax.experimental.pallas import tpu as pltpu
from jax.sharding import PartitionSpec as P

HEADS = 16
HEAD_DIM = 64
TILE = 16
BF16 = jnp.bfloat16
F32 = jnp.float32


def normalize(part):
    count, columns = part.shape
    shaped = part.reshape(count, columns // HEAD_DIM, HEAD_DIM)
    meansq = jnp.mean(shaped * shaped, axis=-1, keepdims=True)
    return (shaped * lax.rsqrt(meansq + 1e-06)).astype(BF16).reshape(count, columns)


def attend(queries, key_piece, value_piece):
    query_count, columns = queries.shape
    key_count = key_piece.shape[0]
    heads = columns // HEAD_DIM
    query_heads = queries.reshape(query_count, heads, HEAD_DIM)
    key_heads = key_piece.reshape(key_count, heads, HEAD_DIM)
    value_heads = value_piece.reshape(key_count, heads, HEAD_DIM)
    scores = jnp.einsum(
        "qhd,khd->hqk", query_heads, key_heads, preferred_element_type=F32
    ) * HEAD_DIM ** (-0.5)
    expw = jnp.exp(scores).astype(BF16)
    denom = jnp.sum(expw, axis=2, dtype=F32)
    numer = jnp.einsum("hqk,khd->qhd", expw, value_heads, preferred_element_type=F32)
    return (numer / denom.T[:, :, None]).astype(BF16).reshape(query_count, columns)


def on_device_general(
    expression, gene_mask, mask_value, w_qkv, w_out, w_first, w_second, cotangent
):
    groups = lax.axis_size("gene")
    local_blocks = w_first.shape[0]
    block_size = w_first.shape[1]
    block_total = local_blocks * groups
    cell_rows = expression.shape[0]
    masked_in = jnp.where(gene_mask == 1, mask_value[None, :], expression)
    qkv_part = jnp.dot(masked_in, w_qkv, preferred_element_type=F32)
    qkv_full = lax.psum(qkv_part.astype(BF16), "gene").astype(F32)
    columns = qkv_full.shape[1] // 3
    queries = normalize(qkv_full[:, :columns])
    keys_normed = normalize(qkv_full[:, columns : 2 * columns])
    values_b = qkv_full[:, 2 * columns :].astype(BF16)
    attended = attend(
        queries,
        lax.all_gather(keys_normed, "cell", axis=0, tiled=True),
        lax.all_gather(values_b, "cell", axis=0, tiled=True),
    )
    added = jnp.dot(attended, w_out, preferred_element_type=F32)
    hidden = (masked_in.astype(F32) + added).astype(BF16)
    blocks = hidden.reshape(cell_rows, local_blocks, block_size)
    first = jnp.einsum("cbi,bio->cbo", blocks, w_first, preferred_element_type=F32).astype(BF16)
    cot_blocks = cotangent.reshape(cell_rows, local_blocks, block_size)
    back_perm = jnp.einsum(
        "cjo,jko->cjk", cot_blocks, w_second, preferred_element_type=F32
    ).astype(BF16)
    back_send = back_perm.reshape(cell_rows, block_size // groups, block_total)
    received = lax.all_to_all(first, "gene", split_axis=2, concat_axis=1, tiled=True)
    permuted = jnp.swapaxes(received, 1, 2).reshape(cell_rows, local_blocks, block_size)
    mixed = jnp.einsum("cjk,jko->cjo", permuted, w_second, preferred_element_type=F32)
    denoised = (
        (blocks.astype(F32) + mixed).astype(BF16).reshape(cell_rows, local_blocks * block_size)
    )
    grad_second = jnp.einsum("cjk,cjo->jko", permuted, cot_blocks, preferred_element_type=F32)
    back_recv = lax.all_to_all(back_send, "gene", split_axis=2, concat_axis=1, tiled=True)
    back_first = jnp.swapaxes(back_recv, 1, 2)
    grad_first = jnp.einsum("cbi,cbo->bio", blocks, back_first, preferred_element_type=F32)
    first_share, second_share = (
        lax.psum_scatter(
            grad_first.astype(BF16), "cell", scatter_dimension=1, tiled=True
        ).astype(F32),
        lax.psum_scatter(
            grad_second.astype(BF16), "cell", scatter_dimension=1, tiled=True
        ).astype(F32),
    )
    return (denoised, first_share, second_share)


def after(value, *earlier):
    return lax.optimization_barrier((value, *earlier))[0]


def flip(value, axis, bit):
    pairs = [(i, i ^ bit) for i in range(lax.axis_size(axis))]
    return lax.ppermute(value, axis, pairs)


def call(body, me, args, in_specs, outs, out_specs, grid=(1,), scratch=(), aliases=None):
    return pl.pallas_call(
        body,
        out_shape=outs,
        grid_spec=pltpu.PrefetchScalarGridSpec(
            num_scalar_prefetch=1,
            grid=grid,
            in_specs=in_specs,
            out_specs=out_specs,
            scratch_shapes=list(scratch),
        ),
        input_output_aliases=aliases or {},
        compiler_params=pltpu.CompilerParams(vmem_limit_bytes=52 * 2**20),
        cost_estimate=pl.CostEstimate(flops=1, bytes_accessed=1, transcendentals=0),
    )(me, *args)


def spec(shape, place):
    return pl.BlockSpec(shape, place)


def whole(shape):
    return pl.BlockSpec(shape, lambda *_: (0,) * len(shape))


def several(count):
    return next(group for group in (4, 2, 1) if count % group == 0)


def array(shape, dtype):
    return jax.ShapeDtypeStruct(shape, dtype)


def grid_turn():
    rows = lax.broadcasted_iota(jnp.int32, (TILE * TILE, TILE * TILE), 0)
    columns = lax.broadcasted_iota(jnp.int32, (TILE * TILE, TILE * TILE), 1)
    return ((rows % TILE) * TILE + rows // TILE == columns).astype(BF16)


def turn(matrix, tile):
    rows = tile.shape[-1]
    flat = tile.reshape(TILE * TILE, rows)
    return jnp.dot(matrix, flat, preferred_element_type=F32).astype(BF16).reshape(TILE, TILE, rows)


def back_kernel(me_ref, turn_ref, second_ref, cot_ref, *refs):
    outs, held = refs[:4], refs[4]
    blocks, rows = held.shape[2], held.shape[3]
    group, size, _ = second_ref.shape
    pair = size // (4 * blocks)
    steps = TILE // (pair * group)
    at = pl.program_id(0) % steps
    for g in range(group):
        back = lax.dot_general(
            second_ref[g],
            cot_ref[:, g * size : (g + 1) * size],
            (((1,), (1,)), ((), ())),
            preferred_element_type=F32,
        ).astype(BF16)
        held[pl.ds((at * group + g) * pair, pair)] = back.reshape(pair, 4, blocks, rows)

    @pl.when(at == steps - 1)
    def _():
        for bits in range(4):
            there = me_ref[0] ^ bits
            for low in range(0, blocks, TILE):
                outs[bits][low : low + TILE] = turn(
                    turn_ref[...], held[:, there, low : low + TILE, :]
                )


def back_call(me, matrix, w_second, cotangent, part, parts):
    blocks, size, _ = w_second.shape
    rows = cotangent.shape[0]
    pair = size // (4 * blocks)
    count = blocks // parts
    group = several(math.gcd(count, TILE // pair))
    steps = TILE // (pair * group)
    first = part * count // group
    piece = array((blocks, count * pair, rows), BF16)
    return call(
        back_kernel,
        me,
        (matrix, w_second, cotangent),
        [
            whole(matrix.shape),
            spec((group, size, size), lambda j, _: (first + j, 0, 0)),
            spec((rows, group * size), lambda j, _: (0, first + j)),
        ],
        [piece] * 4,
        [spec((blocks, TILE, rows), lambda j, _: (0, j // steps, 0))] * 4,
        grid=(count // group,),
        scratch=[pltpu.VMEM((TILE, 4, blocks, rows), BF16)],
    )


def project_kernel(me_ref, value_ref, mask_ref, fill_ref, weight_ref, *refs):
    masked_ref, send_ref, keep_ref, total = refs
    step = pl.program_id(0)
    masked = jnp.where(
        mask_ref[...] == 1, fill_ref[...].astype(F32), value_ref[...].astype(F32)
    ).astype(BF16)
    masked_ref[...] = masked
    width = total.shape[1] // 3

    @pl.when(step == 0)
    def _():
        total[...] = jnp.dot(masked, weight_ref[...], preferred_element_type=F32)

    @pl.when(step > 0)
    def _():
        total[...] += jnp.dot(masked, weight_ref[...], preferred_element_type=F32)

    @pl.when(step == pl.num_programs(0) - 1)
    def _():
        share = width // 4
        for out, flips in ((send_ref, (1, 3)), (keep_ref, (0, 2))):
            for slot, bits in enumerate(flips):
                for kind in range(3):
                    place = pl.multiple_of(kind * width + (me_ref[0] ^ bits) * share, share)
                    out[slot, :, kind * share : (kind + 1) * share] = total[
                        :, pl.ds(place, share)
                    ].astype(out.dtype)


def project_call(me, expression, gene_mask, mask_value, w_qkv):
    rows, genes = expression.shape
    width = w_qkv.shape[1]
    depth = min(genes, 1024)
    wide = spec((rows, depth), lambda i, _: (0, i))
    shape = (2, rows, width // 4)
    return call(
        project_kernel,
        me,
        (expression, gene_mask, mask_value.reshape(1, genes), w_qkv),
        [
            wide,
            wide,
            spec((1, depth), lambda i, _: (0, i)),
            spec((depth, width), lambda i, _: (i, 0)),
        ],
        [array((rows, genes), BF16), array(shape, BF16), array(shape, F32)],
        [wide, whole(shape), whole(shape)],
        grid=(genes // depth,),
        scratch=[pltpu.VMEM((rows, width), F32)],
    )


def store_quarters(me, at, held, send_ref, keep_ref):
    quarter = held.shape[0] // 4
    for bits in range(4):
        start = pl.multiple_of((me ^ bits) * quarter, quarter)
        part = held[pl.ds(start, quarter), :]
        if bits % 2:
            send_ref[bits // 2][at] = part.astype(BF16)
        else:
            keep_ref[bits // 2, at] = part


def quarter_outs(count, group, size):
    shape = (count, size // 4, size)
    one = spec((group, *shape[1:]), lambda j, _: (j, 0, 0))
    two = spec((2, group, *shape[1:]), lambda j, _: (0, j, 0, 0))
    return [array(shape, BF16)] * 2 + [array((2, *shape), F32)], [one, one, two]


def add_kernel(_, keep_ref, came_ref, mine_ref, other_ref):
    mine_ref[...] = keep_ref[0] + came_ref[0].astype(F32)
    other_ref[...] = (keep_ref[1] + came_ref[1].astype(F32)).astype(BF16)


def add_call(me, keep, came):
    _, rows, columns = keep.shape
    some = rows // 4
    two = spec((2, some, columns), lambda i, _: (0, i, 0))
    one = spec((some, columns), lambda i, _: (i, 0))
    return call(
        add_kernel,
        me,
        (keep, came),
        [two, two],
        [array((rows, columns), F32), array((rows, columns), BF16)],
        [one, one],
        grid=(4,),
    )


def normalize_heads(part):
    columns = part.shape[1]
    heads = [lax.broadcasted_iota(jnp.int32, (columns, columns), d) // HEAD_DIM for d in (0, 1)]
    same = (heads[0] == heads[1]).astype(F32)
    sums = jnp.dot(
        part * part, same, precision=lax.Precision.HIGHEST, preferred_element_type=F32
    )
    return (part * lax.rsqrt(sums * (1.0 / HEAD_DIM) + 1e-06)).astype(BF16)


def pair_kernel(_, keep_ref, came_ref, next_ref, mine_ref, other_ref):
    mine_ref[...] = keep_ref[0] + came_ref[...].astype(F32)
    other_ref[...] = (keep_ref[1] + next_ref[...].astype(F32)).astype(BF16)


def pair_call(me, keep, came):
    shape = keep.shape[1:]
    return call(
        pair_kernel,
        me,
        (keep, *came),
        [whole(keep.shape), whole(shape), whole(shape)],
        [array(shape, F32), array(shape, BF16)],
        [whole(shape)] * 2,
    )


def finish_kernel(_, mine_ref, came_ref, *refs):
    refs[-1][...] = mine_ref[...] + came_ref[...].astype(F32)


def finish_call(me, mine, came, total, start, blocks):
    count, quarter, size = mine.shape
    step = math.gcd(count, start) if start else count
    args = [mine, came]
    in_specs = [spec((step, quarter, size), lambda i, _: (i, 0, 0))] * 2
    aliases = {}
    if total is not None:
        args.append(total)
        in_specs.append(pl.BlockSpec(memory_space=pl.ANY))
        aliases = {len(args): 0}
    return call(
        finish_kernel,
        me,
        args,
        in_specs,
        array((blocks, quarter, size), F32),
        spec((step, quarter, size), lambda i, _: (start // step + i, 0, 0)),
        grid=(count // step,),
        aliases=aliases,
    )


def split_kernel(_, mine_ref, came_ref, query_ref, out_ref):
    total = mine_ref[...] + came_ref[...].astype(F32)
    share = total.shape[1] // 3
    query_ref[...] = normalize_heads(total[:, :share])
    out_ref[:, :share] = normalize_heads(total[:, share : 2 * share])
    out_ref[:, share:] = total[:, 2 * share :].astype(BF16)


def split_call(me, mine, came):
    rows, columns = mine.shape
    wides = (columns // 3, 2 * columns // 3)
    some = rows // 4
    return call(
        split_kernel,
        me,
        (mine, came),
        [spec((some, columns), lambda i, _: (i, 0))] * 2,
        [array((rows, wide), BF16) for wide in wides],
        [spec((some, wide), lambda i, _: (i, 0)) for wide in wides],
        grid=(4,),
    )


def attend_kernel(_, query_ref, *refs):
    pieces, out_ref = refs[:-1], refs[-1]
    queries = query_ref[...]
    rows, share = queries.shape
    head_of = lax.broadcasted_iota(jnp.int32, (rows, share), 1) // HEAD_DIM
    out = jnp.zeros((rows, share), F32)
    for head in range(share // HEAD_DIM):
        query = jnp.where(head_of == head, queries.astype(F32) * HEAD_DIM**-0.5, 0.0).astype(BF16)
        numer = jnp.zeros((rows, share), F32)
        denom = jnp.zeros((rows, 1), F32)
        for piece in pieces:
            scores = lax.dot_general(
                query, piece[:, :share], (((1,), (1,)), ((), ())), preferred_element_type=F32
            )
            expw = jnp.exp(scores).astype(BF16)
            denom += jnp.sum(expw.astype(F32), axis=1, keepdims=True)
            numer += jnp.dot(expw, piece[:, share:], preferred_element_type=F32)
        out = jnp.where(head_of == head, numer / denom, out)
    out_ref[...] = out.astype(BF16)


def attend_call(me, queries, pieces):
    rows, share = queries.shape
    some = rows // 2
    part = spec((some, share), lambda i, _: (i, 0))
    return call(
        attend_kernel,
        me,
        (queries, *pieces),
        [part] + [whole(piece.shape) for piece in pieces],
        array((rows, share), BF16),
        part,
        grid=(2,),
    )


def first_kernel(me_ref, turn_ref, own, near, far, rest, w_out_ref, masked_ref, wf_ref, *refs):
    hidden_ref, outs, gathered, held = refs[0], refs[1:-2], refs[-2], refs[-1]
    step = pl.program_id(0)
    share = own.shape[1]
    group, size, _ = wf_ref.shape
    steps = TILE // group

    @pl.when(step == 0)
    def _():
        for bits, piece in enumerate((own, near, far, rest)):
            place = pl.multiple_of((me_ref[0] ^ bits) * share, share)
            gathered[:, pl.ds(place, share)] = piece[...]

    added = jnp.dot(gathered[...], w_out_ref[...], preferred_element_type=F32)
    hidden = (masked_ref[...].astype(F32) + added).astype(BF16)
    hidden_ref[...] = hidden
    for g in range(group):
        held[step % steps * group + g] = lax.dot_general(
            wf_ref[g],
            hidden[:, g * size : (g + 1) * size],
            (((1,), (1,)), ((), ())),
            preferred_element_type=F32,
        ).astype(BF16)

    @pl.when(step % steps == steps - 1)
    def _():
        deeps = [out.shape[1] for out in outs]
        deep = sum(deeps)
        for there in range(4):
            for low in range(0, deep, TILE):
                start = there * deep + low
                tile = turn(turn_ref[...], held[:, start : start + TILE, :])
                for chunk, count in enumerate(deeps):
                    begin = sum(deeps[:chunk])
                    least, most = max(begin, low), min(begin + count, low + TILE)
                    if least < most:
                        outs[chunk][there, least - begin : most - begin] = tile[
                            least - low : most - low
                        ]


def first_call(me, matrix, attended, w_out, masked, w_first_t, deeps):
    blocks, size, _ = w_first_t.shape
    rows, genes = masked.shape
    width = w_out.shape[0]
    group = several(TILE)
    steps = TILE // group
    wide = spec((rows, group * size), lambda b, _: (0, b))
    hidden, *first = call(
        first_kernel,
        me,
        (matrix, *attended, w_out, masked, w_first_t),
        [whole(matrix.shape)]
        + [whole(part.shape) for part in attended]
        + [
            spec((width, group * size), lambda b, _: (0, b)),
            wide,
            spec((group, size, size), lambda b, _: (b, 0, 0)),
        ],
        [array((rows, genes), BF16)] + [array((4, deep, blocks, rows), BF16) for deep in deeps],
        [wide]
        + [spec((4, deep, TILE, rows), lambda b, _: (0, 0, b // steps, 0)) for deep in deeps],
        grid=(blocks // group,),
        scratch=[pltpu.VMEM((rows, width), BF16), pltpu.VMEM((TILE, size, rows), BF16)],
    )
    return hidden, first


def second_kernel(me_ref, *refs):
    piece, w_ref, cot_ref, hidden_ref = refs[:4]
    out_ref, *send_ref, keep_ref, square = refs[-5:]
    group, size, _ = w_ref.shape
    pair = piece.shape[1] // group
    for g in range(group):
        at = slice(g * size, (g + 1) * size)
        permuted = jnp.concatenate(
            [piece[s, g * pair + o] for o in range(pair) for s in range(4)], axis=0
        )
        square[g] = jnp.dot(permuted, cot_ref[:, at], preferred_element_type=F32)
        store_quarters(me_ref[1], g, square.at[g], send_ref, keep_ref)
        mixed = lax.dot_general(
            permuted, w_ref[g], (((0,), (0,)), ((), ())), preferred_element_type=F32
        )
        out_ref[:, at] = (hidden_ref[:, at].astype(F32) + mixed).astype(BF16)


def second_call(me, piece, w_second, cotangent, hidden, denoised, start):
    blocks, size, _ = w_second.shape
    _, deep, _, rows = piece.shape
    pair = size // (4 * blocks)
    count = deep // pair
    group = several(math.gcd(count, start) if start else count)
    begin = start // group
    wide = spec((rows, group * size), lambda j, _: (0, begin + j))
    square = spec((group, size, size), lambda j, _: (begin + j, 0, 0))
    args = [piece, w_second, cotangent, hidden]
    in_specs = [
        spec((4, group * pair, blocks, rows), lambda j, _: (0, j, 0, 0)),
        square,
        wide,
        wide,
    ]
    quarters = quarter_outs(count, group, size)
    aliases = {}
    if denoised is not None:
        args.append(denoised)
        in_specs.append(pl.BlockSpec(memory_space=pl.ANY))
        aliases = {len(args): 0}
    return call(
        second_kernel,
        me,
        args,
        in_specs,
        [array(hidden.shape, BF16), *quarters[0]],
        [wide, *quarters[1]],
        grid=(count // group,),
        scratch=[pltpu.VMEM((group, size, size), F32)],
        aliases=aliases,
    )


def grad_first_kernel(me_ref, *refs):
    pieces, (hidden_ref, *send_ref, keep_ref, held, square) = refs[:-6], refs[-6:]
    group, size, _ = square.shape
    for g in range(group):
        for part in range(len(pieces) // 4):
            for bits in range(4):
                held[g, me_ref[0] ^ bits, part] = pieces[part * 4 + bits][g]
        back = held[g].reshape(size, held.shape[4])
        hidden = hidden_ref[:, g * size : (g + 1) * size]
        square[g] = jnp.dot(back, hidden, preferred_element_type=F32).T
        store_quarters(me_ref[1], g, square.at[g], send_ref, keep_ref)


def grad_first_call(me, pieces, hidden, size, start, count):
    _, deep, rows = pieces[0].shape
    group = several(math.gcd(count, start) if start else count)
    begin = start // group
    return call(
        grad_first_kernel,
        me,
        (*pieces, hidden),
        [spec((group, deep, rows), lambda b, _: (begin + b, 0, 0))] * len(pieces)
        + [spec((rows, group * size), lambda b, _: (0, begin + b))],
        *quarter_outs(count, group, size),
        grid=(count // group,),
        scratch=[
            pltpu.VMEM((group, 4, len(pieces) // 4, deep, rows), BF16),
            pltpu.VMEM((group, size, size), F32),
        ],
    )


def on_device_four(expression, gene_mask, mask_value, w_qkv, w_out, w_first, w_second, cotangent):
    me = jnp.stack([lax.axis_index("gene"), lax.axis_index("cell")]).astype(jnp.int32)
    blocks, size, _ = w_first.shape
    parts = 4
    deep = size // 4
    deeps = [deep // 2, 3 * deep // 8, deep // 8]
    matrix = grid_turn()
    sends, back = [None] * parts, [[None] * 4 for _ in range(parts)]

    def prepare(part, *earlier):
        sends[part] = back_call(me, matrix, w_second, after(cotangent, *earlier), part, parts)
        back[part][0] = sends[part][0]

    def begin(part, bits, *earlier):
        back[part][bits] = flip(after(sends[part][bits], *earlier), "gene", bits)
        return back[part][bits]

    def begin_pair(part, pair, *earlier):
        ends = [pair, pair[::-1]]
        return lax.ppermute(after(sends[part][3], *earlier), "gene", ends)

    prepare(0)
    beside_qkv = [begin(0, bits) for bits in (3, 2, 1)]
    prepare(1, sends[0][0])
    masked, send, keep = project_call(
        me, after(expression, sends[1][0]), gene_mask, mask_value, w_qkv
    )
    came = flip(after(send, *beside_qkv), "gene", 1)
    beside_sum = [begin(1, bits, send, *beside_qkv) for bits in (2, 3)]
    prepare(2, send)
    middle = begin_pair(2, (1, 2))
    prepare(3, sends[2][0])
    w_first_t = jnp.swapaxes(after(w_first, send), 1, 2)
    mine, other = add_call(
        me, keep, after(came, *beside_sum, middle, sends[3][0], w_first_t)
    )
    last = flip(other, "gene", 2)
    beside_sum = [begin(2, 2, other), begin(1, 1, other)]
    queries, key_value = split_call(me, mine, after(last, *beside_sum))
    across = flip(key_value, "cell", 2)
    beside = flip(key_value, "cell", 1)
    corner = flip(across, "cell", 1)
    outer = begin_pair(2, (0, 3), last)
    inner = (me[0] == 1) | (me[0] == 2)
    back[2][3] = jnp.where(inner, middle, outer)
    queries = after(queries, outer, begin(2, 1, last), beside, across, corner)
    attended = attend_call(me, queries, (key_value, beside, across, corner))
    near = flip(attended, "gene", 1)
    far = flip(attended, "gene", 2)
    rest = flip(after(far, near), "gene", 1)
    rest = after(rest, begin(3, 2, queries))
    hidden, first = first_call(
        me, matrix, (attended, near, far, rest), w_out, masked, w_first_t, deeps
    )
    begin(3, 3, rest)
    begin(3, 1, rest)

    got = []

    def launch(t, *earlier):
        piece = after(first[t], *earlier)
        got.append(lax.all_to_all(piece, "gene", split_axis=0, concat_axis=0, tiled=True))

    launch(0, back[3][3], back[3][1])
    denoised, shares = None, [None, None]
    back = sum(back, [])

    def sum_cells(which, start, send, keep):
        came = [flip(piece, "cell", 1) for piece in send]
        mine, other = pair_call(me, keep, came)
        last = flip(other, "cell", 2)
        shares[which] = finish_call(me, mine, last, shares[which], start, blocks)

    *send, keep = grad_first_call(me, back, hidden, size, 0, blocks // 2)
    *send_next, keep_next = grad_first_call(me, back, hidden, size, blocks // 2, blocks // 2)
    sum_cells(0, 0, send, keep)
    sum_cells(0, blocks // 2, send_next, keep_next)
    pin = shares[0]
    for t in range(len(deeps)):
        if t + 1 < len(deeps):
            launch(t + 1, got[t], pin)
        start = sum(deeps[:t]) * blocks // deep
        denoised, *send, keep = second_call(
            me, got[t], w_second, cotangent, hidden, denoised, start
        )
        sum_cells(1, start, send, keep)
        pin = shares[1]
    return (denoised, *shares)


def solution(mesh):
    placed = (
        P(("grp", "cell"), "gene"),
        P(("grp", "cell"), "gene"),
        P("gene"),
        P("gene", None),
        P(None, "gene"),
        P("gene", None, None),
        P("gene", None, None),
        P(("grp", "cell"), "gene"),
    )
    four = mesh.shape["gene"] == 4 and mesh.shape["cell"] == 4
    return jax.shard_map(
        on_device_four if four else on_device_general,
        mesh=mesh,
        in_specs=placed,
        out_specs=(
            P(("grp", "cell"), "gene"),
            P(("grp", "gene"), "cell", None),
            P(("grp", "gene"), "cell", None),
        ),
        check_vma=False,
    )
```

```python
import math

import jax
import jax.numpy as jnp
from jax import lax
from jax.experimental import pallas as pl
from jax.experimental.pallas import tpu as pltpu
from jax.sharding import PartitionSpec as P

HEADS = 16
HEAD_DIM = 64
TILE = 16
BF16 = jnp.bfloat16
F32 = jnp.float32


def normalize(part):
    count, columns = part.shape
    shaped = part.reshape(count, columns // HEAD_DIM, HEAD_DIM)
    meansq = jnp.mean(shaped * shaped, axis=-1, keepdims=True)
    return (shaped * lax.rsqrt(meansq + 1e-06)).astype(BF16).reshape(count, columns)


def attend(queries, key_piece, value_piece):
    query_count, columns = queries.shape
    key_count = key_piece.shape[0]
    heads = columns // HEAD_DIM
    query_heads = queries.reshape(query_count, heads, HEAD_DIM)
    key_heads = key_piece.reshape(key_count, heads, HEAD_DIM)
    value_heads = value_piece.reshape(key_count, heads, HEAD_DIM)
    scores = jnp.einsum(
        "qhd,khd->hqk", query_heads, key_heads, preferred_element_type=F32
    ) * HEAD_DIM ** (-0.5)
    expw = jnp.exp(scores).astype(BF16)
    denom = jnp.sum(expw, axis=2, dtype=F32)
    numer = jnp.einsum("hqk,khd->qhd", expw, value_heads, preferred_element_type=F32)
    return (numer / denom.T[:, :, None]).astype(BF16).reshape(query_count, columns)


def on_device_general(
    expression, gene_mask, mask_value, w_qkv, w_out, w_first, w_second, cotangent
):
    groups = lax.axis_size("gene")
    local_blocks = w_first.shape[0]
    block_size = w_first.shape[1]
    block_total = local_blocks * groups
    cell_rows = expression.shape[0]
    masked_in = jnp.where(gene_mask == 1, mask_value[None, :], expression)
    qkv_part = jnp.dot(masked_in, w_qkv, preferred_element_type=F32)
    qkv_full = lax.psum(qkv_part.astype(BF16), "gene").astype(F32)
    columns = qkv_full.shape[1] // 3
    queries = normalize(qkv_full[:, :columns])
    keys_normed = normalize(qkv_full[:, columns : 2 * columns])
    values_b = qkv_full[:, 2 * columns :].astype(BF16)
    attended = attend(
        queries,
        lax.all_gather(keys_normed, "cell", axis=0, tiled=True),
        lax.all_gather(values_b, "cell", axis=0, tiled=True),
    )
    added = jnp.dot(attended, w_out, preferred_element_type=F32)
    hidden = (masked_in.astype(F32) + added).astype(BF16)
    blocks = hidden.reshape(cell_rows, local_blocks, block_size)
    first = jnp.einsum("cbi,bio->cbo", blocks, w_first, preferred_element_type=F32).astype(BF16)
    cot_blocks = cotangent.reshape(cell_rows, local_blocks, block_size)
    back_perm = jnp.einsum(
        "cjo,jko->cjk", cot_blocks, w_second, preferred_element_type=F32
    ).astype(BF16)
    back_send = back_perm.reshape(cell_rows, block_size // groups, block_total)
    received = lax.all_to_all(first, "gene", split_axis=2, concat_axis=1, tiled=True)
    permuted = jnp.swapaxes(received, 1, 2).reshape(cell_rows, local_blocks, block_size)
    mixed = jnp.einsum("cjk,jko->cjo", permuted, w_second, preferred_element_type=F32)
    denoised = (
        (blocks.astype(F32) + mixed).astype(BF16).reshape(cell_rows, local_blocks * block_size)
    )
    grad_second = jnp.einsum("cjk,cjo->jko", permuted, cot_blocks, preferred_element_type=F32)
    back_recv = lax.all_to_all(back_send, "gene", split_axis=2, concat_axis=1, tiled=True)
    back_first = jnp.swapaxes(back_recv, 1, 2)
    grad_first = jnp.einsum("cbi,cbo->bio", blocks, back_first, preferred_element_type=F32)
    first_share, second_share = (
        lax.psum_scatter(
            grad_first.astype(BF16), "cell", scatter_dimension=1, tiled=True
        ).astype(F32),
        lax.psum_scatter(
            grad_second.astype(BF16), "cell", scatter_dimension=1, tiled=True
        ).astype(F32),
    )
    return (denoised, first_share, second_share)


def after(value, *earlier):
    return lax.optimization_barrier((value, *earlier))[0]


def flip(value, axis, bit):
    pairs = [(i, i ^ bit) for i in range(lax.axis_size(axis))]
    return lax.ppermute(value, axis, pairs)


def call(body, me, args, in_specs, outs, out_specs, grid=(1,), scratch=(), aliases=None):
    return pl.pallas_call(
        body,
        out_shape=outs,
        grid_spec=pltpu.PrefetchScalarGridSpec(
            num_scalar_prefetch=1,
            grid=grid,
            in_specs=in_specs,
            out_specs=out_specs,
            scratch_shapes=list(scratch),
        ),
        input_output_aliases=aliases or {},
        compiler_params=pltpu.CompilerParams(vmem_limit_bytes=52 * 2**20),
        cost_estimate=pl.CostEstimate(flops=1, bytes_accessed=1, transcendentals=0),
    )(me, *args)


def spec(shape, place):
    return pl.BlockSpec(shape, place)


def whole(shape):
    return pl.BlockSpec(shape, lambda *_: (0,) * len(shape))


def several(count):
    return next(group for group in (4, 2, 1) if count % group == 0)


def array(shape, dtype):
    return jax.ShapeDtypeStruct(shape, dtype)


def grid_turn():
    rows = lax.broadcasted_iota(jnp.int32, (TILE * TILE, TILE * TILE), 0)
    columns = lax.broadcasted_iota(jnp.int32, (TILE * TILE, TILE * TILE), 1)
    return ((rows % TILE) * TILE + rows // TILE == columns).astype(BF16)


def turn(matrix, tile):
    rows = tile.shape[-1]
    flat = tile.reshape(TILE * TILE, rows)
    return jnp.dot(matrix, flat, preferred_element_type=F32).astype(BF16).reshape(TILE, TILE, rows)


def back_kernel(_, turn_ref, second_ref, cot_ref, *refs):
    out, held = refs
    blocks, rows = held.shape[2], held.shape[3]
    group, size, _ = second_ref.shape
    pair = size // (4 * blocks)
    steps = TILE // (pair * group)
    at = pl.program_id(0) % steps
    for g in range(group):
        back = lax.dot_general(
            second_ref[g],
            cot_ref[:, g * size : (g + 1) * size],
            (((1,), (1,)), ((), ())),
            preferred_element_type=F32,
        ).astype(BF16)
        held[pl.ds((at * group + g) * pair, pair)] = back.reshape(pair, 4, blocks, rows)

    @pl.when(at == steps - 1)
    def _():
        for there in range(4):
            for low in range(0, blocks, TILE):
                out[there, low : low + TILE] = turn(
                    turn_ref[...], held[:, there, low : low + TILE, :]
                )


def back_call(me, matrix, w_second, cotangent, part, parts):
    blocks, size, _ = w_second.shape
    rows = cotangent.shape[0]
    pair = size // (4 * blocks)
    count = blocks // parts
    group = several(math.gcd(count, TILE // pair))
    steps = TILE // (pair * group)
    first = part * count // group
    return call(
        back_kernel,
        me,
        (matrix, w_second, cotangent),
        [
            whole(matrix.shape),
            spec((group, size, size), lambda j, _: (first + j, 0, 0)),
            spec((rows, group * size), lambda j, _: (0, first + j)),
        ],
        array((4, blocks, count * pair, rows), BF16),
        spec((4, blocks, TILE, rows), lambda j, _: (0, 0, j // steps, 0)),
        grid=(count // group,),
        scratch=[pltpu.VMEM((TILE, 4, blocks, rows), BF16)],
    )


def project_kernel(me_ref, value_ref, mask_ref, fill_ref, weight_ref, *refs):
    masked_ref, send_ref, keep_ref, total = refs
    step = pl.program_id(0)
    masked = jnp.where(
        mask_ref[...] == 1, fill_ref[...].astype(F32), value_ref[...].astype(F32)
    ).astype(BF16)
    masked_ref[...] = masked
    width = total.shape[1] // 3

    @pl.when(step == 0)
    def _():
        total[...] = jnp.dot(masked, weight_ref[...], preferred_element_type=F32)

    @pl.when(step > 0)
    def _():
        total[...] += jnp.dot(masked, weight_ref[...], preferred_element_type=F32)

    @pl.when(step == pl.num_programs(0) - 1)
    def _():
        share = width // 4
        for out, flips in ((send_ref, (1, 3)), (keep_ref, (0, 2))):
            for slot, bits in enumerate(flips):
                for kind in range(3):
                    place = pl.multiple_of(kind * width + (me_ref[0] ^ bits) * share, share)
                    out[slot, :, kind * share : (kind + 1) * share] = total[
                        :, pl.ds(place, share)
                    ].astype(out.dtype)


def project_call(me, expression, gene_mask, mask_value, w_qkv):
    rows, genes = expression.shape
    width = w_qkv.shape[1]
    depth = min(genes, 1024)
    wide = spec((rows, depth), lambda i, _: (0, i))
    shape = (2, rows, width // 4)
    return call(
        project_kernel,
        me,
        (expression, gene_mask, mask_value.reshape(1, genes), w_qkv),
        [
            wide,
            wide,
            spec((1, depth), lambda i, _: (0, i)),
            spec((depth, width), lambda i, _: (i, 0)),
        ],
        [array((rows, genes), BF16), array(shape, BF16), array(shape, F32)],
        [wide, whole(shape), whole(shape)],
        grid=(genes // depth,),
        scratch=[pltpu.VMEM((rows, width), F32)],
    )


def store_quarters(me, at, held, send_ref, keep_ref):
    quarter = held.shape[0] // 4
    for bits in range(4):
        start = pl.multiple_of((me ^ bits) * quarter, quarter)
        part = held[pl.ds(start, quarter), :]
        if bits % 2:
            send_ref[bits // 2][at] = part.astype(BF16)
        else:
            keep_ref[bits // 2, at] = part


def quarter_outs(count, group, size):
    shape = (count, size // 4, size)
    one = spec((group, *shape[1:]), lambda j, _: (j, 0, 0))
    two = spec((2, group, *shape[1:]), lambda j, _: (0, j, 0, 0))
    return [array(shape, BF16)] * 2 + [array((2, *shape), F32)], [one, one, two]


def add_kernel(_, keep_ref, came_ref, mine_ref, other_ref):
    mine_ref[...] = keep_ref[0] + came_ref[0].astype(F32)
    other_ref[...] = (keep_ref[1] + came_ref[1].astype(F32)).astype(BF16)


def add_call(me, keep, came):
    shape = keep.shape
    return call(
        add_kernel,
        me,
        (keep, came),
        [whole(shape), whole(shape)],
        [array(shape[1:], F32), array(shape[1:], BF16)],
        [whole(shape[1:])] * 2,
    )


def normalize_heads(part):
    columns = part.shape[1]
    heads = [lax.broadcasted_iota(jnp.int32, (columns, columns), d) // HEAD_DIM for d in (0, 1)]
    same = (heads[0] == heads[1]).astype(F32)
    sums = jnp.dot(
        part * part, same, precision=lax.Precision.HIGHEST, preferred_element_type=F32
    )
    return (part * lax.rsqrt(sums * (1.0 / HEAD_DIM) + 1e-06)).astype(BF16)


def pair_kernel(_, keep_ref, came_ref, next_ref, mine_ref, other_ref):
    mine_ref[...] = keep_ref[0] + came_ref[...].astype(F32)
    other_ref[...] = (keep_ref[1] + next_ref[...].astype(F32)).astype(BF16)


def pair_call(me, keep, came):
    shape = keep.shape[1:]
    return call(
        pair_kernel,
        me,
        (keep, *came),
        [whole(keep.shape), whole(shape), whole(shape)],
        [array(shape, F32), array(shape, BF16)],
        [whole(shape)] * 2,
    )


def finish_kernel(_, mine_ref, came_ref, *refs):
    refs[-1][...] = mine_ref[...] + came_ref[...].astype(F32)


def finish_call(me, mine, came, total, start, blocks):
    count, quarter, size = mine.shape
    step = math.gcd(count, start) if start else count
    args = [mine, came]
    in_specs = [spec((step, quarter, size), lambda i, _: (i, 0, 0))] * 2
    aliases = {}
    if total is not None:
        args.append(total)
        in_specs.append(pl.BlockSpec(memory_space=pl.ANY))
        aliases = {len(args): 0}
    return call(
        finish_kernel,
        me,
        args,
        in_specs,
        array((blocks, quarter, size), F32),
        spec((step, quarter, size), lambda i, _: (start // step + i, 0, 0)),
        grid=(count // step,),
        aliases=aliases,
    )


def split_kernel(_, mine_ref, came_ref, query_ref, out_ref):
    total = mine_ref[...] + came_ref[...].astype(F32)
    share = total.shape[1] // 3
    query_ref[...] = normalize_heads(total[:, :share])
    out_ref[:, :share] = normalize_heads(total[:, share : 2 * share])
    out_ref[:, share:] = total[:, 2 * share :].astype(BF16)


def split_call(me, mine, came):
    rows, columns = mine.shape
    shapes = ((rows, columns // 3), (rows, 2 * columns // 3))
    return call(
        split_kernel,
        me,
        (mine, came),
        [whole(mine.shape)] * 2,
        [array(shape, BF16) for shape in shapes],
        [whole(shape) for shape in shapes],
    )


def attend_kernel(_, query_ref, *refs):
    pieces, out_ref = refs[:-1], refs[-1]
    queries = query_ref[...]
    rows, share = queries.shape
    head_of = lax.broadcasted_iota(jnp.int32, (rows, share), 1) // HEAD_DIM
    out = jnp.zeros((rows, share), F32)
    for head in range(share // HEAD_DIM):
        query = jnp.where(head_of == head, queries.astype(F32) * HEAD_DIM**-0.5, 0.0).astype(BF16)
        numer = jnp.zeros((rows, share), F32)
        denom = jnp.zeros((rows, 1), F32)
        for piece in pieces:
            scores = lax.dot_general(
                query, piece[:, :share], (((1,), (1,)), ((), ())), preferred_element_type=F32
            )
            expw = jnp.exp(scores).astype(BF16)
            denom += jnp.sum(expw.astype(F32), axis=1, keepdims=True)
            numer += jnp.dot(expw, piece[:, share:], preferred_element_type=F32)
        out = jnp.where(head_of == head, numer / denom, out)
    out_ref[...] = out.astype(BF16)


def attend_call(me, queries, pieces):
    rows, share = queries.shape
    some = rows // 2
    part = spec((some, share), lambda i, _: (i, 0))
    return call(
        attend_kernel,
        me,
        (queries, *pieces),
        [part] + [whole(piece.shape) for piece in pieces],
        array((rows, share), BF16),
        part,
        grid=(2,),
    )


def first_kernel(me_ref, turn_ref, own, near, far, rest, w_out_ref, masked_ref, wf_ref, *refs):
    hidden_ref, outs, gathered, held = refs[0], refs[1:-2], refs[-2], refs[-1]
    step = pl.program_id(0)
    share = own.shape[1]
    group, size, _ = wf_ref.shape
    steps = TILE // group

    @pl.when(step == 0)
    def _():
        for bits, piece in enumerate((own, near, far, rest)):
            place = pl.multiple_of((me_ref[0] ^ bits) * share, share)
            gathered[:, pl.ds(place, share)] = piece[...]

    added = jnp.dot(gathered[...], w_out_ref[...], preferred_element_type=F32)
    hidden = (masked_ref[...].astype(F32) + added).astype(BF16)
    hidden_ref[...] = hidden
    for g in range(group):
        held[step % steps * group + g] = lax.dot_general(
            wf_ref[g],
            hidden[:, g * size : (g + 1) * size],
            (((1,), (1,)), ((), ())),
            preferred_element_type=F32,
        ).astype(BF16)

    @pl.when(step % steps == steps - 1)
    def _():
        deeps = [out.shape[1] for out in outs]
        deep = sum(deeps)
        for there in range(4):
            for low in range(0, deep, TILE):
                start = there * deep + low
                tile = turn(turn_ref[...], held[:, start : start + TILE, :])
                for chunk, count in enumerate(deeps):
                    begin = sum(deeps[:chunk])
                    least, most = max(begin, low), min(begin + count, low + TILE)
                    if least < most:
                        outs[chunk][there, least - begin : most - begin] = tile[
                            least - low : most - low
                        ]


def first_call(me, matrix, attended, w_out, masked, w_first_t, deeps):
    blocks, size, _ = w_first_t.shape
    rows, genes = masked.shape
    width = w_out.shape[0]
    group = several(TILE)
    steps = TILE // group
    wide = spec((rows, group * size), lambda b, _: (0, b))
    hidden, *first = call(
        first_kernel,
        me,
        (matrix, *attended, w_out, masked, w_first_t),
        [whole(matrix.shape)]
        + [whole(part.shape) for part in attended]
        + [
            spec((width, group * size), lambda b, _: (0, b)),
            wide,
            spec((group, size, size), lambda b, _: (b, 0, 0)),
        ],
        [array((rows, genes), BF16)] + [array((4, deep, blocks, rows), BF16) for deep in deeps],
        [wide]
        + [spec((4, deep, TILE, rows), lambda b, _: (0, 0, b // steps, 0)) for deep in deeps],
        grid=(blocks // group,),
        scratch=[pltpu.VMEM((rows, width), BF16), pltpu.VMEM((TILE, size, rows), BF16)],
    )
    return hidden, first


def second_kernel(me_ref, *refs):
    piece, w_ref, cot_ref, hidden_ref = refs[:4]
    out_ref, *send_ref, keep_ref, square = refs[-5:]
    group, size, _ = w_ref.shape
    pair = piece.shape[1] // group
    for g in range(group):
        at = slice(g * size, (g + 1) * size)
        permuted = jnp.concatenate(
            [piece[s, g * pair + o] for o in range(pair) for s in range(4)], axis=0
        )
        square[g] = jnp.dot(permuted, cot_ref[:, at], preferred_element_type=F32)
        store_quarters(me_ref[1], g, square.at[g], send_ref, keep_ref)
        mixed = lax.dot_general(
            permuted, w_ref[g], (((0,), (0,)), ((), ())), preferred_element_type=F32
        )
        out_ref[:, at] = (hidden_ref[:, at].astype(F32) + mixed).astype(BF16)


def second_call(me, piece, w_second, cotangent, hidden, denoised, start):
    blocks, size, _ = w_second.shape
    _, deep, _, rows = piece.shape
    pair = size // (4 * blocks)
    count = deep // pair
    group = several(math.gcd(count, start) if start else count)
    begin = start // group
    wide = spec((rows, group * size), lambda j, _: (0, begin + j))
    square = spec((group, size, size), lambda j, _: (begin + j, 0, 0))
    args = [piece, w_second, cotangent, hidden]
    in_specs = [
        spec((4, group * pair, blocks, rows), lambda j, _: (0, j, 0, 0)),
        square,
        wide,
        wide,
    ]
    quarters = quarter_outs(count, group, size)
    aliases = {}
    if denoised is not None:
        args.append(denoised)
        in_specs.append(pl.BlockSpec(memory_space=pl.ANY))
        aliases = {len(args): 0}
    return call(
        second_kernel,
        me,
        args,
        in_specs,
        [array(hidden.shape, BF16), *quarters[0]],
        [wide, *quarters[1]],
        grid=(count // group,),
        scratch=[pltpu.VMEM((group, size, size), F32)],
        aliases=aliases,
    )


def grad_first_kernel(me_ref, *refs):
    pieces, (hidden_ref, *send_ref, keep_ref, square) = refs[:-5], refs[-5:]
    group, size, _ = square.shape
    for g in range(group):
        back = jnp.concatenate([piece[s, g] for s in range(4) for piece in pieces], axis=0)
        hidden = hidden_ref[:, g * size : (g + 1) * size]
        square[g] = jnp.dot(back, hidden, preferred_element_type=F32).T
        store_quarters(me_ref[1], g, square.at[g], send_ref, keep_ref)


def grad_first_call(me, pieces, hidden, size, start, count):
    _, _, deep, rows = pieces[0].shape
    group = several(math.gcd(count, start) if start else count)
    begin = start // group
    return call(
        grad_first_kernel,
        me,
        (*pieces, hidden),
        [spec((4, group, deep, rows), lambda b, _: (0, begin + b, 0, 0))] * len(pieces)
        + [spec((rows, group * size), lambda b, _: (0, begin + b))],
        *quarter_outs(count, group, size),
        grid=(count // group,),
        scratch=[pltpu.VMEM((group, size, size), F32)],
    )


def on_device_four(expression, gene_mask, mask_value, w_qkv, w_out, w_first, w_second, cotangent):
    me = jnp.stack([lax.axis_index("gene"), lax.axis_index("cell")]).astype(jnp.int32)
    blocks, size, _ = w_first.shape
    deep = size // 4
    deeps = [deep // 2, 3 * deep // 8, deep // 8]
    matrix = grid_turn()

    def swap_genes(piece, *earlier):
        piece = after(piece, *earlier)
        return lax.all_to_all(piece, "gene", split_axis=0, concat_axis=0, tiled=True)

    back_send = back_call(me, matrix, w_second, cotangent, 0, 2)
    back = [swap_genes(back_send)]
    masked, send, keep = project_call(
        me, after(expression, back_send), gene_mask, mask_value, w_qkv
    )
    came = flip(send, "gene", 1)
    back_send = back_call(me, matrix, w_second, after(cotangent, send), 1, 2)
    w_first_t = jnp.swapaxes(after(w_first, send), 1, 2)
    mine, other = add_call(me, keep, after(came, *back, back_send, w_first_t))
    last = flip(other, "gene", 2)
    queries, key_value = split_call(me, mine, last)
    back.append(swap_genes(back_send, last))
    across = flip(key_value, "cell", 2)
    beside = flip(key_value, "cell", 1)
    corner = flip(across, "cell", 1)
    attended = attend_call(me, queries, (key_value, beside, across, corner))
    near = flip(attended, "gene", 1)
    far = flip(attended, "gene", 2)
    rest = flip(after(far, near), "gene", 1)
    hidden, first = first_call(
        me, matrix, (attended, near, far, rest), w_out, masked, w_first_t, deeps
    )

    got = []

    def launch(t, *earlier):
        got.append(swap_genes(first[t], *earlier))

    launch(0, back[1])
    denoised, shares = None, [None, None]

    def sum_cells(which, start, send, keep):
        came = [flip(piece, "cell", 1) for piece in send]
        mine, other = pair_call(me, keep, came)
        last = flip(other, "cell", 2)
        shares[which] = finish_call(me, mine, last, shares[which], start, blocks)

    *send, keep = grad_first_call(me, back, hidden, size, 0, blocks // 2)
    *send_next, keep_next = grad_first_call(me, back, hidden, size, blocks // 2, blocks // 2)
    sum_cells(0, 0, send, keep)
    sum_cells(0, blocks // 2, send_next, keep_next)
    pin = shares[0]
    for t in range(len(deeps)):
        if t + 1 < len(deeps):
            launch(t + 1, got[t], pin)
        start = sum(deeps[:t]) * blocks // deep
        denoised, *send, keep = second_call(
            me, got[t], w_second, cotangent, hidden, denoised, start
        )
        sum_cells(1, start, send, keep)
        pin = shares[1]
    return (denoised, *shares)


def solution(mesh):
    placed = (
        P(("grp", "cell"), "gene"),
        P(("grp", "cell"), "gene"),
        P("gene"),
        P("gene", None),
        P(None, "gene"),
        P("gene", None, None),
        P("gene", None, None),
        P(("grp", "cell"), "gene"),
    )
    four = mesh.shape["gene"] == 4 and mesh.shape["cell"] == 4
    return jax.shard_map(
        on_device_four if four else on_device_general,
        mesh=mesh,
        in_specs=placed,
        out_specs=(
            P(("grp", "cell"), "gene"),
            P(("grp", "gene"), "cell", None),
            P(("grp", "gene"), "cell", None),
        ),
        check_vma=False,
    )
```

```python
import math

import jax
import jax.numpy as jnp
from jax import lax
from jax.experimental import pallas as pl
from jax.experimental.pallas import tpu as pltpu
from jax.sharding import PartitionSpec as P

HEADS = 16
HEAD_DIM = 64
TILE = 16
BF16 = jnp.bfloat16
F32 = jnp.float32


def normalize(part):
    count, columns = part.shape
    shaped = part.reshape(count, columns // HEAD_DIM, HEAD_DIM)
    meansq = jnp.mean(shaped * shaped, axis=-1, keepdims=True)
    return (shaped * lax.rsqrt(meansq + 1e-06)).astype(BF16).reshape(count, columns)


def attend(queries, key_piece, value_piece):
    query_count, columns = queries.shape
    key_count = key_piece.shape[0]
    heads = columns // HEAD_DIM
    query_heads = queries.reshape(query_count, heads, HEAD_DIM)
    key_heads = key_piece.reshape(key_count, heads, HEAD_DIM)
    value_heads = value_piece.reshape(key_count, heads, HEAD_DIM)
    scores = jnp.einsum(
        "qhd,khd->hqk", query_heads, key_heads, preferred_element_type=F32
    ) * HEAD_DIM ** (-0.5)
    expw = jnp.exp(scores).astype(BF16)
    denom = jnp.sum(expw, axis=2, dtype=F32)
    numer = jnp.einsum("hqk,khd->qhd", expw, value_heads, preferred_element_type=F32)
    return (numer / denom.T[:, :, None]).astype(BF16).reshape(query_count, columns)


def on_device_general(
    expression, gene_mask, mask_value, w_qkv, w_out, w_first, w_second, cotangent
):
    groups = lax.axis_size("gene")
    local_blocks = w_first.shape[0]
    block_size = w_first.shape[1]
    block_total = local_blocks * groups
    cell_rows = expression.shape[0]
    masked_in = jnp.where(gene_mask == 1, mask_value[None, :], expression)
    qkv_part = jnp.dot(masked_in, w_qkv, preferred_element_type=F32)
    qkv_full = lax.psum(qkv_part.astype(BF16), "gene").astype(F32)
    columns = qkv_full.shape[1] // 3
    queries = normalize(qkv_full[:, :columns])
    keys_normed = normalize(qkv_full[:, columns : 2 * columns])
    values_b = qkv_full[:, 2 * columns :].astype(BF16)
    attended = attend(
        queries,
        lax.all_gather(keys_normed, "cell", axis=0, tiled=True),
        lax.all_gather(values_b, "cell", axis=0, tiled=True),
    )
    added = jnp.dot(attended, w_out, preferred_element_type=F32)
    hidden = (masked_in.astype(F32) + added).astype(BF16)
    blocks = hidden.reshape(cell_rows, local_blocks, block_size)
    first = jnp.einsum("cbi,bio->cbo", blocks, w_first, preferred_element_type=F32).astype(BF16)
    cot_blocks = cotangent.reshape(cell_rows, local_blocks, block_size)
    back_perm = jnp.einsum(
        "cjo,jko->cjk", cot_blocks, w_second, preferred_element_type=F32
    ).astype(BF16)
    back_send = back_perm.reshape(cell_rows, block_size // groups, block_total)
    received = lax.all_to_all(first, "gene", split_axis=2, concat_axis=1, tiled=True)
    permuted = jnp.swapaxes(received, 1, 2).reshape(cell_rows, local_blocks, block_size)
    mixed = jnp.einsum("cjk,jko->cjo", permuted, w_second, preferred_element_type=F32)
    denoised = (
        (blocks.astype(F32) + mixed).astype(BF16).reshape(cell_rows, local_blocks * block_size)
    )
    grad_second = jnp.einsum("cjk,cjo->jko", permuted, cot_blocks, preferred_element_type=F32)
    back_recv = lax.all_to_all(back_send, "gene", split_axis=2, concat_axis=1, tiled=True)
    back_first = jnp.swapaxes(back_recv, 1, 2)
    grad_first = jnp.einsum("cbi,cbo->bio", blocks, back_first, preferred_element_type=F32)
    first_share, second_share = (
        lax.psum_scatter(
            grad_first.astype(BF16), "cell", scatter_dimension=1, tiled=True
        ).astype(F32),
        lax.psum_scatter(
            grad_second.astype(BF16), "cell", scatter_dimension=1, tiled=True
        ).astype(F32),
    )
    return (denoised, first_share, second_share)


def after(value, *earlier):
    return lax.optimization_barrier((value, *earlier))[0]


def flip(value, axis, bit):
    pairs = [(i, i ^ bit) for i in range(lax.axis_size(axis))]
    return lax.ppermute(value, axis, pairs)


def call(body, me, args, in_specs, outs, out_specs, grid=(1,), scratch=(), aliases=None):
    return pl.pallas_call(
        body,
        out_shape=outs,
        grid_spec=pltpu.PrefetchScalarGridSpec(
            num_scalar_prefetch=1,
            grid=grid,
            in_specs=in_specs,
            out_specs=out_specs,
            scratch_shapes=list(scratch),
        ),
        input_output_aliases=aliases or {},
        compiler_params=pltpu.CompilerParams(vmem_limit_bytes=52 * 2**20),
        cost_estimate=pl.CostEstimate(flops=1, bytes_accessed=1, transcendentals=0),
    )(me, *args)


def spec(shape, place):
    return pl.BlockSpec(shape, place)


def whole(shape):
    return pl.BlockSpec(shape, lambda *_: (0,) * len(shape))


def several(count):
    return next(group for group in (4, 2, 1) if count % group == 0)


def array(shape, dtype):
    return jax.ShapeDtypeStruct(shape, dtype)


def grid_turn():
    rows = lax.broadcasted_iota(jnp.int32, (TILE * TILE, TILE * TILE), 0)
    columns = lax.broadcasted_iota(jnp.int32, (TILE * TILE, TILE * TILE), 1)
    return ((rows % TILE) * TILE + rows // TILE == columns).astype(BF16)


def turn(matrix, tile):
    rows = tile.shape[-1]
    flat = tile.reshape(TILE * TILE, rows)
    return jnp.dot(matrix, flat, preferred_element_type=F32).astype(BF16).reshape(TILE, TILE, rows)


def back_kernel(me_ref, turn_ref, second_ref, cot_ref, *refs):
    outs, held = refs[:4], refs[4]
    blocks, rows = held.shape[2], held.shape[3]
    group, size, _ = second_ref.shape
    pair = size // (4 * blocks)
    steps = TILE // (pair * group)
    at = pl.program_id(0) % steps
    for g in range(group):
        back = lax.dot_general(
            second_ref[g],
            cot_ref[:, g * size : (g + 1) * size],
            (((1,), (1,)), ((), ())),
            preferred_element_type=F32,
        ).astype(BF16)
        held[pl.ds((at * group + g) * pair, pair)] = back.reshape(pair, 4, blocks, rows)

    @pl.when(at == steps - 1)
    def _():
        for bits in range(4):
            there = me_ref[0] ^ bits
            for low in range(0, blocks, TILE):
                outs[bits][low : low + TILE] = turn(
                    turn_ref[...], held[:, there, low : low + TILE, :]
                )


def back_call(me, matrix, w_second, cotangent, start, count):
    blocks, size, _ = w_second.shape
    rows = cotangent.shape[0]
    pair = size // (4 * blocks)
    group = several(math.gcd(count, TILE // pair))
    steps = TILE // (pair * group)
    first = start // group
    piece = array((blocks, count * pair, rows), BF16)
    return call(
        back_kernel,
        me,
        (matrix, w_second, cotangent),
        [
            whole(matrix.shape),
            spec((group, size, size), lambda j, _: (first + j, 0, 0)),
            spec((rows, group * size), lambda j, _: (0, first + j)),
        ],
        [piece] * 4,
        [spec((blocks, TILE, rows), lambda j, _: (0, j // steps, 0))] * 4,
        grid=(count // group,),
        scratch=[pltpu.VMEM((TILE, 4, blocks, rows), BF16)],
    )


def project_kernel(me_ref, value_ref, mask_ref, fill_ref, weight_ref, *refs):
    masked_ref, send_ref, keep_ref, total = refs
    step = pl.program_id(0)
    masked = jnp.where(
        mask_ref[...] == 1, fill_ref[...].astype(F32), value_ref[...].astype(F32)
    ).astype(BF16)
    masked_ref[...] = masked
    width = total.shape[1] // 3

    @pl.when(step == 0)
    def _():
        total[...] = jnp.dot(masked, weight_ref[...], preferred_element_type=F32)

    @pl.when(step > 0)
    def _():
        total[...] += jnp.dot(masked, weight_ref[...], preferred_element_type=F32)

    @pl.when(step == pl.num_programs(0) - 1)
    def _():
        share = width // 4
        for out, flips in ((send_ref, (1, 3)), (keep_ref, (0, 2))):
            for slot, bits in enumerate(flips):
                for kind in range(3):
                    place = pl.multiple_of(kind * width + (me_ref[0] ^ bits) * share, share)
                    out[slot, :, kind * share : (kind + 1) * share] = total[
                        :, pl.ds(place, share)
                    ].astype(out.dtype)


def project_call(me, expression, gene_mask, mask_value, w_qkv):
    rows, genes = expression.shape
    width = w_qkv.shape[1]
    depth = min(genes, 1024)
    wide = spec((rows, depth), lambda i, _: (0, i))
    shape = (2, rows, width // 4)
    return call(
        project_kernel,
        me,
        (expression, gene_mask, mask_value.reshape(1, genes), w_qkv),
        [
            wide,
            wide,
            spec((1, depth), lambda i, _: (0, i)),
            spec((depth, width), lambda i, _: (i, 0)),
        ],
        [array((rows, genes), BF16), array(shape, BF16), array(shape, F32)],
        [wide, whole(shape), whole(shape)],
        grid=(genes // depth,),
        scratch=[pltpu.VMEM((rows, width), F32)],
    )


def store_quarters(me, at, held, send_ref, keep_ref):
    quarter = held.shape[0] // 4
    for bits in range(4):
        start = pl.multiple_of((me ^ bits) * quarter, quarter)
        part = held[pl.ds(start, quarter), :]
        if bits % 2:
            send_ref[bits // 2][at] = part.astype(BF16)
        else:
            keep_ref[bits // 2, at] = part


def quarter_outs(count, group, size):
    shape = (count, size // 4, size)
    one = spec((group, *shape[1:]), lambda j, _: (j, 0, 0))
    two = spec((2, group, *shape[1:]), lambda j, _: (0, j, 0, 0))
    return [array(shape, BF16)] * 2 + [array((2, *shape), F32)], [one, one, two]


def add_kernel(_, keep_ref, came_ref, mine_ref, other_ref):
    mine_ref[...] = keep_ref[0] + came_ref[0].astype(F32)
    other_ref[...] = (keep_ref[1] + came_ref[1].astype(F32)).astype(BF16)


def add_call(me, keep, came):
    shape = keep.shape
    return call(
        add_kernel,
        me,
        (keep, came),
        [whole(shape), whole(shape)],
        [array(shape[1:], F32), array(shape[1:], BF16)],
        [whole(shape[1:])] * 2,
    )


def normalize_heads(part):
    columns = part.shape[1]
    heads = [lax.broadcasted_iota(jnp.int32, (columns, columns), d) // HEAD_DIM for d in (0, 1)]
    same = (heads[0] == heads[1]).astype(F32)
    sums = jnp.dot(
        part * part, same, precision=lax.Precision.HIGHEST, preferred_element_type=F32
    )
    return (part * lax.rsqrt(sums * (1.0 / HEAD_DIM) + 1e-06)).astype(BF16)


def pair_kernel(_, keep_ref, came_ref, next_ref, mine_ref, other_ref):
    mine_ref[...] = keep_ref[0] + came_ref[...].astype(F32)
    other_ref[...] = (keep_ref[1] + next_ref[...].astype(F32)).astype(BF16)


def pair_call(me, keep, came):
    shape = keep.shape[1:]
    return call(
        pair_kernel,
        me,
        (keep, *came),
        [whole(keep.shape), whole(shape), whole(shape)],
        [array(shape, F32), array(shape, BF16)],
        [whole(shape)] * 2,
    )


def finish_kernel(_, mine_ref, came_ref, *refs):
    refs[-1][...] = mine_ref[...] + came_ref[...].astype(F32)


def finish_call(me, mine, came, total, start, blocks):
    count, quarter, size = mine.shape
    step = math.gcd(count, start) if start else count
    args = [mine, came]
    in_specs = [spec((step, quarter, size), lambda i, _: (i, 0, 0))] * 2
    aliases = {}
    if total is not None:
        args.append(total)
        in_specs.append(pl.BlockSpec(memory_space=pl.ANY))
        aliases = {len(args): 0}
    return call(
        finish_kernel,
        me,
        args,
        in_specs,
        array((blocks, quarter, size), F32),
        spec((step, quarter, size), lambda i, _: (start // step + i, 0, 0)),
        grid=(count // step,),
        aliases=aliases,
    )


def split_kernel(_, mine_ref, came_ref, query_ref, out_ref):
    total = mine_ref[...] + came_ref[...].astype(F32)
    share = total.shape[1] // 3
    query_ref[...] = normalize_heads(total[:, :share])
    out_ref[:, :share] = normalize_heads(total[:, share : 2 * share])
    out_ref[:, share:] = total[:, 2 * share :].astype(BF16)


def split_call(me, mine, came):
    rows, columns = mine.shape
    shapes = ((rows, columns // 3), (rows, 2 * columns // 3))
    return call(
        split_kernel,
        me,
        (mine, came),
        [whole(mine.shape)] * 2,
        [array(shape, BF16) for shape in shapes],
        [whole(shape) for shape in shapes],
    )


def attend_kernel(_, query_ref, *refs):
    pieces, out_ref = refs[:-1], refs[-1]
    queries = query_ref[...]
    rows, share = queries.shape
    head_of = lax.broadcasted_iota(jnp.int32, (rows, share), 1) // HEAD_DIM
    out = jnp.zeros((rows, share), F32)
    for head in range(share // HEAD_DIM):
        query = jnp.where(head_of == head, queries.astype(F32) * HEAD_DIM**-0.5, 0.0).astype(BF16)
        numer = jnp.zeros((rows, share), F32)
        denom = jnp.zeros((rows, 1), F32)
        for piece in pieces:
            scores = lax.dot_general(
                query, piece[:, :share], (((1,), (1,)), ((), ())), preferred_element_type=F32
            )
            expw = jnp.exp(scores).astype(BF16)
            denom += jnp.sum(expw.astype(F32), axis=1, keepdims=True)
            numer += jnp.dot(expw, piece[:, share:], preferred_element_type=F32)
        out = jnp.where(head_of == head, numer / denom, out)
    out_ref[...] = out.astype(BF16)


def attend_call(me, queries, pieces):
    rows, share = queries.shape
    some = rows // 2
    part = spec((some, share), lambda i, _: (i, 0))
    return call(
        attend_kernel,
        me,
        (queries, *pieces),
        [part] + [whole(piece.shape) for piece in pieces],
        array((rows, share), BF16),
        part,
        grid=(2,),
    )


def first_kernel(me_ref, turn_ref, own, near, far, rest, w_out_ref, masked_ref, wf_ref, *refs):
    hidden_ref, outs, gathered, held = refs[0], refs[1:-2], refs[-2], refs[-1]
    step = pl.program_id(0)
    share = own.shape[1]
    group, size, _ = wf_ref.shape
    steps = TILE // group

    @pl.when(step == 0)
    def _():
        for bits, piece in enumerate((own, near, far, rest)):
            place = pl.multiple_of((me_ref[0] ^ bits) * share, share)
            gathered[:, pl.ds(place, share)] = piece[...]

    added = jnp.dot(gathered[...], w_out_ref[...], preferred_element_type=F32)
    hidden = (masked_ref[...].astype(F32) + added).astype(BF16)
    hidden_ref[...] = hidden
    for g in range(group):
        held[step % steps * group + g] = lax.dot_general(
            wf_ref[g],
            hidden[:, g * size : (g + 1) * size],
            (((1,), (1,)), ((), ())),
            preferred_element_type=F32,
        ).astype(BF16)

    @pl.when(step % steps == steps - 1)
    def _():
        chunks = []
        rest = list(outs)
        while rest:
            swapped = len(rest[0].shape) == 4
            refs = rest[: 1 if swapped else 4]
            rest = rest[len(refs) :]
            chunks.append((refs, refs[0].shape[1 if swapped else 0]))
        deep = sum(count for _, count in chunks)
        for bits in range(4):
            there = me_ref[0] ^ bits
            for low in range(0, deep, TILE):
                start = pl.multiple_of(there * deep + low, TILE)
                tile = turn(turn_ref[...], held[:, pl.ds(start, TILE), :])
                begin = 0
                for refs, count in chunks:
                    least, most = max(begin, low), min(begin + count, low + TILE)
                    if least < most:
                        target = refs[0].at[there] if len(refs) == 1 else refs[bits]
                        target[least - begin : most - begin] = tile[least - low : most - low]
                    begin += count


def first_call(me, matrix, attended, w_out, masked, w_first_t, chunks):
    blocks, size, _ = w_first_t.shape
    rows, genes = masked.shape
    width = w_out.shape[0]
    group = several(TILE)
    steps = TILE // group
    wide = spec((rows, group * size), lambda b, _: (0, b))
    outs, places = [array((rows, genes), BF16)], [wide]
    for deep, swapped in chunks:
        if swapped:
            outs.append(array((4, deep, blocks, rows), BF16))
            places.append(spec((4, deep, TILE, rows), lambda b, _: (0, 0, b // steps, 0)))
        else:
            outs += [array((deep, blocks, rows), BF16)] * 4
            places += [spec((deep, TILE, rows), lambda b, _: (0, b // steps, 0))] * 4
    hidden, *first = call(
        first_kernel,
        me,
        (matrix, *attended, w_out, masked, w_first_t),
        [whole(matrix.shape)]
        + [whole(part.shape) for part in attended]
        + [
            spec((width, group * size), lambda b, _: (0, b)),
            wide,
            spec((group, size, size), lambda b, _: (b, 0, 0)),
        ],
        outs,
        places,
        grid=(blocks // group,),
        scratch=[pltpu.VMEM((rows, width), BF16), pltpu.VMEM((TILE, size, rows), BF16)],
    )
    taken = []
    for _, swapped in chunks:
        wanted = 1 if swapped else 4
        taken.append(first[:wanted])
        first = first[wanted:]
    return hidden, taken


def second_kernel(me_ref, *refs):
    pieces = refs[: 1 if len(refs[0].shape) == 4 else 4]
    w_ref, cot_ref, hidden_ref = refs[len(pieces) : len(pieces) + 3]
    out_ref, *send_ref, keep_ref, square, held = refs[-6:]
    group, size, _ = w_ref.shape
    pair = held.shape[1]
    for g in range(group):
        at = slice(g * size, (g + 1) * size)
        mine = slice(g * pair, (g + 1) * pair)
        if len(pieces) == 1:
            for source in range(4):
                held[g, :, source] = pieces[0][source, mine]
        else:
            for bits in range(4):
                held[g, :, me_ref[0] ^ bits] = pieces[bits][mine]
        permuted = held[g].reshape(size, held.shape[4])
        square[g] = jnp.dot(permuted, cot_ref[:, at], preferred_element_type=F32)
        store_quarters(me_ref[1], g, square.at[g], send_ref, keep_ref)
        mixed = lax.dot_general(
            permuted, w_ref[g], (((0,), (0,)), ((), ())), preferred_element_type=F32
        )
        out_ref[:, at] = (hidden_ref[:, at].astype(F32) + mixed).astype(BF16)


def second_call(me, pieces, w_second, cotangent, hidden, denoised, start):
    blocks, size, _ = w_second.shape
    deep, _, rows = pieces[0].shape[-3:]
    pair = size // (4 * blocks)
    count = deep // pair
    group = several(math.gcd(count, start) if start else count)
    begin = start // group
    wide = spec((rows, group * size), lambda j, _: (0, begin + j))
    square = spec((group, size, size), lambda j, _: (begin + j, 0, 0))
    args = [*pieces, w_second, cotangent, hidden]
    part = (group * pair, blocks, rows)
    if len(pieces) == 1:
        in_specs = [spec((4, *part), lambda j, _: (0, j, 0, 0))]
    else:
        in_specs = [spec(part, lambda j, _: (j, 0, 0))] * 4
    in_specs += [square, wide, wide]
    quarters = quarter_outs(count, group, size)
    aliases = {}
    if denoised is not None:
        args.append(denoised)
        in_specs.append(pl.BlockSpec(memory_space=pl.ANY))
        aliases = {len(args): 0}
    return call(
        second_kernel,
        me,
        args,
        in_specs,
        [array(hidden.shape, BF16), *quarters[0]],
        [wide, *quarters[1]],
        grid=(count // group,),
        scratch=[
            pltpu.VMEM((group, size, size), F32),
            pltpu.VMEM((group, pair, 4, blocks, rows), BF16),
        ],
        aliases=aliases,
    )


def grad_first_kernel(me_ref, *refs):
    pieces, (hidden_ref, *send_ref, keep_ref, held, square) = refs[:-6], refs[-6:]
    group, size, _ = square.shape
    for g in range(group):
        low = 0
        for part in range(0, len(pieces), 4):
            deep = pieces[part].shape[1]
            for bits in range(4):
                held[g, me_ref[0] ^ bits, low : low + deep] = pieces[part + bits][g]
            low += deep
        back = held[g].reshape(size, held.shape[3])
        hidden = hidden_ref[:, g * size : (g + 1) * size]
        square[g] = jnp.dot(back, hidden, preferred_element_type=F32).T
        store_quarters(me_ref[1], g, square.at[g], send_ref, keep_ref)


def grad_first_call(me, pieces, hidden, size, start, count):
    rows = hidden.shape[0]
    group = several(math.gcd(count, start) if start else count)
    begin = start // group
    return call(
        grad_first_kernel,
        me,
        (*pieces, hidden),
        [spec((group, *piece.shape[1:]), lambda b, _: (begin + b, 0, 0)) for piece in pieces]
        + [spec((rows, group * size), lambda b, _: (0, begin + b))],
        *quarter_outs(count, group, size),
        grid=(count // group,),
        scratch=[
            pltpu.VMEM((group, 4, size // 4, rows), BF16),
            pltpu.VMEM((group, size, size), F32),
        ],
    )


def on_device_four(expression, gene_mask, mask_value, w_qkv, w_out, w_first, w_second, cotangent):
    me = jnp.stack([lax.axis_index("gene"), lax.axis_index("cell")]).astype(jnp.int32)
    blocks, size, _ = w_first.shape
    deep = size // 4
    counts = [blocks // 4, blocks // 2, blocks // 4]
    chunks = [(deep // 2, True), (3 * deep // 8, True), (deep // 8, True)]
    matrix = grid_turn()
    sends, back = [None] * 3, [[None] * 4 for _ in range(3)]

    def prepare(part, *earlier):
        sends[part] = back_call(
            me, matrix, w_second, after(cotangent, *earlier), sum(counts[:part]), counts[part]
        )
        back[part][0] = sends[part][0]

    def begin(part, bits, *earlier):
        back[part][bits] = flip(after(sends[part][bits], *earlier), "gene", bits)
        return back[part][bits]

    prepare(0)
    beside_qkv = [begin(0, bits) for bits in (3, 2, 1)]
    prepare(1, sends[0][0])
    masked, send, keep = project_call(
        me, after(expression, sends[1][0]), gene_mask, mask_value, w_qkv
    )
    came = flip(after(send, *beside_qkv), "gene", 1)
    beside_sum = begin(1, 3, send, *beside_qkv)
    prepare(2, send)
    w_first_t = jnp.swapaxes(after(w_first, send), 1, 2)
    mine, other = add_call(me, keep, after(came, sends[2][0], w_first_t))
    last = flip(other, "gene", 2)
    queries, key_value = split_call(me, mine, after(last, beside_sum))
    across = flip(key_value, "cell", 2)
    beside = flip(key_value, "cell", 1)
    corner = flip(across, "cell", 1)
    beside_keys = [begin(1, 2, last), begin(1, 1, last)]
    attended = attend_call(me, queries, (key_value, beside, across, corner))
    attended = after(attended, *beside_keys)
    near = flip(attended, "gene", 1)
    far = flip(attended, "gene", 2)
    rest = flip(after(far, near), "gene", 1)
    rest = after(rest, begin(2, 2, attended))
    hidden, first = first_call(
        me, matrix, (attended, near, far, rest), w_out, masked, w_first_t, chunks
    )
    begin(2, 3, rest)
    begin(2, 1, rest)

    got = []

    def launch(t, *earlier):
        pieces = after(first[t], *earlier)
        if chunks[t][1]:
            got.append([lax.all_to_all(pieces[0], "gene", split_axis=0, concat_axis=0, tiled=True)])
        else:
            got.append([pieces[0]] + [flip(pieces[bits], "gene", bits) for bits in (1, 2, 3)])

    launch(0, back[2][3], back[2][1])
    denoised, shares = None, [None, None]
    back = sum(back, [])

    def sum_cells(which, start, send, keep):
        came = [flip(piece, "cell", 1) for piece in send]
        mine, other = pair_call(me, keep, came)
        last = flip(other, "cell", 2)
        shares[which] = finish_call(me, mine, last, shares[which], start, blocks)

    *send, keep = grad_first_call(me, back, hidden, size, 0, blocks // 2)
    *send_next, keep_next = grad_first_call(me, back, hidden, size, blocks // 2, blocks // 2)
    sum_cells(0, 0, send, keep)
    sum_cells(0, blocks // 2, send_next, keep_next)
    pin = shares[0]
    for t in range(len(chunks)):
        start = sum(count for count, _ in chunks[:t]) * blocks // deep
        if t + 1 < len(chunks):
            launch(t + 1, *got[t], pin)
        denoised, *send, keep = second_call(
            me, got[t], w_second, cotangent, hidden, denoised, start
        )
        sum_cells(1, start, send, keep)
        pin = shares[1]
    return (denoised, *shares)


def solution(mesh):
    placed = (
        P(("grp", "cell"), "gene"),
        P(("grp", "cell"), "gene"),
        P("gene"),
        P("gene", None),
        P(None, "gene"),
        P("gene", None, None),
        P("gene", None, None),
        P(("grp", "cell"), "gene"),
    )
    four = mesh.shape["gene"] == 4 and mesh.shape["cell"] == 4
    return jax.shard_map(
        on_device_four if four else on_device_general,
        mesh=mesh,
        in_specs=placed,
        out_specs=(
            P(("grp", "cell"), "gene"),
            P(("grp", "gene"), "cell", None),
            P(("grp", "gene"), "cell", None),
        ),
        check_vma=False,
    )
```

```python
import math

import jax
import jax.numpy as jnp
from jax import lax
from jax.experimental import pallas as pl
from jax.experimental.pallas import tpu as pltpu
from jax.sharding import PartitionSpec as P

HEADS = 16
HEAD_DIM = 64
TILE = 16
BF16 = jnp.bfloat16
F32 = jnp.float32


def normalize(part):
    count, columns = part.shape
    shaped = part.reshape(count, columns // HEAD_DIM, HEAD_DIM)
    meansq = jnp.mean(shaped * shaped, axis=-1, keepdims=True)
    return (shaped * lax.rsqrt(meansq + 1e-06)).astype(BF16).reshape(count, columns)


def attend(queries, key_piece, value_piece):
    query_count, columns = queries.shape
    key_count = key_piece.shape[0]
    heads = columns // HEAD_DIM
    query_heads = queries.reshape(query_count, heads, HEAD_DIM)
    key_heads = key_piece.reshape(key_count, heads, HEAD_DIM)
    value_heads = value_piece.reshape(key_count, heads, HEAD_DIM)
    scores = jnp.einsum(
        "qhd,khd->hqk", query_heads, key_heads, preferred_element_type=F32
    ) * HEAD_DIM ** (-0.5)
    expw = jnp.exp(scores).astype(BF16)
    denom = jnp.sum(expw, axis=2, dtype=F32)
    numer = jnp.einsum("hqk,khd->qhd", expw, value_heads, preferred_element_type=F32)
    return (numer / denom.T[:, :, None]).astype(BF16).reshape(query_count, columns)


def on_device_general(
    expression, gene_mask, mask_value, w_qkv, w_out, w_first, w_second, cotangent
):
    groups = lax.axis_size("gene")
    local_blocks = w_first.shape[0]
    block_size = w_first.shape[1]
    block_total = local_blocks * groups
    cell_rows = expression.shape[0]
    masked_in = jnp.where(gene_mask == 1, mask_value[None, :], expression)
    qkv_part = jnp.dot(masked_in, w_qkv, preferred_element_type=F32)
    qkv_full = lax.psum(qkv_part.astype(BF16), "gene").astype(F32)
    columns = qkv_full.shape[1] // 3
    queries = normalize(qkv_full[:, :columns])
    keys_normed = normalize(qkv_full[:, columns : 2 * columns])
    values_b = qkv_full[:, 2 * columns :].astype(BF16)
    attended = attend(
        queries,
        lax.all_gather(keys_normed, "cell", axis=0, tiled=True),
        lax.all_gather(values_b, "cell", axis=0, tiled=True),
    )
    added = jnp.dot(attended, w_out, preferred_element_type=F32)
    hidden = (masked_in.astype(F32) + added).astype(BF16)
    blocks = hidden.reshape(cell_rows, local_blocks, block_size)
    first = jnp.einsum("cbi,bio->cbo", blocks, w_first, preferred_element_type=F32).astype(BF16)
    cot_blocks = cotangent.reshape(cell_rows, local_blocks, block_size)
    back_perm = jnp.einsum(
        "cjo,jko->cjk", cot_blocks, w_second, preferred_element_type=F32
    ).astype(BF16)
    back_send = back_perm.reshape(cell_rows, block_size // groups, block_total)
    received = lax.all_to_all(first, "gene", split_axis=2, concat_axis=1, tiled=True)
    permuted = jnp.swapaxes(received, 1, 2).reshape(cell_rows, local_blocks, block_size)
    mixed = jnp.einsum("cjk,jko->cjo", permuted, w_second, preferred_element_type=F32)
    denoised = (
        (blocks.astype(F32) + mixed).astype(BF16).reshape(cell_rows, local_blocks * block_size)
    )
    grad_second = jnp.einsum("cjk,cjo->jko", permuted, cot_blocks, preferred_element_type=F32)
    back_recv = lax.all_to_all(back_send, "gene", split_axis=2, concat_axis=1, tiled=True)
    back_first = jnp.swapaxes(back_recv, 1, 2)
    grad_first = jnp.einsum("cbi,cbo->bio", blocks, back_first, preferred_element_type=F32)
    first_share, second_share = (
        lax.psum_scatter(
            grad_first.astype(BF16), "cell", scatter_dimension=1, tiled=True
        ).astype(F32),
        lax.psum_scatter(
            grad_second.astype(BF16), "cell", scatter_dimension=1, tiled=True
        ).astype(F32),
    )
    return (denoised, first_share, second_share)


def after(value, *earlier):
    return lax.optimization_barrier((value, *earlier))[0]


def flip(value, axis, bit):
    pairs = [(i, i ^ bit) for i in range(lax.axis_size(axis))]
    return lax.ppermute(value, axis, pairs)


def call(body, me, args, in_specs, outs, out_specs, grid=(1,), scratch=(), aliases=None):
    return pl.pallas_call(
        body,
        out_shape=outs,
        grid_spec=pltpu.PrefetchScalarGridSpec(
            num_scalar_prefetch=1,
            grid=grid,
            in_specs=in_specs,
            out_specs=out_specs,
            scratch_shapes=list(scratch),
        ),
        input_output_aliases=aliases or {},
        compiler_params=pltpu.CompilerParams(vmem_limit_bytes=52 * 2**20),
        cost_estimate=pl.CostEstimate(flops=1, bytes_accessed=1, transcendentals=0),
    )(me, *args)


def spec(shape, place):
    return pl.BlockSpec(shape, place)


def whole(shape):
    return pl.BlockSpec(shape, lambda *_: (0,) * len(shape))


def several(count):
    return next(group for group in (4, 2, 1) if count % group == 0)


def array(shape, dtype):
    return jax.ShapeDtypeStruct(shape, dtype)


def grid_turn():
    rows = lax.broadcasted_iota(jnp.int32, (TILE * TILE, TILE * TILE), 0)
    columns = lax.broadcasted_iota(jnp.int32, (TILE * TILE, TILE * TILE), 1)
    return ((rows % TILE) * TILE + rows // TILE == columns).astype(BF16)


def turn(matrix, tile):
    rows = tile.shape[-1]
    flat = tile.reshape(TILE * TILE, rows)
    return jnp.dot(matrix, flat, preferred_element_type=F32).astype(BF16).reshape(TILE, TILE, rows)


def back_kernel(me_ref, turn_ref, second_ref, cot_ref, *refs):
    outs, held = refs[:4], refs[4]
    blocks, rows = held.shape[2], held.shape[3]
    group, size, _ = second_ref.shape
    pair = size // (4 * blocks)
    steps = TILE // (pair * group)
    at = pl.program_id(0) % steps
    for g in range(group):
        back = lax.dot_general(
            second_ref[g],
            cot_ref[:, g * size : (g + 1) * size],
            (((1,), (1,)), ((), ())),
            preferred_element_type=F32,
        ).astype(BF16)
        held[pl.ds((at * group + g) * pair, pair)] = back.reshape(pair, 4, blocks, rows)

    @pl.when(at == steps - 1)
    def _():
        for bits in range(4):
            there = me_ref[0] ^ bits
            for low in range(0, blocks, TILE):
                outs[bits][low : low + TILE] = turn(
                    turn_ref[...], held[:, there, low : low + TILE, :]
                )


def back_call(me, matrix, w_second, cotangent, start, count):
    blocks, size, _ = w_second.shape
    rows = cotangent.shape[0]
    pair = size // (4 * blocks)
    group = several(math.gcd(count, TILE // pair))
    steps = TILE // (pair * group)
    first = start // group
    piece = array((blocks, count * pair, rows), BF16)
    return call(
        back_kernel,
        me,
        (matrix, w_second, cotangent),
        [
            whole(matrix.shape),
            spec((group, size, size), lambda j, _: (first + j, 0, 0)),
            spec((rows, group * size), lambda j, _: (0, first + j)),
        ],
        [piece] * 4,
        [spec((blocks, TILE, rows), lambda j, _: (0, j // steps, 0))] * 4,
        grid=(count // group,),
        scratch=[pltpu.VMEM((TILE, 4, blocks, rows), BF16)],
    )


def project_kernel(me_ref, value_ref, mask_ref, fill_ref, weight_ref, *refs):
    masked_ref, send_ref, keep_ref, total = refs
    step = pl.program_id(0)
    masked = jnp.where(
        mask_ref[...] == 1, fill_ref[...].astype(F32), value_ref[...].astype(F32)
    ).astype(BF16)
    masked_ref[...] = masked
    width = total.shape[1] // 3

    @pl.when(step == 0)
    def _():
        total[...] = jnp.dot(masked, weight_ref[...], preferred_element_type=F32)

    @pl.when(step > 0)
    def _():
        total[...] += jnp.dot(masked, weight_ref[...], preferred_element_type=F32)

    @pl.when(step == pl.num_programs(0) - 1)
    def _():
        share = width // 4
        for out, flips in ((send_ref, (1, 3)), (keep_ref, (0, 2))):
            for slot, bits in enumerate(flips):
                for kind in range(3):
                    place = pl.multiple_of(kind * width + (me_ref[0] ^ bits) * share, share)
                    out[slot, :, kind * share : (kind + 1) * share] = total[
                        :, pl.ds(place, share)
                    ].astype(out.dtype)


def project_call(me, expression, gene_mask, mask_value, w_qkv):
    rows, genes = expression.shape
    width = w_qkv.shape[1]
    depth = min(genes, 1024)
    wide = spec((rows, depth), lambda i, _: (0, i))
    shape = (2, rows, width // 4)
    return call(
        project_kernel,
        me,
        (expression, gene_mask, mask_value.reshape(1, genes), w_qkv),
        [
            wide,
            wide,
            spec((1, depth), lambda i, _: (0, i)),
            spec((depth, width), lambda i, _: (i, 0)),
        ],
        [array((rows, genes), BF16), array(shape, BF16), array(shape, F32)],
        [wide, whole(shape), whole(shape)],
        grid=(genes // depth,),
        scratch=[pltpu.VMEM((rows, width), F32)],
    )


def store_quarters(me, at, held, send_ref, keep_ref):
    quarter = held.shape[0] // 4
    for bits in range(4):
        start = pl.multiple_of((me ^ bits) * quarter, quarter)
        part = held[pl.ds(start, quarter), :]
        if bits % 2:
            send_ref[bits // 2][at] = part.astype(BF16)
        else:
            keep_ref[bits // 2, at] = part


def quarter_outs(count, group, size):
    shape = (count, size // 4, size)
    one = spec((group, *shape[1:]), lambda j, _: (j, 0, 0))
    two = spec((2, group, *shape[1:]), lambda j, _: (0, j, 0, 0))
    return [array(shape, BF16)] * 2 + [array((2, *shape), F32)], [one, one, two]


def add_kernel(_, keep_ref, came_ref, mine_ref, other_ref):
    mine_ref[...] = keep_ref[0] + came_ref[0].astype(F32)
    other_ref[...] = (keep_ref[1] + came_ref[1].astype(F32)).astype(BF16)


def add_call(me, keep, came):
    shape = keep.shape
    return call(
        add_kernel,
        me,
        (keep, came),
        [whole(shape), whole(shape)],
        [array(shape[1:], F32), array(shape[1:], BF16)],
        [whole(shape[1:])] * 2,
    )


def normalize_heads(part):
    columns = part.shape[1]
    heads = [lax.broadcasted_iota(jnp.int32, (columns, columns), d) // HEAD_DIM for d in (0, 1)]
    same = (heads[0] == heads[1]).astype(F32)
    sums = jnp.dot(
        part * part, same, precision=lax.Precision.HIGHEST, preferred_element_type=F32
    )
    return (part * lax.rsqrt(sums * (1.0 / HEAD_DIM) + 1e-06)).astype(BF16)


def pair_kernel(_, keep_ref, came_ref, next_ref, mine_ref, other_ref):
    mine_ref[...] = keep_ref[0] + came_ref[...].astype(F32)
    other_ref[...] = (keep_ref[1] + next_ref[...].astype(F32)).astype(BF16)


def pair_call(me, keep, came):
    shape = keep.shape[1:]
    return call(
        pair_kernel,
        me,
        (keep, *came),
        [whole(keep.shape), whole(shape), whole(shape)],
        [array(shape, F32), array(shape, BF16)],
        [whole(shape)] * 2,
    )


def finish_kernel(_, mine_ref, came_ref, *refs):
    refs[-1][...] = mine_ref[...] + came_ref[...].astype(F32)


def finish_call(me, mine, came, total, start, blocks):
    count, quarter, size = mine.shape
    step = math.gcd(count, start) if start else count
    args = [mine, came]
    in_specs = [spec((step, quarter, size), lambda i, _: (i, 0, 0))] * 2
    aliases = {}
    if total is not None:
        args.append(total)
        in_specs.append(pl.BlockSpec(memory_space=pl.ANY))
        aliases = {len(args): 0}
    return call(
        finish_kernel,
        me,
        args,
        in_specs,
        array((blocks, quarter, size), F32),
        spec((step, quarter, size), lambda i, _: (start // step + i, 0, 0)),
        grid=(count // step,),
        aliases=aliases,
    )


def split_kernel(_, mine_ref, came_ref, query_ref, key_ref, value_ref):
    total = mine_ref[...] + came_ref[...].astype(F32)
    share = total.shape[1] // 3
    query_ref[...] = normalize_heads(total[:, :share])
    key_ref[...] = normalize_heads(total[:, share : 2 * share])
    value_ref[...] = total[:, 2 * share :].astype(BF16)


def split_call(me, mine, came):
    rows, columns = mine.shape
    shapes = ((rows, columns // 3),) * 3
    return call(
        split_kernel,
        me,
        (mine, came),
        [whole(mine.shape)] * 2,
        [array(shape, BF16) for shape in shapes],
        [whole(shape) for shape in shapes],
    )


def attend_kernel(_, query_ref, *refs):
    count = len(refs) // 2
    keys, values, out_ref = refs[:count], refs[count:-1], refs[-1]
    queries = query_ref[...]
    rows, share = queries.shape
    head_of = lax.broadcasted_iota(jnp.int32, (rows, share), 1) // HEAD_DIM
    out = jnp.zeros((rows, share), F32)
    for head in range(share // HEAD_DIM):
        query = jnp.where(head_of == head, queries.astype(F32) * HEAD_DIM**-0.5, 0.0).astype(BF16)
        numer = jnp.zeros((rows, share), F32)
        denom = jnp.zeros((rows, 1), F32)
        for key, value in zip(keys, values):
            scores = lax.dot_general(
                query, key[...], (((1,), (1,)), ((), ())), preferred_element_type=F32
            )
            expw = jnp.exp(scores).astype(BF16)
            denom += jnp.sum(expw.astype(F32), axis=1, keepdims=True)
            numer += jnp.dot(expw, value[...], preferred_element_type=F32)
        out = jnp.where(head_of == head, numer / denom, out)
    out_ref[...] = out.astype(BF16)


def attend_call(me, queries, pieces):
    rows, share = queries.shape
    some = rows // 2
    part = spec((some, share), lambda i, _: (i, 0))
    return call(
        attend_kernel,
        me,
        (queries, *pieces),
        [part] + [whole(piece.shape) for piece in pieces],
        array((rows, share), BF16),
        part,
        grid=(2,),
    )


def first_kernel(me_ref, turn_ref, own, near, far, rest, w_out_ref, masked_ref, wf_ref, *refs):
    hidden_ref, outs, gathered, held = refs[0], refs[1:-2], refs[-2], refs[-1]
    step = pl.program_id(0)
    share = own.shape[1]
    group, size, _ = wf_ref.shape
    steps = TILE // group

    @pl.when(step == 0)
    def _():
        for bits, piece in enumerate((own, near, far, rest)):
            place = pl.multiple_of((me_ref[0] ^ bits) * share, share)
            gathered[:, pl.ds(place, share)] = piece[...]

    added = jnp.dot(gathered[...], w_out_ref[...], preferred_element_type=F32)
    hidden = (masked_ref[...].astype(F32) + added).astype(BF16)
    hidden_ref[...] = hidden
    for g in range(group):
        held[step % steps * group + g] = lax.dot_general(
            wf_ref[g],
            hidden[:, g * size : (g + 1) * size],
            (((1,), (1,)), ((), ())),
            preferred_element_type=F32,
        ).astype(BF16)

    @pl.when(step % steps == steps - 1)
    def _():
        chunks = []
        rest = list(outs)
        while rest:
            swapped = len(rest[0].shape) == 4
            refs = rest[: 1 if swapped else 4]
            rest = rest[len(refs) :]
            chunks.append((refs, refs[0].shape[1 if swapped else 0]))
        deep = sum(count for _, count in chunks)
        for bits in range(4):
            there = me_ref[0] ^ bits
            for low in range(0, deep, TILE):
                start = pl.multiple_of(there * deep + low, TILE)
                tile = turn(turn_ref[...], held[:, pl.ds(start, TILE), :])
                begin = 0
                for refs, count in chunks:
                    least, most = max(begin, low), min(begin + count, low + TILE)
                    if least < most:
                        target = refs[0].at[there] if len(refs) == 1 else refs[bits]
                        target[least - begin : most - begin] = tile[least - low : most - low]
                    begin += count


def first_call(me, matrix, attended, w_out, masked, w_first_t, chunks):
    blocks, size, _ = w_first_t.shape
    rows, genes = masked.shape
    width = w_out.shape[0]
    group = several(TILE)
    steps = TILE // group
    wide = spec((rows, group * size), lambda b, _: (0, b))
    outs, places = [array((rows, genes), BF16)], [wide]
    for deep, swapped in chunks:
        if swapped:
            outs.append(array((4, deep, blocks, rows), BF16))
            places.append(spec((4, deep, TILE, rows), lambda b, _: (0, 0, b // steps, 0)))
        else:
            outs += [array((deep, blocks, rows), BF16)] * 4
            places += [spec((deep, TILE, rows), lambda b, _: (0, b // steps, 0))] * 4
    hidden, *first = call(
        first_kernel,
        me,
        (matrix, *attended, w_out, masked, w_first_t),
        [whole(matrix.shape)]
        + [whole(part.shape) for part in attended]
        + [
            spec((width, group * size), lambda b, _: (0, b)),
            wide,
            spec((group, size, size), lambda b, _: (b, 0, 0)),
        ],
        outs,
        places,
        grid=(blocks // group,),
        scratch=[pltpu.VMEM((rows, width), BF16), pltpu.VMEM((TILE, size, rows), BF16)],
    )
    taken = []
    for _, swapped in chunks:
        wanted = 1 if swapped else 4
        taken.append(first[:wanted])
        first = first[wanted:]
    return hidden, taken


def second_kernel(me_ref, *refs):
    pieces = refs[: 1 if len(refs[0].shape) == 4 else 4]
    w_ref, cot_ref, hidden_ref = refs[len(pieces) : len(pieces) + 3]
    out_ref, *send_ref, keep_ref, square, held = refs[-6:]
    group, size, _ = w_ref.shape
    pair = held.shape[1]
    for g in range(group):
        at = slice(g * size, (g + 1) * size)
        mine = slice(g * pair, (g + 1) * pair)
        if len(pieces) == 1:
            for source in range(4):
                held[g, :, source] = pieces[0][source, mine]
        else:
            for bits in range(4):
                held[g, :, me_ref[0] ^ bits] = pieces[bits][mine]
        permuted = held[g].reshape(size, held.shape[4])
        square[g] = jnp.dot(permuted, cot_ref[:, at], preferred_element_type=F32)
        store_quarters(me_ref[1], g, square.at[g], send_ref, keep_ref)
        mixed = lax.dot_general(
            permuted, w_ref[g], (((0,), (0,)), ((), ())), preferred_element_type=F32
        )
        out_ref[:, at] = (hidden_ref[:, at].astype(F32) + mixed).astype(BF16)


def second_call(me, pieces, w_second, cotangent, hidden, denoised, start):
    blocks, size, _ = w_second.shape
    deep, _, rows = pieces[0].shape[-3:]
    pair = size // (4 * blocks)
    count = deep // pair
    group = several(math.gcd(count, start) if start else count)
    begin = start // group
    wide = spec((rows, group * size), lambda j, _: (0, begin + j))
    square = spec((group, size, size), lambda j, _: (begin + j, 0, 0))
    args = [*pieces, w_second, cotangent, hidden]
    part = (group * pair, blocks, rows)
    if len(pieces) == 1:
        in_specs = [spec((4, *part), lambda j, _: (0, j, 0, 0))]
    else:
        in_specs = [spec(part, lambda j, _: (j, 0, 0))] * 4
    in_specs += [square, wide, wide]
    quarters = quarter_outs(count, group, size)
    aliases = {}
    if denoised is not None:
        args.append(denoised)
        in_specs.append(pl.BlockSpec(memory_space=pl.ANY))
        aliases = {len(args): 0}
    return call(
        second_kernel,
        me,
        args,
        in_specs,
        [array(hidden.shape, BF16), *quarters[0]],
        [wide, *quarters[1]],
        grid=(count // group,),
        scratch=[
            pltpu.VMEM((group, size, size), F32),
            pltpu.VMEM((group, pair, 4, blocks, rows), BF16),
        ],
        aliases=aliases,
    )


def grad_first_kernel(me_ref, *refs):
    pieces, (hidden_ref, *send_ref, keep_ref, held, square) = refs[:-6], refs[-6:]
    group, size, _ = square.shape
    for g in range(group):
        low = 0
        for part in range(0, len(pieces), 4):
            deep = pieces[part].shape[1]
            for bits in range(4):
                held[g, me_ref[0] ^ bits, low : low + deep] = pieces[part + bits][g]
            low += deep
        back = held[g].reshape(size, held.shape[3])
        hidden = hidden_ref[:, g * size : (g + 1) * size]
        square[g] = jnp.dot(back, hidden, preferred_element_type=F32).T
        store_quarters(me_ref[1], g, square.at[g], send_ref, keep_ref)


def grad_first_call(me, pieces, hidden, size, start, count):
    rows = hidden.shape[0]
    group = several(math.gcd(count, start) if start else count)
    begin = start // group
    return call(
        grad_first_kernel,
        me,
        (*pieces, hidden),
        [spec((group, *piece.shape[1:]), lambda b, _: (begin + b, 0, 0)) for piece in pieces]
        + [spec((rows, group * size), lambda b, _: (0, begin + b))],
        *quarter_outs(count, group, size),
        grid=(count // group,),
        scratch=[
            pltpu.VMEM((group, 4, size // 4, rows), BF16),
            pltpu.VMEM((group, size, size), F32),
        ],
    )


def on_device_four(expression, gene_mask, mask_value, w_qkv, w_out, w_first, w_second, cotangent):
    me = jnp.stack([lax.axis_index("gene"), lax.axis_index("cell")]).astype(jnp.int32)
    blocks, size, _ = w_first.shape
    deep = size // 4
    counts = [blocks // 4, blocks // 2, blocks // 4]
    chunks = [(3 * deep // 4, True), (deep // 4, True)]
    matrix = grid_turn()
    sends, back = [None] * 3, [[None] * 4 for _ in range(3)]

    def prepare(part, *earlier):
        sends[part] = back_call(
            me, matrix, w_second, after(cotangent, *earlier), sum(counts[:part]), counts[part]
        )
        back[part][0] = sends[part][0]

    def begin(part, bits, *earlier):
        back[part][bits] = flip(after(sends[part][bits], *earlier), "gene", bits)
        return back[part][bits]

    prepare(0)
    beside_qkv = [begin(0, bits) for bits in (3, 2, 1)]
    prepare(1, sends[0][0])
    masked, send, keep = project_call(
        me, after(expression, sends[1][0]), gene_mask, mask_value, w_qkv
    )
    came = flip(after(send, *beside_qkv), "gene", 1)
    beside_sum = begin(1, 3, send, *beside_qkv)
    prepare(2, send)
    w_first_t = jnp.swapaxes(after(w_first, send), 1, 2)
    mine, other = add_call(me, keep, after(came, sends[2][0], w_first_t))
    last = flip(other, "gene", 2)
    queries, *own = split_call(me, mine, after(last, beside_sum))
    across = [flip(piece, "cell", 2) for piece in own]
    beside = [flip(piece, "cell", 1) for piece in own]
    corner = [flip(piece, "cell", 1) for piece in across]
    beside_keys = [begin(1, bits, last, beside_sum) for bits in (2, 1)]
    gathered = [piece for kind in zip(own, beside, across, corner) for piece in kind]
    attended = attend_call(me, queries, gathered)
    attended = after(attended, *beside_keys)
    near = flip(attended, "gene", 1)
    far = flip(attended, "gene", 2)
    rest = flip(after(far, near), "gene", 1)
    begin(2, 2, attended)
    hidden, first = first_call(
        me, matrix, (attended, near, far, rest), w_out, masked, w_first_t, chunks
    )
    begin(2, 3, rest)
    begin(2, 1, rest)

    got = []

    def launch(t, *earlier):
        pieces = after(first[t], *earlier)
        if chunks[t][1]:
            got.append([lax.all_to_all(pieces[0], "gene", split_axis=0, concat_axis=0, tiled=True)])
        else:
            got.append([pieces[0]] + [flip(pieces[bits], "gene", bits) for bits in (1, 2, 3)])

    launch(0, *back[2][1:])
    denoised, shares = None, [None, None]
    back = sum(back, [])

    def sum_cells(which, start, send, keep):
        came = [flip(piece, "cell", 1) for piece in send]
        mine, other = pair_call(me, keep, came)
        last = flip(other, "cell", 2)
        shares[which] = finish_call(me, mine, last, shares[which], start, blocks)

    *send, keep = grad_first_call(me, back, hidden, size, 0, blocks // 2)
    *send_next, keep_next = grad_first_call(me, back, hidden, size, blocks // 2, blocks // 2)
    sum_cells(0, 0, send, keep)
    sum_cells(0, blocks // 2, send_next, keep_next)
    pin = shares[0]
    for t in range(len(chunks)):
        start = sum(count for count, _ in chunks[:t]) * blocks // deep
        if t + 1 < len(chunks):
            launch(t + 1, *got[t], pin)
        denoised, *send, keep = second_call(
            me, got[t], w_second, cotangent, hidden, denoised, start
        )
        sum_cells(1, start, send, keep)
        pin = shares[1]
    return (denoised, *shares)


def solution(mesh):
    placed = (
        P(("grp", "cell"), "gene"),
        P(("grp", "cell"), "gene"),
        P("gene"),
        P("gene", None),
        P(None, "gene"),
        P("gene", None, None),
        P("gene", None, None),
        P(("grp", "cell"), "gene"),
    )
    four = mesh.shape["gene"] == 4 and mesh.shape["cell"] == 4
    return jax.shard_map(
        on_device_four if four else on_device_general,
        mesh=mesh,
        in_specs=placed,
        out_specs=(
            P(("grp", "cell"), "gene"),
            P(("grp", "gene"), "cell", None),
            P(("grp", "gene"), "cell", None),
        ),
        check_vma=False,
    )
```

```python
import math

import jax
import jax.numpy as jnp
from jax import lax
from jax.experimental import pallas as pl
from jax.experimental.pallas import tpu as pltpu
from jax.sharding import PartitionSpec as P

HEADS = 16
HEAD_DIM = 64
TILE = 16
BF16 = jnp.bfloat16
F32 = jnp.float32


def normalize(part):
    count, columns = part.shape
    shaped = part.reshape(count, columns // HEAD_DIM, HEAD_DIM)
    meansq = jnp.mean(shaped * shaped, axis=-1, keepdims=True)
    return (shaped * lax.rsqrt(meansq + 1e-06)).astype(BF16).reshape(count, columns)


def attend(queries, key_piece, value_piece):
    query_count, columns = queries.shape
    key_count = key_piece.shape[0]
    heads = columns // HEAD_DIM
    query_heads = queries.reshape(query_count, heads, HEAD_DIM)
    key_heads = key_piece.reshape(key_count, heads, HEAD_DIM)
    value_heads = value_piece.reshape(key_count, heads, HEAD_DIM)
    scores = jnp.einsum(
        "qhd,khd->hqk", query_heads, key_heads, preferred_element_type=F32
    ) * HEAD_DIM ** (-0.5)
    expw = jnp.exp(scores).astype(BF16)
    denom = jnp.sum(expw, axis=2, dtype=F32)
    numer = jnp.einsum("hqk,khd->qhd", expw, value_heads, preferred_element_type=F32)
    return (numer / denom.T[:, :, None]).astype(BF16).reshape(query_count, columns)


def on_device_general(
    expression, gene_mask, mask_value, w_qkv, w_out, w_first, w_second, cotangent
):
    groups = lax.axis_size("gene")
    local_blocks = w_first.shape[0]
    block_size = w_first.shape[1]
    block_total = local_blocks * groups
    cell_rows = expression.shape[0]
    masked_in = jnp.where(gene_mask == 1, mask_value[None, :], expression)
    qkv_part = jnp.dot(masked_in, w_qkv, preferred_element_type=F32)
    qkv_full = lax.psum(qkv_part.astype(BF16), "gene").astype(F32)
    columns = qkv_full.shape[1] // 3
    queries = normalize(qkv_full[:, :columns])
    keys_normed = normalize(qkv_full[:, columns : 2 * columns])
    values_b = qkv_full[:, 2 * columns :].astype(BF16)
    attended = attend(
        queries,
        lax.all_gather(keys_normed, "cell", axis=0, tiled=True),
        lax.all_gather(values_b, "cell", axis=0, tiled=True),
    )
    added = jnp.dot(attended, w_out, preferred_element_type=F32)
    hidden = (masked_in.astype(F32) + added).astype(BF16)
    blocks = hidden.reshape(cell_rows, local_blocks, block_size)
    first = jnp.einsum("cbi,bio->cbo", blocks, w_first, preferred_element_type=F32).astype(BF16)
    cot_blocks = cotangent.reshape(cell_rows, local_blocks, block_size)
    back_perm = jnp.einsum(
        "cjo,jko->cjk", cot_blocks, w_second, preferred_element_type=F32
    ).astype(BF16)
    back_send = back_perm.reshape(cell_rows, block_size // groups, block_total)
    received = lax.all_to_all(first, "gene", split_axis=2, concat_axis=1, tiled=True)
    permuted = jnp.swapaxes(received, 1, 2).reshape(cell_rows, local_blocks, block_size)
    mixed = jnp.einsum("cjk,jko->cjo", permuted, w_second, preferred_element_type=F32)
    denoised = (
        (blocks.astype(F32) + mixed).astype(BF16).reshape(cell_rows, local_blocks * block_size)
    )
    grad_second = jnp.einsum("cjk,cjo->jko", permuted, cot_blocks, preferred_element_type=F32)
    back_recv = lax.all_to_all(back_send, "gene", split_axis=2, concat_axis=1, tiled=True)
    back_first = jnp.swapaxes(back_recv, 1, 2)
    grad_first = jnp.einsum("cbi,cbo->bio", blocks, back_first, preferred_element_type=F32)
    first_share, second_share = (
        lax.psum_scatter(
            grad_first.astype(BF16), "cell", scatter_dimension=1, tiled=True
        ).astype(F32),
        lax.psum_scatter(
            grad_second.astype(BF16), "cell", scatter_dimension=1, tiled=True
        ).astype(F32),
    )
    return (denoised, first_share, second_share)


def after(value, *earlier):
    return lax.optimization_barrier((value, *earlier))[0]


def flip(value, axis, bit):
    pairs = [(i, i ^ bit) for i in range(lax.axis_size(axis))]
    return lax.ppermute(value, axis, pairs)


def call(body, me, args, in_specs, outs, out_specs, grid=(1,), scratch=(), aliases=None):
    return pl.pallas_call(
        body,
        out_shape=outs,
        grid_spec=pltpu.PrefetchScalarGridSpec(
            num_scalar_prefetch=1,
            grid=grid,
            in_specs=in_specs,
            out_specs=out_specs,
            scratch_shapes=list(scratch),
        ),
        input_output_aliases=aliases or {},
        compiler_params=pltpu.CompilerParams(vmem_limit_bytes=52 * 2**20),
        cost_estimate=pl.CostEstimate(flops=1, bytes_accessed=1, transcendentals=0),
    )(me, *args)


def spec(shape, place):
    return pl.BlockSpec(shape, place)


def whole(shape):
    return pl.BlockSpec(shape, lambda *_: (0,) * len(shape))


def several(count):
    return next(group for group in (4, 2, 1) if count % group == 0)


def array(shape, dtype):
    return jax.ShapeDtypeStruct(shape, dtype)


def grid_turn():
    rows = lax.broadcasted_iota(jnp.int32, (TILE * TILE, TILE * TILE), 0)
    columns = lax.broadcasted_iota(jnp.int32, (TILE * TILE, TILE * TILE), 1)
    return ((rows % TILE) * TILE + rows // TILE == columns).astype(BF16)


def turn(matrix, tile):
    rows = tile.shape[-1]
    flat = tile.reshape(TILE * TILE, rows)
    return jnp.dot(matrix, flat, preferred_element_type=F32).astype(BF16).reshape(TILE, TILE, rows)


def back_kernel(me_ref, turn_ref, second_ref, cot_ref, *refs):
    outs, held = refs[:4], refs[4]
    blocks, rows = held.shape[2], held.shape[3]
    group, size, _ = second_ref.shape
    pair = size // (4 * blocks)
    steps = TILE // (pair * group)
    at = pl.program_id(0) % steps
    for g in range(group):
        back = lax.dot_general(
            second_ref[g],
            cot_ref[:, g * size : (g + 1) * size],
            (((1,), (1,)), ((), ())),
            preferred_element_type=F32,
        ).astype(BF16)
        held[pl.ds((at * group + g) * pair, pair)] = back.reshape(pair, 4, blocks, rows)

    @pl.when(at == steps - 1)
    def _():
        for bits in range(4):
            there = me_ref[0] ^ bits
            for low in range(0, blocks, TILE):
                outs[bits][low : low + TILE] = turn(
                    turn_ref[...], held[:, there, low : low + TILE, :]
                )


def back_call(me, matrix, w_second, cotangent, start, count):
    blocks, size, _ = w_second.shape
    rows = cotangent.shape[0]
    pair = size // (4 * blocks)
    group = several(math.gcd(count, TILE // pair))
    steps = TILE // (pair * group)
    first = start // group
    piece = array((blocks, count * pair, rows), BF16)
    return call(
        back_kernel,
        me,
        (matrix, w_second, cotangent),
        [
            whole(matrix.shape),
            spec((group, size, size), lambda j, _: (first + j, 0, 0)),
            spec((rows, group * size), lambda j, _: (0, first + j)),
        ],
        [piece] * 4,
        [spec((blocks, TILE, rows), lambda j, _: (0, j // steps, 0))] * 4,
        grid=(count // group,),
        scratch=[pltpu.VMEM((TILE, 4, blocks, rows), BF16)],
    )


def project_kernel(me_ref, value_ref, mask_ref, fill_ref, weight_ref, *refs):
    masked_ref, send_ref, keep_ref, total = refs
    step = pl.program_id(0)
    masked = jnp.where(
        mask_ref[...] == 1, fill_ref[...].astype(F32), value_ref[...].astype(F32)
    ).astype(BF16)
    masked_ref[...] = masked
    width = total.shape[1] // 3

    @pl.when(step == 0)
    def _():
        total[...] = jnp.dot(masked, weight_ref[...], preferred_element_type=F32)

    @pl.when(step > 0)
    def _():
        total[...] += jnp.dot(masked, weight_ref[...], preferred_element_type=F32)

    @pl.when(step == pl.num_programs(0) - 1)
    def _():
        share = width // 4
        for out, flips in ((send_ref, (1, 3)), (keep_ref, (0, 2))):
            for slot, bits in enumerate(flips):
                for kind in range(3):
                    place = pl.multiple_of(kind * width + (me_ref[0] ^ bits) * share, share)
                    out[slot, :, kind * share : (kind + 1) * share] = total[
                        :, pl.ds(place, share)
                    ].astype(out.dtype)


def project_call(me, expression, gene_mask, mask_value, w_qkv):
    rows, genes = expression.shape
    width = w_qkv.shape[1]
    depth = min(genes, 1024)
    wide = spec((rows, depth), lambda i, _: (0, i))
    shape = (2, rows, width // 4)
    return call(
        project_kernel,
        me,
        (expression, gene_mask, mask_value.reshape(1, genes), w_qkv),
        [
            wide,
            wide,
            spec((1, depth), lambda i, _: (0, i)),
            spec((depth, width), lambda i, _: (i, 0)),
        ],
        [array((rows, genes), BF16), array(shape, BF16), array(shape, F32)],
        [wide, whole(shape), whole(shape)],
        grid=(genes // depth,),
        scratch=[pltpu.VMEM((rows, width), F32)],
    )


def store_quarters(me, at, held, send_ref, keep_ref):
    quarter = held.shape[0] // 4
    for bits in range(4):
        start = pl.multiple_of((me ^ bits) * quarter, quarter)
        part = held[pl.ds(start, quarter), :]
        if bits % 2:
            send_ref[bits // 2][at] = part.astype(BF16)
        else:
            keep_ref[bits // 2, at] = part


def quarter_outs(count, group, size):
    shape = (count, size // 4, size)
    one = spec((group, *shape[1:]), lambda j, _: (j, 0, 0))
    two = spec((2, group, *shape[1:]), lambda j, _: (0, j, 0, 0))
    return [array(shape, BF16)] * 2 + [array((2, *shape), F32)], [one, one, two]


def add_kernel(_, keep_ref, came_ref, mine_ref, other_ref):
    mine_ref[...] = keep_ref[0] + came_ref[0].astype(F32)
    other_ref[...] = (keep_ref[1] + came_ref[1].astype(F32)).astype(BF16)


def add_call(me, keep, came):
    shape = keep.shape
    return call(
        add_kernel,
        me,
        (keep, came),
        [whole(shape), whole(shape)],
        [array(shape[1:], F32), array(shape[1:], BF16)],
        [whole(shape[1:])] * 2,
    )


def normalize_heads(part):
    columns = part.shape[1]
    heads = [lax.broadcasted_iota(jnp.int32, (columns, columns), d) // HEAD_DIM for d in (0, 1)]
    same = (heads[0] == heads[1]).astype(F32)
    sums = jnp.dot(
        part * part, same, precision=lax.Precision.HIGHEST, preferred_element_type=F32
    )
    return (part * lax.rsqrt(sums * (1.0 / HEAD_DIM) + 1e-06)).astype(BF16)


def pair_kernel(_, keep_ref, came_ref, next_ref, mine_ref, other_ref):
    mine_ref[...] = keep_ref[0] + came_ref[...].astype(F32)
    other_ref[...] = (keep_ref[1] + next_ref[...].astype(F32)).astype(BF16)


def pair_call(me, keep, came):
    shape = keep.shape[1:]
    return call(
        pair_kernel,
        me,
        (keep, *came),
        [whole(keep.shape), whole(shape), whole(shape)],
        [array(shape, F32), array(shape, BF16)],
        [whole(shape)] * 2,
    )


def finish_kernel(_, mine_ref, came_ref, *refs):
    refs[-1][...] = mine_ref[...] + came_ref[...].astype(F32)


def finish_call(me, mine, came, total, start, blocks):
    count, quarter, size = mine.shape
    step = math.gcd(count, start) if start else count
    args = [mine, came]
    in_specs = [spec((step, quarter, size), lambda i, _: (i, 0, 0))] * 2
    aliases = {}
    if total is not None:
        args.append(total)
        in_specs.append(pl.BlockSpec(memory_space=pl.ANY))
        aliases = {len(args): 0}
    return call(
        finish_kernel,
        me,
        args,
        in_specs,
        array((blocks, quarter, size), F32),
        spec((step, quarter, size), lambda i, _: (start // step + i, 0, 0)),
        grid=(count // step,),
        aliases=aliases,
    )


def split_kernel(_, mine_ref, came_ref, query_ref, key_ref, value_ref):
    total = mine_ref[...] + came_ref[...].astype(F32)
    share = total.shape[1] // 3
    query_ref[...] = normalize_heads(total[:, :share])
    key_ref[...] = normalize_heads(total[:, share : 2 * share])
    value_ref[...] = total[:, 2 * share :].astype(BF16)


def split_call(me, mine, came):
    rows, columns = mine.shape
    shapes = ((rows, columns // 3),) * 3
    return call(
        split_kernel,
        me,
        (mine, came),
        [whole(mine.shape)] * 2,
        [array(shape, BF16) for shape in shapes],
        [whole(shape) for shape in shapes],
    )


def attend_kernel(_, query_ref, *refs):
    count = len(refs) // 2
    keys, values, out_ref = refs[:count], refs[count:-1], refs[-1]
    queries = query_ref[...]
    rows, share = queries.shape
    head_of = lax.broadcasted_iota(jnp.int32, (rows, share), 1) // HEAD_DIM
    out = jnp.zeros((rows, share), F32)
    for head in range(share // HEAD_DIM):
        query = jnp.where(head_of == head, queries.astype(F32) * HEAD_DIM**-0.5, 0.0).astype(BF16)
        numer = jnp.zeros((rows, share), F32)
        denom = jnp.zeros((rows, 1), F32)
        for key, value in zip(keys, values):
            scores = lax.dot_general(
                query, key[...], (((1,), (1,)), ((), ())), preferred_element_type=F32
            )
            expw = jnp.exp(scores).astype(BF16)
            denom += jnp.sum(expw.astype(F32), axis=1, keepdims=True)
            numer += jnp.dot(expw, value[...], preferred_element_type=F32)
        out = jnp.where(head_of == head, numer / denom, out)
    out_ref[...] = out.astype(BF16)


def attend_call(me, queries, pieces):
    rows, share = queries.shape
    some = rows // 2
    part = spec((some, share), lambda i, _: (i, 0))
    return call(
        attend_kernel,
        me,
        (queries, *pieces),
        [part] + [whole(piece.shape) for piece in pieces],
        array((rows, share), BF16),
        part,
        grid=(2,),
    )


def first_kernel(me_ref, turn_ref, own, near, far, rest, w_out_ref, masked_ref, wf_ref, *refs):
    hidden_ref, outs, gathered, held = refs[0], refs[1:-2], refs[-2], refs[-1]
    step = pl.program_id(0)
    share = own.shape[1]
    group, size, _ = wf_ref.shape
    steps = TILE // group

    @pl.when(step == 0)
    def _():
        for bits, piece in enumerate((own, near, far, rest)):
            place = pl.multiple_of((me_ref[0] ^ bits) * share, share)
            gathered[:, pl.ds(place, share)] = piece[...]

    added = jnp.dot(gathered[...], w_out_ref[...], preferred_element_type=F32)
    hidden = (masked_ref[...].astype(F32) + added).astype(BF16)
    hidden_ref[...] = hidden
    for g in range(group):
        held[step % steps * group + g] = lax.dot_general(
            wf_ref[g],
            hidden[:, g * size : (g + 1) * size],
            (((1,), (1,)), ((), ())),
            preferred_element_type=F32,
        ).astype(BF16)

    @pl.when(step % steps == steps - 1)
    def _():
        chunks = []
        rest = list(outs)
        while rest:
            swapped = len(rest[0].shape) == 4
            refs = rest[: 1 if swapped else 4]
            rest = rest[len(refs) :]
            chunks.append((refs, refs[0].shape[1 if swapped else 0]))
        deep = sum(count for _, count in chunks)
        for bits in range(4):
            there = me_ref[0] ^ bits
            for low in range(0, deep, TILE):
                start = pl.multiple_of(there * deep + low, TILE)
                tile = turn(turn_ref[...], held[:, pl.ds(start, TILE), :])
                begin = 0
                for refs, count in chunks:
                    least, most = max(begin, low), min(begin + count, low + TILE)
                    if least < most:
                        target = refs[0].at[there] if len(refs) == 1 else refs[bits]
                        target[least - begin : most - begin] = tile[least - low : most - low]
                    begin += count


def first_call(me, matrix, attended, w_out, masked, w_first_t, chunks):
    blocks, size, _ = w_first_t.shape
    rows, genes = masked.shape
    width = w_out.shape[0]
    group = several(TILE)
    steps = TILE // group
    wide = spec((rows, group * size), lambda b, _: (0, b))
    outs, places = [array((rows, genes), BF16)], [wide]
    for deep, swapped in chunks:
        if swapped:
            outs.append(array((4, deep, blocks, rows), BF16))
            places.append(spec((4, deep, TILE, rows), lambda b, _: (0, 0, b // steps, 0)))
        else:
            outs += [array((deep, blocks, rows), BF16)] * 4
            places += [spec((deep, TILE, rows), lambda b, _: (0, b // steps, 0))] * 4
    hidden, *first = call(
        first_kernel,
        me,
        (matrix, *attended, w_out, masked, w_first_t),
        [whole(matrix.shape)]
        + [whole(part.shape) for part in attended]
        + [
            spec((width, group * size), lambda b, _: (0, b)),
            wide,
            spec((group, size, size), lambda b, _: (b, 0, 0)),
        ],
        outs,
        places,
        grid=(blocks // group,),
        scratch=[pltpu.VMEM((rows, width), BF16), pltpu.VMEM((TILE, size, rows), BF16)],
    )
    taken = []
    for _, swapped in chunks:
        wanted = 1 if swapped else 4
        taken.append(first[:wanted])
        first = first[wanted:]
    return hidden, taken


def second_kernel(me_ref, *refs):
    pieces = refs[: 1 if len(refs[0].shape) == 4 else 4]
    w_ref, cot_ref, hidden_ref = refs[len(pieces) : len(pieces) + 3]
    out_ref, *send_ref, keep_ref, square, held = refs[-6:]
    group, size, _ = w_ref.shape
    pair = held.shape[1]
    for g in range(group):
        at = slice(g * size, (g + 1) * size)
        mine = slice(g * pair, (g + 1) * pair)
        if len(pieces) == 1:
            for source in range(4):
                held[g, :, source] = pieces[0][source, mine]
        else:
            for bits in range(4):
                held[g, :, me_ref[0] ^ bits] = pieces[bits][mine]
        permuted = held[g].reshape(size, held.shape[4])
        square[g] = jnp.dot(permuted, cot_ref[:, at], preferred_element_type=F32)
        store_quarters(me_ref[1], g, square.at[g], send_ref, keep_ref)
        mixed = lax.dot_general(
            permuted, w_ref[g], (((0,), (0,)), ((), ())), preferred_element_type=F32
        )
        out_ref[:, at] = (hidden_ref[:, at].astype(F32) + mixed).astype(BF16)


def second_call(me, pieces, w_second, cotangent, hidden, denoised, start):
    blocks, size, _ = w_second.shape
    deep, _, rows = pieces[0].shape[-3:]
    pair = size // (4 * blocks)
    count = deep // pair
    group = several(math.gcd(count, start) if start else count)
    begin = start // group
    wide = spec((rows, group * size), lambda j, _: (0, begin + j))
    square = spec((group, size, size), lambda j, _: (begin + j, 0, 0))
    args = [*pieces, w_second, cotangent, hidden]
    part = (group * pair, blocks, rows)
    if len(pieces) == 1:
        in_specs = [spec((4, *part), lambda j, _: (0, j, 0, 0))]
    else:
        in_specs = [spec(part, lambda j, _: (j, 0, 0))] * 4
    in_specs += [square, wide, wide]
    quarters = quarter_outs(count, group, size)
    aliases = {}
    if denoised is not None:
        args.append(denoised)
        in_specs.append(pl.BlockSpec(memory_space=pl.ANY))
        aliases = {len(args): 0}
    return call(
        second_kernel,
        me,
        args,
        in_specs,
        [array(hidden.shape, BF16), *quarters[0]],
        [wide, *quarters[1]],
        grid=(count // group,),
        scratch=[
            pltpu.VMEM((group, size, size), F32),
            pltpu.VMEM((group, pair, 4, blocks, rows), BF16),
        ],
        aliases=aliases,
    )


def grad_first_kernel(me_ref, *refs):
    pieces, (hidden_ref, *send_ref, keep_ref, held, square) = refs[:-6], refs[-6:]
    group, size, _ = square.shape
    for g in range(group):
        low = 0
        for part in range(0, len(pieces), 4):
            deep = pieces[part].shape[1]
            for bits in range(4):
                held[g, me_ref[0] ^ bits, low : low + deep] = pieces[part + bits][g]
            low += deep
        back = held[g].reshape(size, held.shape[3])
        hidden = hidden_ref[:, g * size : (g + 1) * size]
        square[g] = jnp.dot(back, hidden, preferred_element_type=F32).T
        store_quarters(me_ref[1], g, square.at[g], send_ref, keep_ref)


def grad_first_call(me, pieces, hidden, size, start, count):
    rows = hidden.shape[0]
    group = several(math.gcd(count, start) if start else count)
    begin = start // group
    return call(
        grad_first_kernel,
        me,
        (*pieces, hidden),
        [spec((group, *piece.shape[1:]), lambda b, _: (begin + b, 0, 0)) for piece in pieces]
        + [spec((rows, group * size), lambda b, _: (0, begin + b))],
        *quarter_outs(count, group, size),
        grid=(count // group,),
        scratch=[
            pltpu.VMEM((group, 4, size // 4, rows), BF16),
            pltpu.VMEM((group, size, size), F32),
        ],
    )


def on_device_four(expression, gene_mask, mask_value, w_qkv, w_out, w_first, w_second, cotangent):
    me = jnp.stack([lax.axis_index("gene"), lax.axis_index("cell")]).astype(jnp.int32)
    blocks, size, _ = w_first.shape
    deep = size // 4
    counts = [blocks // 4, blocks // 2, blocks // 4]
    chunks = [(3 * deep // 4, True), (deep // 4, True)]
    matrix = grid_turn()
    sends, back = [None] * 3, [[None] * 4 for _ in range(3)]

    def prepare(part, *earlier):
        sends[part] = back_call(
            me, matrix, w_second, after(cotangent, *earlier), sum(counts[:part]), counts[part]
        )
        back[part][0] = sends[part][0]

    def begin(part, bits, *earlier):
        back[part][bits] = flip(after(sends[part][bits], *earlier), "gene", bits)
        return back[part][bits]

    prepare(0)
    beside_qkv = [begin(0, bits) for bits in (3, 2, 1)]
    prepare(1, sends[0][0])
    masked, send, keep = project_call(
        me, after(expression, sends[1][0]), gene_mask, mask_value, w_qkv
    )
    came = flip(after(send, *beside_qkv), "gene", 1)
    beside_sum = begin(1, 3, send, *beside_qkv)
    prepare(2, send)
    w_first_t = jnp.swapaxes(after(w_first, send), 1, 2)
    mine, other = add_call(me, keep, after(came, sends[2][0], w_first_t))
    last = flip(other, "gene", 2)
    queries, *own = split_call(me, mine, after(last, beside_sum))
    across = [flip(piece, "cell", 2) for piece in own]
    beside = [flip(piece, "cell", 1) for piece in own]
    corner = [flip(piece, "cell", 1) for piece in across]
    beside_keys = [begin(1, bits, other) for bits in (2, 1)]
    gathered = [piece for kind in zip(own, beside, across, corner) for piece in kind]
    attended = attend_call(me, queries, gathered)
    near = flip(attended, "gene", 1)
    far = flip(attended, "gene", 2)
    rest = flip(after(far, near, *beside_keys), "gene", 1)
    begin(2, 2, attended)
    hidden, first = first_call(
        me, matrix, (attended, near, far, rest), w_out, masked, w_first_t, chunks
    )
    begin(2, 3, rest)
    begin(2, 1, rest)

    got = []

    def launch(t, *earlier):
        pieces = after(first[t], *earlier)
        if chunks[t][1]:
            got.append([lax.all_to_all(pieces[0], "gene", split_axis=0, concat_axis=0, tiled=True)])
        else:
            got.append([pieces[0]] + [flip(pieces[bits], "gene", bits) for bits in (1, 2, 3)])

    launch(0, *back[2][1:])
    denoised, shares = None, [None, None]
    back = sum(back, [])

    def sum_cells(which, start, send, keep):
        came = [flip(piece, "cell", 1) for piece in send]
        mine, other = pair_call(me, keep, came)
        last = flip(other, "cell", 2)
        shares[which] = finish_call(me, mine, last, shares[which], start, blocks)

    *send, keep = grad_first_call(me, back, hidden, size, 0, blocks // 2)
    *send_next, keep_next = grad_first_call(me, back, hidden, size, blocks // 2, blocks // 2)
    sum_cells(0, 0, send, keep)
    sum_cells(0, blocks // 2, send_next, keep_next)
    pin = shares[0]
    for t in range(len(chunks)):
        start = sum(count for count, _ in chunks[:t]) * blocks // deep
        if t + 1 < len(chunks):
            launch(t + 1, *got[t], pin)
        denoised, *send, keep = second_call(
            me, got[t], w_second, cotangent, hidden, denoised, start
        )
        sum_cells(1, start, send, keep)
        pin = shares[1]
    return (denoised, *shares)


def solution(mesh):
    placed = (
        P(("grp", "cell"), "gene"),
        P(("grp", "cell"), "gene"),
        P("gene"),
        P("gene", None),
        P(None, "gene"),
        P("gene", None, None),
        P("gene", None, None),
        P(("grp", "cell"), "gene"),
    )
    four = mesh.shape["gene"] == 4 and mesh.shape["cell"] == 4
    return jax.shard_map(
        on_device_four if four else on_device_general,
        mesh=mesh,
        in_specs=placed,
        out_specs=(
            P(("grp", "cell"), "gene"),
            P(("grp", "gene"), "cell", None),
            P(("grp", "gene"), "cell", None),
        ),
        check_vma=False,
    )
```

```python
import math

import jax
import jax.numpy as jnp
from jax import lax
from jax.experimental import pallas as pl
from jax.experimental.pallas import tpu as pltpu
from jax.sharding import PartitionSpec as P

HEADS = 16
HEAD_DIM = 64
TILE = 16
BF16 = jnp.bfloat16
F32 = jnp.float32


def normalize(part):
    count, columns = part.shape
    shaped = part.reshape(count, columns // HEAD_DIM, HEAD_DIM)
    meansq = jnp.mean(shaped * shaped, axis=-1, keepdims=True)
    return (shaped * lax.rsqrt(meansq + 1e-06)).astype(BF16).reshape(count, columns)


def attend(queries, key_piece, value_piece):
    query_count, columns = queries.shape
    key_count = key_piece.shape[0]
    heads = columns // HEAD_DIM
    query_heads = queries.reshape(query_count, heads, HEAD_DIM)
    key_heads = key_piece.reshape(key_count, heads, HEAD_DIM)
    value_heads = value_piece.reshape(key_count, heads, HEAD_DIM)
    scores = jnp.einsum(
        "qhd,khd->hqk", query_heads, key_heads, preferred_element_type=F32
    ) * HEAD_DIM ** (-0.5)
    expw = jnp.exp(scores).astype(BF16)
    denom = jnp.sum(expw, axis=2, dtype=F32)
    numer = jnp.einsum("hqk,khd->qhd", expw, value_heads, preferred_element_type=F32)
    return (numer / denom.T[:, :, None]).astype(BF16).reshape(query_count, columns)


def on_device_general(
    expression, gene_mask, mask_value, w_qkv, w_out, w_first, w_second, cotangent
):
    groups = lax.axis_size("gene")
    local_blocks = w_first.shape[0]
    block_size = w_first.shape[1]
    block_total = local_blocks * groups
    cell_rows = expression.shape[0]
    masked_in = jnp.where(gene_mask == 1, mask_value[None, :], expression)
    qkv_part = jnp.dot(masked_in, w_qkv, preferred_element_type=F32)
    qkv_full = lax.psum(qkv_part.astype(BF16), "gene").astype(F32)
    columns = qkv_full.shape[1] // 3
    queries = normalize(qkv_full[:, :columns])
    keys_normed = normalize(qkv_full[:, columns : 2 * columns])
    values_b = qkv_full[:, 2 * columns :].astype(BF16)
    attended = attend(
        queries,
        lax.all_gather(keys_normed, "cell", axis=0, tiled=True),
        lax.all_gather(values_b, "cell", axis=0, tiled=True),
    )
    added = jnp.dot(attended, w_out, preferred_element_type=F32)
    hidden = (masked_in.astype(F32) + added).astype(BF16)
    blocks = hidden.reshape(cell_rows, local_blocks, block_size)
    first = jnp.einsum("cbi,bio->cbo", blocks, w_first, preferred_element_type=F32).astype(BF16)
    cot_blocks = cotangent.reshape(cell_rows, local_blocks, block_size)
    back_perm = jnp.einsum(
        "cjo,jko->cjk", cot_blocks, w_second, preferred_element_type=F32
    ).astype(BF16)
    back_send = back_perm.reshape(cell_rows, block_size // groups, block_total)
    received = lax.all_to_all(first, "gene", split_axis=2, concat_axis=1, tiled=True)
    permuted = jnp.swapaxes(received, 1, 2).reshape(cell_rows, local_blocks, block_size)
    mixed = jnp.einsum("cjk,jko->cjo", permuted, w_second, preferred_element_type=F32)
    denoised = (
        (blocks.astype(F32) + mixed).astype(BF16).reshape(cell_rows, local_blocks * block_size)
    )
    grad_second = jnp.einsum("cjk,cjo->jko", permuted, cot_blocks, preferred_element_type=F32)
    back_recv = lax.all_to_all(back_send, "gene", split_axis=2, concat_axis=1, tiled=True)
    back_first = jnp.swapaxes(back_recv, 1, 2)
    grad_first = jnp.einsum("cbi,cbo->bio", blocks, back_first, preferred_element_type=F32)
    first_share, second_share = (
        lax.psum_scatter(
            grad_first.astype(BF16), "cell", scatter_dimension=1, tiled=True
        ).astype(F32),
        lax.psum_scatter(
            grad_second.astype(BF16), "cell", scatter_dimension=1, tiled=True
        ).astype(F32),
    )
    return (denoised, first_share, second_share)


def after(value, *earlier):
    return lax.optimization_barrier((value, *earlier))[0]


def flip(value, axis, bit):
    pairs = [(i, i ^ bit) for i in range(lax.axis_size(axis))]
    return lax.ppermute(value, axis, pairs)


def call(body, me, args, in_specs, outs, out_specs, grid=(1,), scratch=(), aliases=None):
    return pl.pallas_call(
        body,
        out_shape=outs,
        grid_spec=pltpu.PrefetchScalarGridSpec(
            num_scalar_prefetch=1,
            grid=grid,
            in_specs=in_specs,
            out_specs=out_specs,
            scratch_shapes=list(scratch),
        ),
        input_output_aliases=aliases or {},
        compiler_params=pltpu.CompilerParams(vmem_limit_bytes=52 * 2**20),
        cost_estimate=pl.CostEstimate(flops=1, bytes_accessed=1, transcendentals=0),
    )(me, *args)


def spec(shape, place):
    return pl.BlockSpec(shape, place)


def whole(shape):
    return pl.BlockSpec(shape, lambda *_: (0,) * len(shape))


def several(count):
    return next(group for group in (4, 2, 1) if count % group == 0)


def array(shape, dtype):
    return jax.ShapeDtypeStruct(shape, dtype)


def grid_turn():
    rows = lax.broadcasted_iota(jnp.int32, (TILE * TILE, TILE * TILE), 0)
    columns = lax.broadcasted_iota(jnp.int32, (TILE * TILE, TILE * TILE), 1)
    return ((rows % TILE) * TILE + rows // TILE == columns).astype(BF16)


def turn(matrix, tile):
    rows = tile.shape[-1]
    flat = tile.reshape(TILE * TILE, rows)
    return jnp.dot(matrix, flat, preferred_element_type=F32).astype(BF16).reshape(TILE, TILE, rows)


def back_kernel(me_ref, turn_ref, second_ref, cot_ref, *refs):
    outs, held = refs[:4], refs[4]
    blocks, rows = held.shape[2], held.shape[3]
    group, size, _ = second_ref.shape
    pair = size // (4 * blocks)
    steps = TILE // (pair * group)
    at = pl.program_id(0) % steps
    for g in range(group):
        back = lax.dot_general(
            second_ref[g],
            cot_ref[:, g * size : (g + 1) * size],
            (((1,), (1,)), ((), ())),
            preferred_element_type=F32,
        ).astype(BF16)
        held[pl.ds((at * group + g) * pair, pair)] = back.reshape(pair, 4, blocks, rows)

    @pl.when(at == steps - 1)
    def _():
        for bits in range(4):
            there = me_ref[0] ^ bits
            for low in range(0, blocks, TILE):
                outs[bits][low : low + TILE] = turn(
                    turn_ref[...], held[:, there, low : low + TILE, :]
                )


def back_call(me, matrix, w_second, cotangent, start, count):
    blocks, size, _ = w_second.shape
    rows = cotangent.shape[0]
    pair = size // (4 * blocks)
    group = several(math.gcd(count, TILE // pair))
    steps = TILE // (pair * group)
    first = start // group
    piece = array((blocks, count * pair, rows), BF16)
    return call(
        back_kernel,
        me,
        (matrix, w_second, cotangent),
        [
            whole(matrix.shape),
            spec((group, size, size), lambda j, _: (first + j, 0, 0)),
            spec((rows, group * size), lambda j, _: (0, first + j)),
        ],
        [piece] * 4,
        [spec((blocks, TILE, rows), lambda j, _: (0, j // steps, 0))] * 4,
        grid=(count // group,),
        scratch=[pltpu.VMEM((TILE, 4, blocks, rows), BF16)],
    )


def project_kernel(me_ref, value_ref, mask_ref, fill_ref, weight_ref, *refs):
    masked_ref, send_ref, keep_ref, total = refs
    step = pl.program_id(0)
    masked = jnp.where(
        mask_ref[...] == 1, fill_ref[...].astype(F32), value_ref[...].astype(F32)
    ).astype(BF16)
    masked_ref[...] = masked
    width = total.shape[1] // 3

    @pl.when(step == 0)
    def _():
        total[...] = jnp.dot(masked, weight_ref[...], preferred_element_type=F32)

    @pl.when(step > 0)
    def _():
        total[...] += jnp.dot(masked, weight_ref[...], preferred_element_type=F32)

    @pl.when(step == pl.num_programs(0) - 1)
    def _():
        share = width // 4
        for out, flips in ((send_ref, (1, 3)), (keep_ref, (0, 2))):
            for slot, bits in enumerate(flips):
                for kind in range(3):
                    place = pl.multiple_of(kind * width + (me_ref[0] ^ bits) * share, share)
                    out[slot, :, kind * share : (kind + 1) * share] = total[
                        :, pl.ds(place, share)
                    ].astype(out.dtype)


def project_call(me, expression, gene_mask, mask_value, w_qkv):
    rows, genes = expression.shape
    width = w_qkv.shape[1]
    depth = min(genes, 1024)
    wide = spec((rows, depth), lambda i, _: (0, i))
    shape = (2, rows, width // 4)
    return call(
        project_kernel,
        me,
        (expression, gene_mask, mask_value.reshape(1, genes), w_qkv),
        [
            wide,
            wide,
            spec((1, depth), lambda i, _: (0, i)),
            spec((depth, width), lambda i, _: (i, 0)),
        ],
        [array((rows, genes), BF16), array(shape, BF16), array(shape, F32)],
        [wide, whole(shape), whole(shape)],
        grid=(genes // depth,),
        scratch=[pltpu.VMEM((rows, width), F32)],
    )


def store_quarters(me, at, held, send_ref, keep_ref):
    quarter = held.shape[0] // 4
    for bits in range(4):
        start = pl.multiple_of((me ^ bits) * quarter, quarter)
        part = held[pl.ds(start, quarter), :]
        if bits % 2:
            send_ref[bits // 2][at] = part.astype(BF16)
        else:
            keep_ref[bits // 2, at] = part


def quarter_outs(count, group, size):
    shape = (count, size // 4, size)
    one = spec((group, *shape[1:]), lambda j, _: (j, 0, 0))
    two = spec((2, group, *shape[1:]), lambda j, _: (0, j, 0, 0))
    return [array(shape, BF16)] * 2 + [array((2, *shape), F32)], [one, one, two]


def add_kernel(_, keep_ref, came_ref, mine_ref, other_ref):
    mine_ref[...] = keep_ref[0] + came_ref[0].astype(F32)
    other_ref[...] = (keep_ref[1] + came_ref[1].astype(F32)).astype(BF16)


def add_call(me, keep, came):
    shape = keep.shape
    return call(
        add_kernel,
        me,
        (keep, came),
        [whole(shape), whole(shape)],
        [array(shape[1:], F32), array(shape[1:], BF16)],
        [whole(shape[1:])] * 2,
    )


def normalize_heads(part):
    columns = part.shape[1]
    heads = [lax.broadcasted_iota(jnp.int32, (columns, columns), d) // HEAD_DIM for d in (0, 1)]
    same = (heads[0] == heads[1]).astype(F32)
    sums = jnp.dot(
        part * part, same, precision=lax.Precision.HIGHEST, preferred_element_type=F32
    )
    return (part * lax.rsqrt(sums * (1.0 / HEAD_DIM) + 1e-06)).astype(BF16)


def pair_kernel(_, keep_ref, came_ref, next_ref, mine_ref, other_ref):
    mine_ref[...] = keep_ref[0] + came_ref[...].astype(F32)
    other_ref[...] = (keep_ref[1] + next_ref[...].astype(F32)).astype(BF16)


def pair_call(me, keep, came):
    shape = keep.shape[1:]
    return call(
        pair_kernel,
        me,
        (keep, *came),
        [whole(keep.shape), whole(shape), whole(shape)],
        [array(shape, F32), array(shape, BF16)],
        [whole(shape)] * 2,
    )


def finish_kernel(_, mine_ref, came_ref, *refs):
    refs[-1][...] = mine_ref[...] + came_ref[...].astype(F32)


def finish_call(me, mine, came, total, start, blocks):
    count, quarter, size = mine.shape
    step = math.gcd(count, start) if start else count
    args = [mine, came]
    in_specs = [spec((step, quarter, size), lambda i, _: (i, 0, 0))] * 2
    aliases = {}
    if total is not None:
        args.append(total)
        in_specs.append(pl.BlockSpec(memory_space=pl.ANY))
        aliases = {len(args): 0}
    return call(
        finish_kernel,
        me,
        args,
        in_specs,
        array((blocks, quarter, size), F32),
        spec((step, quarter, size), lambda i, _: (start // step + i, 0, 0)),
        grid=(count // step,),
        aliases=aliases,
    )


def split_kernel(_, mine_ref, came_ref, query_ref, key_ref, value_ref):
    total = mine_ref[...] + came_ref[...].astype(F32)
    share = total.shape[1] // 3
    query_ref[...] = normalize_heads(total[:, :share])
    key_ref[...] = normalize_heads(total[:, share : 2 * share])
    value_ref[...] = total[:, 2 * share :].astype(BF16)


def split_call(me, mine, came):
    rows, columns = mine.shape
    shapes = ((rows, columns // 3),) * 3
    return call(
        split_kernel,
        me,
        (mine, came),
        [whole(mine.shape)] * 2,
        [array(shape, BF16) for shape in shapes],
        [whole(shape) for shape in shapes],
    )


def attend_kernel(_, query_ref, *refs):
    count = len(refs) // 2
    keys, values, out_ref = refs[:count], refs[count:-1], refs[-1]
    queries = query_ref[...]
    rows, share = queries.shape
    head_of = lax.broadcasted_iota(jnp.int32, (rows, share), 1) // HEAD_DIM
    out = jnp.zeros((rows, share), F32)
    for head in range(share // HEAD_DIM):
        query = jnp.where(head_of == head, queries.astype(F32) * HEAD_DIM**-0.5, 0.0).astype(BF16)
        numer = jnp.zeros((rows, share), F32)
        denom = jnp.zeros((rows, 1), F32)
        for key, value in zip(keys, values):
            scores = lax.dot_general(
                query, key[...], (((1,), (1,)), ((), ())), preferred_element_type=F32
            )
            expw = jnp.exp(scores).astype(BF16)
            denom += jnp.sum(expw.astype(F32), axis=1, keepdims=True)
            numer += jnp.dot(expw, value[...], preferred_element_type=F32)
        out = jnp.where(head_of == head, numer / denom, out)
    out_ref[...] = out.astype(BF16)


def attend_call(me, queries, pieces):
    rows, share = queries.shape
    some = rows // 2
    part = spec((some, share), lambda i, _: (i, 0))
    return call(
        attend_kernel,
        me,
        (queries, *pieces),
        [part] + [whole(piece.shape) for piece in pieces],
        array((rows, share), BF16),
        part,
        grid=(2,),
    )


def first_kernel(me_ref, turn_ref, own, near, far, rest, w_out_ref, masked_ref, wf_ref, *refs):
    hidden_ref, outs, gathered, held = refs[0], refs[1:-2], refs[-2], refs[-1]
    step = pl.program_id(0)
    share = own.shape[1]
    group, size, _ = wf_ref.shape
    steps = TILE // group

    @pl.when(step == 0)
    def _():
        for bits, piece in enumerate((own, near, far, rest)):
            place = pl.multiple_of((me_ref[0] ^ bits) * share, share)
            gathered[:, pl.ds(place, share)] = piece[...]

    added = jnp.dot(gathered[...], w_out_ref[...], preferred_element_type=F32)
    hidden = (masked_ref[...].astype(F32) + added).astype(BF16)
    hidden_ref[...] = hidden
    for g in range(group):
        held[step % steps * group + g] = lax.dot_general(
            wf_ref[g],
            hidden[:, g * size : (g + 1) * size],
            (((1,), (1,)), ((), ())),
            preferred_element_type=F32,
        ).astype(BF16)

    @pl.when(step % steps == steps - 1)
    def _():
        chunks = []
        rest = list(outs)
        while rest:
            swapped = len(rest[0].shape) == 4
            refs = rest[: 1 if swapped else 4]
            rest = rest[len(refs) :]
            chunks.append((refs, refs[0].shape[1 if swapped else 0]))
        deep = sum(count for _, count in chunks)
        for bits in range(4):
            there = me_ref[0] ^ bits
            for low in range(0, deep, TILE):
                start = pl.multiple_of(there * deep + low, TILE)
                tile = turn(turn_ref[...], held[:, pl.ds(start, TILE), :])
                begin = 0
                for refs, count in chunks:
                    least, most = max(begin, low), min(begin + count, low + TILE)
                    if least < most:
                        target = refs[0].at[there] if len(refs) == 1 else refs[bits]
                        target[least - begin : most - begin] = tile[least - low : most - low]
                    begin += count


def first_call(me, matrix, attended, w_out, masked, w_first_t, chunks):
    blocks, size, _ = w_first_t.shape
    rows, genes = masked.shape
    width = w_out.shape[0]
    group = several(TILE)
    steps = TILE // group
    wide = spec((rows, group * size), lambda b, _: (0, b))
    outs, places = [array((rows, genes), BF16)], [wide]
    for deep, swapped in chunks:
        if swapped:
            outs.append(array((4, deep, blocks, rows), BF16))
            places.append(spec((4, deep, TILE, rows), lambda b, _: (0, 0, b // steps, 0)))
        else:
            outs += [array((deep, blocks, rows), BF16)] * 4
            places += [spec((deep, TILE, rows), lambda b, _: (0, b // steps, 0))] * 4
    hidden, *first = call(
        first_kernel,
        me,
        (matrix, *attended, w_out, masked, w_first_t),
        [whole(matrix.shape)]
        + [whole(part.shape) for part in attended]
        + [
            spec((width, group * size), lambda b, _: (0, b)),
            wide,
            spec((group, size, size), lambda b, _: (b, 0, 0)),
        ],
        outs,
        places,
        grid=(blocks // group,),
        scratch=[pltpu.VMEM((rows, width), BF16), pltpu.VMEM((TILE, size, rows), BF16)],
    )
    taken = []
    for _, swapped in chunks:
        wanted = 1 if swapped else 4
        taken.append(first[:wanted])
        first = first[wanted:]
    return hidden, taken


def second_kernel(me_ref, *refs):
    pieces = refs[: 1 if len(refs[0].shape) == 4 else 4]
    w_ref, cot_ref, hidden_ref = refs[len(pieces) : len(pieces) + 3]
    out_ref, *send_ref, keep_ref, square, held = refs[-6:]
    group, size, _ = w_ref.shape
    pair = held.shape[1]
    for g in range(group):
        at = slice(g * size, (g + 1) * size)
        mine = slice(g * pair, (g + 1) * pair)
        if len(pieces) == 1:
            for source in range(4):
                held[g, :, source] = pieces[0][source, mine]
        else:
            for bits in range(4):
                held[g, :, me_ref[0] ^ bits] = pieces[bits][mine]
        permuted = held[g].reshape(size, held.shape[4])
        square[g] = jnp.dot(permuted, cot_ref[:, at], preferred_element_type=F32)
        store_quarters(me_ref[1], g, square.at[g], send_ref, keep_ref)
        mixed = lax.dot_general(
            permuted, w_ref[g], (((0,), (0,)), ((), ())), preferred_element_type=F32
        )
        out_ref[:, at] = (hidden_ref[:, at].astype(F32) + mixed).astype(BF16)


def second_call(me, pieces, w_second, cotangent, hidden, denoised, start, low, count):
    blocks, size, _ = w_second.shape
    rows = hidden.shape[0]
    pair = size // (4 * blocks)
    group = several(math.gcd(count, start, low))
    begin, low = start // group, low // group
    wide = spec((rows, group * size), lambda j, _: (0, begin + j))
    square = spec((group, size, size), lambda j, _: (begin + j, 0, 0))
    args = [*pieces, w_second, cotangent, hidden]
    part = (group * pair, blocks, rows)
    if len(pieces) == 1:
        in_specs = [spec((4, *part), lambda j, _: (0, low + j, 0, 0))]
    else:
        in_specs = [spec(part, lambda j, _: (low + j, 0, 0))] * 4
    in_specs += [square, wide, wide]
    quarters = quarter_outs(count, group, size)
    aliases = {}
    if denoised is not None:
        args.append(denoised)
        in_specs.append(pl.BlockSpec(memory_space=pl.ANY))
        aliases = {len(args): 0}
    return call(
        second_kernel,
        me,
        args,
        in_specs,
        [array(hidden.shape, BF16), *quarters[0]],
        [wide, *quarters[1]],
        grid=(count // group,),
        scratch=[
            pltpu.VMEM((group, size, size), F32),
            pltpu.VMEM((group, pair, 4, blocks, rows), BF16),
        ],
        aliases=aliases,
    )


def grad_first_kernel(me_ref, *refs):
    pieces, (hidden_ref, *send_ref, keep_ref, held, square) = refs[:-6], refs[-6:]
    group, size, _ = square.shape
    for g in range(group):
        low = 0
        for part in range(0, len(pieces), 4):
            deep = pieces[part].shape[1]
            for bits in range(4):
                held[g, me_ref[0] ^ bits, low : low + deep] = pieces[part + bits][g]
            low += deep
        back = held[g].reshape(size, held.shape[3])
        hidden = hidden_ref[:, g * size : (g + 1) * size]
        square[g] = jnp.dot(back, hidden, preferred_element_type=F32).T
        store_quarters(me_ref[1], g, square.at[g], send_ref, keep_ref)


def grad_first_call(me, pieces, hidden, size, start, count):
    rows = hidden.shape[0]
    group = several(math.gcd(count, start) if start else count)
    begin = start // group
    return call(
        grad_first_kernel,
        me,
        (*pieces, hidden),
        [spec((group, *piece.shape[1:]), lambda b, _: (begin + b, 0, 0)) for piece in pieces]
        + [spec((rows, group * size), lambda b, _: (0, begin + b))],
        *quarter_outs(count, group, size),
        grid=(count // group,),
        scratch=[
            pltpu.VMEM((group, 4, size // 4, rows), BF16),
            pltpu.VMEM((group, size, size), F32),
        ],
    )


def on_device_four(expression, gene_mask, mask_value, w_qkv, w_out, w_first, w_second, cotangent):
    me = jnp.stack([lax.axis_index("gene"), lax.axis_index("cell")]).astype(jnp.int32)
    blocks, size, _ = w_first.shape
    deep = size // 4
    counts = [blocks // 4, blocks // 2, blocks // 4]
    chunks = [(3 * deep // 4, True), (deep // 4, True)]
    matrix = grid_turn()
    sends, back = [None] * 3, [[None] * 4 for _ in range(3)]

    def prepare(part, *earlier):
        sends[part] = back_call(
            me, matrix, w_second, after(cotangent, *earlier), sum(counts[:part]), counts[part]
        )
        back[part][0] = sends[part][0]

    def begin(part, bits, *earlier):
        back[part][bits] = flip(after(sends[part][bits], *earlier), "gene", bits)
        return back[part][bits]

    prepare(0)
    beside_qkv = [begin(0, bits) for bits in (3, 2, 1)]
    prepare(1, sends[0][0])
    masked, send, keep = project_call(
        me, after(expression, sends[1][0]), gene_mask, mask_value, w_qkv
    )
    came = flip(after(send, *beside_qkv), "gene", 1)
    beside_sum = begin(1, 3, send, *beside_qkv)
    prepare(2, send)
    w_first_t = jnp.swapaxes(after(w_first, send), 1, 2)
    mine, other = add_call(me, keep, after(came, sends[2][0], w_first_t))
    last = flip(other, "gene", 2)
    queries, *own = split_call(me, mine, after(last, beside_sum))
    across = [flip(piece, "cell", 2) for piece in own]
    beside = [flip(piece, "cell", 1) for piece in own]
    corner = [flip(piece, "cell", 1) for piece in across]
    beside_keys = [begin(1, bits, last, beside_sum) for bits in (2, 1)]
    gathered = [piece for kind in zip(own, beside, across, corner) for piece in kind]
    attended = attend_call(me, queries, gathered)
    near = flip(attended, "gene", 1)
    far = flip(attended, "gene", 2)
    rest = flip(after(far, near, *beside_keys), "gene", 1)
    begin(2, 2, attended)
    hidden, first = first_call(
        me, matrix, (attended, near, far, rest), w_out, masked, w_first_t, chunks
    )
    begin(2, 3, rest)
    begin(2, 1, rest)

    got = []

    def launch(t, *earlier):
        pieces = after(first[t], *earlier)
        if chunks[t][1]:
            got.append([lax.all_to_all(pieces[0], "gene", split_axis=0, concat_axis=0, tiled=True)])
        else:
            got.append([pieces[0]] + [flip(pieces[bits], "gene", bits) for bits in (1, 2, 3)])

    launch(0, *back[2][1:])
    denoised, shares = None, [None, None]
    back = sum(back, [])

    def sum_cells(which, start, send, keep):
        came = [flip(piece, "cell", 1) for piece in send]
        mine, other = pair_call(me, keep, came)
        last = flip(other, "cell", 2)
        shares[which] = finish_call(me, mine, last, shares[which], start, blocks)

    *send, keep = grad_first_call(me, back, hidden, size, 0, blocks // 2)
    *send_next, keep_next = grad_first_call(me, back, hidden, size, blocks // 2, blocks // 2)
    sum_cells(0, 0, send, keep)
    sum_cells(0, blocks // 2, send_next, keep_next)
    pin = shares[0]
    for t in range(len(chunks)):
        if t + 1 < len(chunks):
            launch(t + 1, *got[t], pin)
        start, count = (n * blocks // deep for n in (sum(n for n, _ in chunks[:t]), chunks[t][0]))
        calls = 2 if t == len(chunks) - 1 else 1
        count //= calls
        for low in range(0, calls * count, count):
            denoised, *send, keep = second_call(
                me, got[t], w_second, cotangent, hidden, denoised, start + low, low, count
            )
            sum_cells(1, start + low, send, keep)
        pin = shares[1]
    return (denoised, *shares)


def solution(mesh):
    placed = (
        P(("grp", "cell"), "gene"),
        P(("grp", "cell"), "gene"),
        P("gene"),
        P("gene", None),
        P(None, "gene"),
        P("gene", None, None),
        P("gene", None, None),
        P(("grp", "cell"), "gene"),
    )
    four = mesh.shape["gene"] == 4 and mesh.shape["cell"] == 4
    return jax.shard_map(
        on_device_four if four else on_device_general,
        mesh=mesh,
        in_specs=placed,
        out_specs=(
            P(("grp", "cell"), "gene"),
            P(("grp", "gene"), "cell", None),
            P(("grp", "gene"), "cell", None),
        ),
        check_vma=False,
    )
```

```python
import math

import jax
import jax.numpy as jnp
from jax import lax
from jax.experimental import pallas as pl
from jax.experimental.pallas import tpu as pltpu
from jax.sharding import PartitionSpec as P

HEADS = 16
HEAD_DIM = 64
TILE = 16
BF16 = jnp.bfloat16
F32 = jnp.float32


def normalize(part):
    count, columns = part.shape
    shaped = part.reshape(count, columns // HEAD_DIM, HEAD_DIM)
    meansq = jnp.mean(shaped * shaped, axis=-1, keepdims=True)
    return (shaped * lax.rsqrt(meansq + 1e-06)).astype(BF16).reshape(count, columns)


def attend(queries, key_piece, value_piece):
    query_count, columns = queries.shape
    key_count = key_piece.shape[0]
    heads = columns // HEAD_DIM
    query_heads = queries.reshape(query_count, heads, HEAD_DIM)
    key_heads = key_piece.reshape(key_count, heads, HEAD_DIM)
    value_heads = value_piece.reshape(key_count, heads, HEAD_DIM)
    scores = jnp.einsum(
        "qhd,khd->hqk", query_heads, key_heads, preferred_element_type=F32
    ) * HEAD_DIM ** (-0.5)
    expw = jnp.exp(scores).astype(BF16)
    denom = jnp.sum(expw, axis=2, dtype=F32)
    numer = jnp.einsum("hqk,khd->qhd", expw, value_heads, preferred_element_type=F32)
    return (numer / denom.T[:, :, None]).astype(BF16).reshape(query_count, columns)


def on_device_general(
    expression, gene_mask, mask_value, w_qkv, w_out, w_first, w_second, cotangent
):
    groups = lax.axis_size("gene")
    local_blocks = w_first.shape[0]
    block_size = w_first.shape[1]
    block_total = local_blocks * groups
    cell_rows = expression.shape[0]
    masked_in = jnp.where(gene_mask == 1, mask_value[None, :], expression)
    qkv_part = jnp.dot(masked_in, w_qkv, preferred_element_type=F32)
    qkv_full = lax.psum(qkv_part.astype(BF16), "gene").astype(F32)
    columns = qkv_full.shape[1] // 3
    queries = normalize(qkv_full[:, :columns])
    keys_normed = normalize(qkv_full[:, columns : 2 * columns])
    values_b = qkv_full[:, 2 * columns :].astype(BF16)
    attended = attend(
        queries,
        lax.all_gather(keys_normed, "cell", axis=0, tiled=True),
        lax.all_gather(values_b, "cell", axis=0, tiled=True),
    )
    added = jnp.dot(attended, w_out, preferred_element_type=F32)
    hidden = (masked_in.astype(F32) + added).astype(BF16)
    blocks = hidden.reshape(cell_rows, local_blocks, block_size)
    first = jnp.einsum("cbi,bio->cbo", blocks, w_first, preferred_element_type=F32).astype(BF16)
    cot_blocks = cotangent.reshape(cell_rows, local_blocks, block_size)
    back_perm = jnp.einsum(
        "cjo,jko->cjk", cot_blocks, w_second, preferred_element_type=F32
    ).astype(BF16)
    back_send = back_perm.reshape(cell_rows, block_size // groups, block_total)
    received = lax.all_to_all(first, "gene", split_axis=2, concat_axis=1, tiled=True)
    permuted = jnp.swapaxes(received, 1, 2).reshape(cell_rows, local_blocks, block_size)
    mixed = jnp.einsum("cjk,jko->cjo", permuted, w_second, preferred_element_type=F32)
    denoised = (
        (blocks.astype(F32) + mixed).astype(BF16).reshape(cell_rows, local_blocks * block_size)
    )
    grad_second = jnp.einsum("cjk,cjo->jko", permuted, cot_blocks, preferred_element_type=F32)
    back_recv = lax.all_to_all(back_send, "gene", split_axis=2, concat_axis=1, tiled=True)
    back_first = jnp.swapaxes(back_recv, 1, 2)
    grad_first = jnp.einsum("cbi,cbo->bio", blocks, back_first, preferred_element_type=F32)
    first_share, second_share = (
        lax.psum_scatter(
            grad_first.astype(BF16), "cell", scatter_dimension=1, tiled=True
        ).astype(F32),
        lax.psum_scatter(
            grad_second.astype(BF16), "cell", scatter_dimension=1, tiled=True
        ).astype(F32),
    )
    return (denoised, first_share, second_share)


def after(value, *earlier):
    return lax.optimization_barrier((value, *earlier))[0]


def flip(value, axis, bit):
    pairs = [(i, i ^ bit) for i in range(lax.axis_size(axis))]
    return lax.ppermute(value, axis, pairs)


def call(body, me, args, in_specs, outs, out_specs, grid=(1,), scratch=(), aliases=None):
    return pl.pallas_call(
        body,
        out_shape=outs,
        grid_spec=pltpu.PrefetchScalarGridSpec(
            num_scalar_prefetch=1,
            grid=grid,
            in_specs=in_specs,
            out_specs=out_specs,
            scratch_shapes=list(scratch),
        ),
        input_output_aliases=aliases or {},
        compiler_params=pltpu.CompilerParams(vmem_limit_bytes=52 * 2**20),
        cost_estimate=pl.CostEstimate(flops=1, bytes_accessed=1, transcendentals=0),
    )(me, *args)


def spec(shape, place):
    return pl.BlockSpec(shape, place)


def whole(shape):
    return pl.BlockSpec(shape, lambda *_: (0,) * len(shape))


def several(count):
    return next(group for group in (4, 2, 1) if count % group == 0)


def array(shape, dtype):
    return jax.ShapeDtypeStruct(shape, dtype)


def grid_turn():
    rows = lax.broadcasted_iota(jnp.int32, (TILE * TILE, TILE * TILE), 0)
    columns = lax.broadcasted_iota(jnp.int32, (TILE * TILE, TILE * TILE), 1)
    return ((rows % TILE) * TILE + rows // TILE == columns).astype(BF16)


def turn(matrix, tile):
    rows = tile.shape[-1]
    flat = tile.reshape(TILE * TILE, rows)
    return jnp.dot(matrix, flat, preferred_element_type=F32).astype(BF16).reshape(TILE, TILE, rows)


def back_kernel(me_ref, turn_ref, second_ref, cot_ref, *refs):
    outs, held = refs[:4], refs[4]
    blocks, rows = held.shape[2], held.shape[3]
    group, size, _ = second_ref.shape
    pair = size // (4 * blocks)
    steps = TILE // (pair * group)
    at = pl.program_id(0) % steps
    for g in range(group):
        back = lax.dot_general(
            second_ref[g],
            cot_ref[:, g * size : (g + 1) * size],
            (((1,), (1,)), ((), ())),
            preferred_element_type=F32,
        ).astype(BF16)
        held[pl.ds((at * group + g) * pair, pair)] = back.reshape(pair, 4, blocks, rows)

    @pl.when(at == steps - 1)
    def _():
        for bits in range(4):
            there = me_ref[0] ^ bits
            for low in range(0, blocks, TILE):
                outs[bits][low : low + TILE] = turn(
                    turn_ref[...], held[:, there, low : low + TILE, :]
                )


def back_call(me, matrix, w_second, cotangent, start, count):
    blocks, size, _ = w_second.shape
    rows = cotangent.shape[0]
    pair = size // (4 * blocks)
    group = several(math.gcd(count, TILE // pair))
    steps = TILE // (pair * group)
    first = start // group
    piece = array((blocks, count * pair, rows), BF16)
    return call(
        back_kernel,
        me,
        (matrix, w_second, cotangent),
        [
            whole(matrix.shape),
            spec((group, size, size), lambda j, _: (first + j, 0, 0)),
            spec((rows, group * size), lambda j, _: (0, first + j)),
        ],
        [piece] * 4,
        [spec((blocks, TILE, rows), lambda j, _: (0, j // steps, 0))] * 4,
        grid=(count // group,),
        scratch=[pltpu.VMEM((TILE, 4, blocks, rows), BF16)],
    )


def project_kernel(me_ref, value_ref, mask_ref, fill_ref, weight_ref, *refs):
    masked_ref, send_ref, keep_ref, total = refs
    step = pl.program_id(0)
    masked = jnp.where(
        mask_ref[...] == 1, fill_ref[...].astype(F32), value_ref[...].astype(F32)
    ).astype(BF16)
    masked_ref[...] = masked
    width = total.shape[1] // 3

    @pl.when(step == 0)
    def _():
        total[...] = jnp.dot(masked, weight_ref[...], preferred_element_type=F32)

    @pl.when(step > 0)
    def _():
        total[...] += jnp.dot(masked, weight_ref[...], preferred_element_type=F32)

    @pl.when(step == pl.num_programs(0) - 1)
    def _():
        share = width // 4
        for out, flips in ((send_ref, (1, 3)), (keep_ref, (0, 2))):
            for slot, bits in enumerate(flips):
                for kind in range(3):
                    place = pl.multiple_of(kind * width + (me_ref[0] ^ bits) * share, share)
                    out[slot, :, kind * share : (kind + 1) * share] = total[
                        :, pl.ds(place, share)
                    ].astype(out.dtype)


def project_call(me, expression, gene_mask, mask_value, w_qkv):
    rows, genes = expression.shape
    width = w_qkv.shape[1]
    depth = min(genes, 1024)
    wide = spec((rows, depth), lambda i, _: (0, i))
    shape = (2, rows, width // 4)
    return call(
        project_kernel,
        me,
        (expression, gene_mask, mask_value.reshape(1, genes), w_qkv),
        [
            wide,
            wide,
            spec((1, depth), lambda i, _: (0, i)),
            spec((depth, width), lambda i, _: (i, 0)),
        ],
        [array((rows, genes), BF16), array(shape, BF16), array(shape, F32)],
        [wide, whole(shape), whole(shape)],
        grid=(genes // depth,),
        scratch=[pltpu.VMEM((rows, width), F32)],
    )


def store_quarters(me, at, held, send_ref, keep_ref):
    quarter = held.shape[0] // 4
    for bits in range(4):
        start = pl.multiple_of((me ^ bits) * quarter, quarter)
        part = held[pl.ds(start, quarter), :]
        if bits % 2:
            send_ref[bits // 2][at] = part.astype(BF16)
        else:
            keep_ref[bits // 2, at] = part


def quarter_outs(count, group, size):
    shape = (count, size // 4, size)
    one = spec((group, *shape[1:]), lambda j, _: (j, 0, 0))
    two = spec((2, group, *shape[1:]), lambda j, _: (0, j, 0, 0))
    return [array(shape, BF16)] * 2 + [array((2, *shape), F32)], [one, one, two]


def add_kernel(_, keep_ref, came_ref, mine_ref, other_ref):
    mine_ref[...] = keep_ref[0] + came_ref[0].astype(F32)
    other_ref[...] = (keep_ref[1] + came_ref[1].astype(F32)).astype(BF16)


def add_call(me, keep, came):
    shape = keep.shape
    return call(
        add_kernel,
        me,
        (keep, came),
        [whole(shape), whole(shape)],
        [array(shape[1:], F32), array(shape[1:], BF16)],
        [whole(shape[1:])] * 2,
    )


def normalize_heads(part):
    columns = part.shape[1]
    heads = [lax.broadcasted_iota(jnp.int32, (columns, columns), d) // HEAD_DIM for d in (0, 1)]
    same = (heads[0] == heads[1]).astype(F32)
    sums = jnp.dot(
        part * part, same, precision=lax.Precision.HIGHEST, preferred_element_type=F32
    )
    return (part * lax.rsqrt(sums * (1.0 / HEAD_DIM) + 1e-06)).astype(BF16)


def pair_kernel(_, keep_ref, came_ref, next_ref, mine_ref, other_ref):
    mine_ref[...] = keep_ref[0] + came_ref[...].astype(F32)
    other_ref[...] = (keep_ref[1] + next_ref[...].astype(F32)).astype(BF16)


def pair_call(me, keep, came):
    shape = keep.shape[1:]
    return call(
        pair_kernel,
        me,
        (keep, *came),
        [whole(keep.shape), whole(shape), whole(shape)],
        [array(shape, F32), array(shape, BF16)],
        [whole(shape)] * 2,
    )


def finish_kernel(_, mine_ref, came_ref, *refs):
    refs[-1][...] = mine_ref[...] + came_ref[...].astype(F32)


def finish_call(me, mine, came, total, start, blocks):
    count, quarter, size = mine.shape
    step = math.gcd(count, start) if start else count
    args = [mine, came]
    in_specs = [spec((step, quarter, size), lambda i, _: (i, 0, 0))] * 2
    aliases = {}
    if total is not None:
        args.append(total)
        in_specs.append(pl.BlockSpec(memory_space=pl.ANY))
        aliases = {len(args): 0}
    return call(
        finish_kernel,
        me,
        args,
        in_specs,
        array((blocks, quarter, size), F32),
        spec((step, quarter, size), lambda i, _: (start // step + i, 0, 0)),
        grid=(count // step,),
        aliases=aliases,
    )


def split_kernel(_, mine_ref, came_ref, query_ref, key_ref, value_ref):
    total = mine_ref[...] + came_ref[...].astype(F32)
    share = total.shape[1] // 3
    query_ref[...] = normalize_heads(total[:, :share])
    key_ref[...] = normalize_heads(total[:, share : 2 * share])
    value_ref[...] = total[:, 2 * share :].astype(BF16)


def split_call(me, mine, came):
    rows, columns = mine.shape
    shapes = ((rows, columns // 3),) * 3
    return call(
        split_kernel,
        me,
        (mine, came),
        [whole(mine.shape)] * 2,
        [array(shape, BF16) for shape in shapes],
        [whole(shape) for shape in shapes],
    )


def attend_kernel(_, query_ref, *refs):
    count = len(refs) // 2
    keys, values, out_ref = refs[:count], refs[count:-1], refs[-1]
    queries = query_ref[...]
    rows, share = queries.shape
    head_of = lax.broadcasted_iota(jnp.int32, (rows, share), 1) // HEAD_DIM
    out = jnp.zeros((rows, share), F32)
    for head in range(share // HEAD_DIM):
        query = jnp.where(head_of == head, queries.astype(F32) * HEAD_DIM**-0.5, 0.0).astype(BF16)
        numer = jnp.zeros((rows, share), F32)
        denom = jnp.zeros((rows, 1), F32)
        for key, value in zip(keys, values):
            scores = lax.dot_general(
                query, key[...], (((1,), (1,)), ((), ())), preferred_element_type=F32
            )
            expw = jnp.exp(scores).astype(BF16)
            denom += jnp.sum(expw.astype(F32), axis=1, keepdims=True)
            numer += jnp.dot(expw, value[...], preferred_element_type=F32)
        out = jnp.where(head_of == head, numer / denom, out)
    out_ref[...] = out.astype(BF16)


def attend_call(me, queries, pieces):
    rows, share = queries.shape
    some = rows // 2
    part = spec((some, share), lambda i, _: (i, 0))
    return call(
        attend_kernel,
        me,
        (queries, *pieces),
        [part] + [whole(piece.shape) for piece in pieces],
        array((rows, share), BF16),
        part,
        grid=(2,),
    )


def first_kernel(me_ref, turn_ref, own, near, far, rest, w_out_ref, masked_ref, wf_ref, *refs):
    hidden_ref, outs, gathered, held = refs[0], refs[1:-2], refs[-2], refs[-1]
    step = pl.program_id(0)
    share = own.shape[1]
    group, size, _ = wf_ref.shape
    steps = TILE // group

    @pl.when(step == 0)
    def _():
        for bits, piece in enumerate((own, near, far, rest)):
            place = pl.multiple_of((me_ref[0] ^ bits) * share, share)
            gathered[:, pl.ds(place, share)] = piece[...]

    added = jnp.dot(gathered[...], w_out_ref[...], preferred_element_type=F32)
    hidden = (masked_ref[...].astype(F32) + added).astype(BF16)
    hidden_ref[...] = hidden
    for g in range(group):
        held[step % steps * group + g] = lax.dot_general(
            wf_ref[g],
            hidden[:, g * size : (g + 1) * size],
            (((1,), (1,)), ((), ())),
            preferred_element_type=F32,
        ).astype(BF16)

    @pl.when(step % steps == steps - 1)
    def _():
        chunks = []
        rest = list(outs)
        while rest:
            swapped = len(rest[0].shape) == 4
            refs = rest[: 1 if swapped else 4]
            rest = rest[len(refs) :]
            chunks.append((refs, refs[0].shape[1 if swapped else 0]))
        deep = sum(count for _, count in chunks)
        for bits in range(4):
            there = me_ref[0] ^ bits
            for low in range(0, deep, TILE):
                start = pl.multiple_of(there * deep + low, TILE)
                tile = turn(turn_ref[...], held[:, pl.ds(start, TILE), :])
                begin = 0
                for refs, count in chunks:
                    least, most = max(begin, low), min(begin + count, low + TILE)
                    if least < most:
                        target = refs[0].at[there] if len(refs) == 1 else refs[bits]
                        target[least - begin : most - begin] = tile[least - low : most - low]
                    begin += count


def first_call(me, matrix, attended, w_out, masked, w_first_t, chunks):
    blocks, size, _ = w_first_t.shape
    rows, genes = masked.shape
    width = w_out.shape[0]
    group = several(TILE)
    steps = TILE // group
    wide = spec((rows, group * size), lambda b, _: (0, b))
    outs, places = [array((rows, genes), BF16)], [wide]
    for deep, swapped in chunks:
        if swapped:
            outs.append(array((4, deep, blocks, rows), BF16))
            places.append(spec((4, deep, TILE, rows), lambda b, _: (0, 0, b // steps, 0)))
        else:
            outs += [array((deep, blocks, rows), BF16)] * 4
            places += [spec((deep, TILE, rows), lambda b, _: (0, b // steps, 0))] * 4
    hidden, *first = call(
        first_kernel,
        me,
        (matrix, *attended, w_out, masked, w_first_t),
        [whole(matrix.shape)]
        + [whole(part.shape) for part in attended]
        + [
            spec((width, group * size), lambda b, _: (0, b)),
            wide,
            spec((group, size, size), lambda b, _: (b, 0, 0)),
        ],
        outs,
        places,
        grid=(blocks // group,),
        scratch=[pltpu.VMEM((rows, width), BF16), pltpu.VMEM((TILE, size, rows), BF16)],
    )
    taken = []
    for _, swapped in chunks:
        wanted = 1 if swapped else 4
        taken.append(first[:wanted])
        first = first[wanted:]
    return hidden, taken


def second_kernel(me_ref, *refs):
    pieces = refs[: 1 if len(refs[0].shape) == 4 else 4]
    w_ref, cot_ref, hidden_ref = refs[len(pieces) : len(pieces) + 3]
    out_ref, *send_ref, keep_ref, square, held = refs[-6:]
    group, size, _ = w_ref.shape
    pair = held.shape[1]
    for g in range(group):
        at = slice(g * size, (g + 1) * size)
        mine = slice(g * pair, (g + 1) * pair)
        if len(pieces) == 1:
            for source in range(4):
                held[g, :, source] = pieces[0][source, mine]
        else:
            for bits in range(4):
                held[g, :, me_ref[0] ^ bits] = pieces[bits][mine]
        permuted = held[g].reshape(size, held.shape[4])
        square[g] = jnp.dot(permuted, cot_ref[:, at], preferred_element_type=F32)
        store_quarters(me_ref[1], g, square.at[g], send_ref, keep_ref)
        mixed = lax.dot_general(
            permuted, w_ref[g], (((0,), (0,)), ((), ())), preferred_element_type=F32
        )
        out_ref[:, at] = (hidden_ref[:, at].astype(F32) + mixed).astype(BF16)


def second_call(me, pieces, w_second, cotangent, hidden, denoised, start, low, count):
    blocks, size, _ = w_second.shape
    rows = hidden.shape[0]
    pair = size // (4 * blocks)
    group = several(math.gcd(count, start, low))
    begin, low = start // group, low // group
    wide = spec((rows, group * size), lambda j, _: (0, begin + j))
    square = spec((group, size, size), lambda j, _: (begin + j, 0, 0))
    args = [*pieces, w_second, cotangent, hidden]
    part = (group * pair, blocks, rows)
    if len(pieces) == 1:
        in_specs = [spec((4, *part), lambda j, _: (0, low + j, 0, 0))]
    else:
        in_specs = [spec(part, lambda j, _: (low + j, 0, 0))] * 4
    in_specs += [square, wide, wide]
    quarters = quarter_outs(count, group, size)
    aliases = {}
    if denoised is not None:
        args.append(denoised)
        in_specs.append(pl.BlockSpec(memory_space=pl.ANY))
        aliases = {len(args): 0}
    return call(
        second_kernel,
        me,
        args,
        in_specs,
        [array(hidden.shape, BF16), *quarters[0]],
        [wide, *quarters[1]],
        grid=(count // group,),
        scratch=[
            pltpu.VMEM((group, size, size), F32),
            pltpu.VMEM((group, pair, 4, blocks, rows), BF16),
        ],
        aliases=aliases,
    )


def grad_first_kernel(me_ref, *refs):
    pieces, (hidden_ref, *send_ref, keep_ref, held, square) = refs[:-6], refs[-6:]
    group, size, _ = square.shape
    for g in range(group):
        low = 0
        for part in range(0, len(pieces), 4):
            deep = pieces[part].shape[1]
            for bits in range(4):
                held[g, me_ref[0] ^ bits, low : low + deep] = pieces[part + bits][g]
            low += deep
        back = held[g].reshape(size, held.shape[3])
        hidden = hidden_ref[:, g * size : (g + 1) * size]
        square[g] = jnp.dot(back, hidden, preferred_element_type=F32).T
        store_quarters(me_ref[1], g, square.at[g], send_ref, keep_ref)


def grad_first_call(me, pieces, hidden, size, start, count):
    rows = hidden.shape[0]
    group = several(math.gcd(count, start) if start else count)
    begin = start // group
    return call(
        grad_first_kernel,
        me,
        (*pieces, hidden),
        [spec((group, *piece.shape[1:]), lambda b, _: (begin + b, 0, 0)) for piece in pieces]
        + [spec((rows, group * size), lambda b, _: (0, begin + b))],
        *quarter_outs(count, group, size),
        grid=(count // group,),
        scratch=[
            pltpu.VMEM((group, 4, size // 4, rows), BF16),
            pltpu.VMEM((group, size, size), F32),
        ],
    )


def on_device_four(expression, gene_mask, mask_value, w_qkv, w_out, w_first, w_second, cotangent):
    me = jnp.stack([lax.axis_index("gene"), lax.axis_index("cell")]).astype(jnp.int32)
    blocks, size, _ = w_first.shape
    deep = size // 4
    counts = [blocks // 4, blocks // 2, blocks // 4]
    chunks = [(3 * deep // 4, True), (deep // 4, True)]
    matrix = grid_turn()
    sends, back = [None] * 3, [[None] * 4 for _ in range(3)]

    def prepare(part, *earlier):
        sends[part] = back_call(
            me, matrix, w_second, after(cotangent, *earlier), sum(counts[:part]), counts[part]
        )
        back[part][0] = sends[part][0]

    def begin(part, bits, *earlier):
        back[part][bits] = flip(after(sends[part][bits], *earlier), "gene", bits)
        return back[part][bits]

    prepare(0)
    beside_qkv = [begin(0, bits) for bits in (3, 2, 1)]
    prepare(1, sends[0][0])
    masked, send, keep = project_call(
        me, after(expression, sends[1][0]), gene_mask, mask_value, w_qkv
    )
    came = flip(after(send, *beside_qkv), "gene", 1)
    beside_sum = begin(1, 3, send, *beside_qkv)
    prepare(2, send)
    w_first_t = jnp.swapaxes(after(w_first, send), 1, 2)
    mine, other = add_call(me, keep, after(came, sends[2][0], w_first_t))
    last = flip(other, "gene", 2)
    queries, *own = split_call(me, mine, after(last, beside_sum, begin(2, 1, other)))
    across = [flip(piece, "cell", 2) for piece in own]
    beside = [flip(piece, "cell", 1) for piece in own]
    corner = [flip(piece, "cell", 1) for piece in across]
    beside_keys = [begin(1, bits, last, beside_sum) for bits in (2, 1)]
    gathered = [piece for kind in zip(own, beside, across, corner) for piece in kind]
    attended = attend_call(me, queries, gathered)
    near = flip(attended, "gene", 1)
    far = flip(attended, "gene", 2)
    rest = flip(after(far, near, *beside_keys), "gene", 1)
    begin(2, 2, attended)
    hidden, first = first_call(
        me, matrix, (attended, near, far, rest), w_out, masked, w_first_t, chunks
    )
    begin(2, 3, rest)

    got = []

    def launch(t, *earlier):
        pieces = after(first[t], *earlier)
        if chunks[t][1]:
            got.append([lax.all_to_all(pieces[0], "gene", split_axis=0, concat_axis=0, tiled=True)])
        else:
            got.append([pieces[0]] + [flip(pieces[bits], "gene", bits) for bits in (1, 2, 3)])

    launch(0, *back[2][2:])
    denoised, shares = None, [None, None]
    back = sum(back, [])

    def sum_cells(which, start, send, keep):
        came = [flip(piece, "cell", 1) for piece in send]
        mine, other = pair_call(me, keep, came)
        last = flip(other, "cell", 2)
        shares[which] = finish_call(me, mine, last, shares[which], start, blocks)

    *send, keep = grad_first_call(me, back, hidden, size, 0, blocks // 2)
    *send_next, keep_next = grad_first_call(me, back, hidden, size, blocks // 2, blocks // 2)
    sum_cells(0, 0, send, keep)
    sum_cells(0, blocks // 2, send_next, keep_next)
    pin = shares[0]
    for t in range(len(chunks)):
        if t + 1 < len(chunks):
            launch(t + 1, *got[t], pin)
        start, count = (n * blocks // deep for n in (sum(n for n, _ in chunks[:t]), chunks[t][0]))
        pieces = got[t] if t + 1 < len(chunks) else after(got[t], pin)
        calls = 2 if t == len(chunks) - 1 else 1
        count //= calls
        for low in range(0, calls * count, count):
            denoised, *send, keep = second_call(
                me, pieces, w_second, cotangent, hidden, denoised, start + low, low, count
            )
            sum_cells(1, start + low, send, keep)
        pin = shares[1]
    return (denoised, *shares)


def solution(mesh):
    placed = (
        P(("grp", "cell"), "gene"),
        P(("grp", "cell"), "gene"),
        P("gene"),
        P("gene", None),
        P(None, "gene"),
        P("gene", None, None),
        P("gene", None, None),
        P(("grp", "cell"), "gene"),
    )
    four = mesh.shape["gene"] == 4 and mesh.shape["cell"] == 4
    return jax.shard_map(
        on_device_four if four else on_device_general,
        mesh=mesh,
        in_specs=placed,
        out_specs=(
            P(("grp", "cell"), "gene"),
            P(("grp", "gene"), "cell", None),
            P(("grp", "gene"), "cell", None),
        ),
        check_vma=False,
    )
```

```python
import math

import jax
import jax.numpy as jnp
from jax import lax
from jax.experimental import pallas as pl
from jax.experimental.pallas import tpu as pltpu
from jax.sharding import PartitionSpec as P

HEADS = 16
HEAD_DIM = 64
TILE = 16
BF16 = jnp.bfloat16
F32 = jnp.float32


def normalize(part):
    count, columns = part.shape
    shaped = part.reshape(count, columns // HEAD_DIM, HEAD_DIM)
    meansq = jnp.mean(shaped * shaped, axis=-1, keepdims=True)
    return (shaped * lax.rsqrt(meansq + 1e-06)).astype(BF16).reshape(count, columns)


def attend(queries, key_piece, value_piece):
    query_count, columns = queries.shape
    key_count = key_piece.shape[0]
    heads = columns // HEAD_DIM
    query_heads = queries.reshape(query_count, heads, HEAD_DIM)
    key_heads = key_piece.reshape(key_count, heads, HEAD_DIM)
    value_heads = value_piece.reshape(key_count, heads, HEAD_DIM)
    scores = jnp.einsum(
        "qhd,khd->hqk", query_heads, key_heads, preferred_element_type=F32
    ) * HEAD_DIM ** (-0.5)
    expw = jnp.exp(scores).astype(BF16)
    denom = jnp.sum(expw, axis=2, dtype=F32)
    numer = jnp.einsum("hqk,khd->qhd", expw, value_heads, preferred_element_type=F32)
    return (numer / denom.T[:, :, None]).astype(BF16).reshape(query_count, columns)


def on_device_general(
    expression, gene_mask, mask_value, w_qkv, w_out, w_first, w_second, cotangent
):
    groups = lax.axis_size("gene")
    local_blocks = w_first.shape[0]
    block_size = w_first.shape[1]
    block_total = local_blocks * groups
    cell_rows = expression.shape[0]
    masked_in = jnp.where(gene_mask == 1, mask_value[None, :], expression)
    qkv_part = jnp.dot(masked_in, w_qkv, preferred_element_type=F32)
    qkv_full = lax.psum(qkv_part.astype(BF16), "gene").astype(F32)
    columns = qkv_full.shape[1] // 3
    queries = normalize(qkv_full[:, :columns])
    keys_normed = normalize(qkv_full[:, columns : 2 * columns])
    values_b = qkv_full[:, 2 * columns :].astype(BF16)
    attended = attend(
        queries,
        lax.all_gather(keys_normed, "cell", axis=0, tiled=True),
        lax.all_gather(values_b, "cell", axis=0, tiled=True),
    )
    added = jnp.dot(attended, w_out, preferred_element_type=F32)
    hidden = (masked_in.astype(F32) + added).astype(BF16)
    blocks = hidden.reshape(cell_rows, local_blocks, block_size)
    first = jnp.einsum("cbi,bio->cbo", blocks, w_first, preferred_element_type=F32).astype(BF16)
    cot_blocks = cotangent.reshape(cell_rows, local_blocks, block_size)
    back_perm = jnp.einsum(
        "cjo,jko->cjk", cot_blocks, w_second, preferred_element_type=F32
    ).astype(BF16)
    back_send = back_perm.reshape(cell_rows, block_size // groups, block_total)
    received = lax.all_to_all(first, "gene", split_axis=2, concat_axis=1, tiled=True)
    permuted = jnp.swapaxes(received, 1, 2).reshape(cell_rows, local_blocks, block_size)
    mixed = jnp.einsum("cjk,jko->cjo", permuted, w_second, preferred_element_type=F32)
    denoised = (
        (blocks.astype(F32) + mixed).astype(BF16).reshape(cell_rows, local_blocks * block_size)
    )
    grad_second = jnp.einsum("cjk,cjo->jko", permuted, cot_blocks, preferred_element_type=F32)
    back_recv = lax.all_to_all(back_send, "gene", split_axis=2, concat_axis=1, tiled=True)
    back_first = jnp.swapaxes(back_recv, 1, 2)
    grad_first = jnp.einsum("cbi,cbo->bio", blocks, back_first, preferred_element_type=F32)
    first_share, second_share = (
        lax.psum_scatter(
            grad_first.astype(BF16), "cell", scatter_dimension=1, tiled=True
        ).astype(F32),
        lax.psum_scatter(
            grad_second.astype(BF16), "cell", scatter_dimension=1, tiled=True
        ).astype(F32),
    )
    return (denoised, first_share, second_share)


def after(value, *earlier):
    return lax.optimization_barrier((value, *earlier))[0]


def flip(value, axis, bit):
    pairs = [(i, i ^ bit) for i in range(lax.axis_size(axis))]
    return lax.ppermute(value, axis, pairs)


def call(
    body, me, args, in_specs, outs, out_specs, grid=(1,), scratch=(), aliases=None, flops=1
):
    return pl.pallas_call(
        body,
        out_shape=outs,
        grid_spec=pltpu.PrefetchScalarGridSpec(
            num_scalar_prefetch=1,
            grid=grid,
            in_specs=in_specs,
            out_specs=out_specs,
            scratch_shapes=list(scratch),
        ),
        input_output_aliases=aliases or {},
        compiler_params=pltpu.CompilerParams(vmem_limit_bytes=52 * 2**20),
        cost_estimate=pl.CostEstimate(flops=flops, bytes_accessed=1, transcendentals=0),
    )(me, *args)


def spec(shape, place):
    return pl.BlockSpec(shape, place)


def whole(shape):
    return pl.BlockSpec(shape, lambda *_: (0,) * len(shape))


def several(count):
    return next(group for group in (4, 2, 1) if count % group == 0)


def array(shape, dtype):
    return jax.ShapeDtypeStruct(shape, dtype)


def grid_turn():
    rows = lax.broadcasted_iota(jnp.int32, (TILE * TILE, TILE * TILE), 0)
    columns = lax.broadcasted_iota(jnp.int32, (TILE * TILE, TILE * TILE), 1)
    return ((rows % TILE) * TILE + rows // TILE == columns).astype(BF16)


def turn(matrix, tile):
    rows = tile.shape[-1]
    flat = tile.reshape(TILE * TILE, rows)
    return jnp.dot(matrix, flat, preferred_element_type=F32).astype(BF16).reshape(TILE, TILE, rows)


def back_kernel(me_ref, turn_ref, second_ref, cot_ref, *refs):
    outs, held = refs[:4], refs[4]
    blocks, rows = held.shape[2], held.shape[3]
    group, size, _ = second_ref.shape
    pair = size // (4 * blocks)
    steps = TILE // (pair * group)
    at = pl.program_id(0) % steps
    for g in range(group):
        back = lax.dot_general(
            second_ref[g],
            cot_ref[:, g * size : (g + 1) * size],
            (((1,), (1,)), ((), ())),
            preferred_element_type=F32,
        ).astype(BF16)
        held[pl.ds((at * group + g) * pair, pair)] = back.reshape(pair, 4, blocks, rows)

    @pl.when(at == steps - 1)
    def _():
        for bits in range(4):
            there = me_ref[0] ^ bits
            for low in range(0, blocks, TILE):
                outs[bits][low : low + TILE] = turn(
                    turn_ref[...], held[:, there, low : low + TILE, :]
                )


def back_call(me, matrix, w_second, cotangent, start, count):
    blocks, size, _ = w_second.shape
    rows = cotangent.shape[0]
    pair = size // (4 * blocks)
    group = several(math.gcd(count, TILE // pair))
    steps = TILE // (pair * group)
    first = start // group
    piece = array((blocks, count * pair, rows), BF16)
    return call(
        back_kernel,
        me,
        (matrix, w_second, cotangent),
        [
            whole(matrix.shape),
            spec((group, size, size), lambda j, _: (first + j, 0, 0)),
            spec((rows, group * size), lambda j, _: (0, first + j)),
        ],
        [piece] * 4,
        [spec((blocks, TILE, rows), lambda j, _: (0, j // steps, 0))] * 4,
        grid=(count // group,),
        scratch=[pltpu.VMEM((TILE, 4, blocks, rows), BF16)],
    )


def project_kernel(me_ref, value_ref, mask_ref, fill_ref, weight_ref, *refs):
    masked_ref, send_ref, keep_ref, total = refs
    step = pl.program_id(0)
    masked = jnp.where(
        mask_ref[...] == 1, fill_ref[...].astype(F32), value_ref[...].astype(F32)
    ).astype(BF16)
    masked_ref[...] = masked
    width = total.shape[1] // 3

    @pl.when(step == 0)
    def _():
        total[...] = jnp.dot(masked, weight_ref[...], preferred_element_type=F32)

    @pl.when(step > 0)
    def _():
        total[...] += jnp.dot(masked, weight_ref[...], preferred_element_type=F32)

    @pl.when(step == pl.num_programs(0) - 1)
    def _():
        share = width // 4
        for out, flips in ((send_ref, (1, 3)), (keep_ref, (0, 2))):
            for slot, bits in enumerate(flips):
                for kind in range(3):
                    place = pl.multiple_of(kind * width + (me_ref[0] ^ bits) * share, share)
                    out[slot, :, kind * share : (kind + 1) * share] = total[
                        :, pl.ds(place, share)
                    ].astype(out.dtype)


def project_call(me, expression, gene_mask, mask_value, w_qkv):
    rows, genes = expression.shape
    width = w_qkv.shape[1]
    depth = min(genes, 1024)
    wide = spec((rows, depth), lambda i, _: (0, i))
    shape = (2, rows, width // 4)
    return call(
        project_kernel,
        me,
        (expression, gene_mask, mask_value.reshape(1, genes), w_qkv),
        [
            wide,
            wide,
            spec((1, depth), lambda i, _: (0, i)),
            spec((depth, width), lambda i, _: (i, 0)),
        ],
        [array((rows, genes), BF16), array(shape, BF16), array(shape, F32)],
        [wide, whole(shape), whole(shape)],
        grid=(genes // depth,),
        scratch=[pltpu.VMEM((rows, width), F32)],
    )


def store_quarters(me, at, held, send_ref, keep_ref):
    quarter = held.shape[0] // 4
    for bits in range(4):
        start = pl.multiple_of((me ^ bits) * quarter, quarter)
        part = held[pl.ds(start, quarter), :]
        if bits % 2:
            send_ref[bits // 2][at] = part.astype(BF16)
        else:
            keep_ref[bits // 2, at] = part


def quarter_outs(count, group, size):
    shape = (count, size // 4, size)
    one = spec((group, *shape[1:]), lambda j, _: (j, 0, 0))
    two = spec((2, group, *shape[1:]), lambda j, _: (0, j, 0, 0))
    return [array(shape, BF16)] * 2 + [array((2, *shape), F32)], [one, one, two]


def add_kernel(_, keep_ref, came_ref, mine_ref, other_ref):
    mine_ref[...] = keep_ref[0] + came_ref[0].astype(F32)
    other_ref[...] = (keep_ref[1] + came_ref[1].astype(F32)).astype(BF16)


def add_call(me, keep, came):
    shape = keep.shape
    return call(
        add_kernel,
        me,
        (keep, came),
        [whole(shape), whole(shape)],
        [array(shape[1:], F32), array(shape[1:], BF16)],
        [whole(shape[1:])] * 2,
    )


def normalize_heads(part):
    columns = part.shape[1]
    heads = [lax.broadcasted_iota(jnp.int32, (columns, columns), d) // HEAD_DIM for d in (0, 1)]
    same = (heads[0] == heads[1]).astype(F32)
    sums = jnp.dot(
        part * part, same, precision=lax.Precision.HIGHEST, preferred_element_type=F32
    )
    return (part * lax.rsqrt(sums * (1.0 / HEAD_DIM) + 1e-06)).astype(BF16)


def pair_kernel(_, keep_ref, came_ref, next_ref, mine_ref, other_ref):
    mine_ref[...] = keep_ref[0] + came_ref[...].astype(F32)
    other_ref[...] = (keep_ref[1] + next_ref[...].astype(F32)).astype(BF16)


def pair_call(me, keep, came):
    shape = keep.shape[1:]
    return call(
        pair_kernel,
        me,
        (keep, *came),
        [whole(keep.shape), whole(shape), whole(shape)],
        [array(shape, F32), array(shape, BF16)],
        [whole(shape)] * 2,
    )


def finish_kernel(_, mine_ref, came_ref, *refs):
    refs[-1][...] = mine_ref[...] + came_ref[...].astype(F32)


def finish_call(me, mine, came, total, start, blocks):
    count, quarter, size = mine.shape
    step = math.gcd(count, start) if start else count
    args = [mine, came]
    in_specs = [spec((step, quarter, size), lambda i, _: (i, 0, 0))] * 2
    aliases = {}
    if total is not None:
        args.append(total)
        in_specs.append(pl.BlockSpec(memory_space=pl.ANY))
        aliases = {len(args): 0}
    return call(
        finish_kernel,
        me,
        args,
        in_specs,
        array((blocks, quarter, size), F32),
        spec((step, quarter, size), lambda i, _: (start // step + i, 0, 0)),
        grid=(count // step,),
        aliases=aliases,
    )


def split_kernel(_, mine_ref, came_ref, query_ref, key_ref, value_ref):
    total = mine_ref[...] + came_ref[...].astype(F32)
    share = total.shape[1] // 3
    query_ref[...] = normalize_heads(total[:, :share])
    key_ref[...] = normalize_heads(total[:, share : 2 * share])
    value_ref[...] = total[:, 2 * share :].astype(BF16)


def split_call(me, mine, came):
    rows, columns = mine.shape
    shapes = ((rows, columns // 3),) * 3
    return call(
        split_kernel,
        me,
        (mine, came),
        [whole(mine.shape)] * 2,
        [array(shape, BF16) for shape in shapes],
        [whole(shape) for shape in shapes],
    )


def attend_kernel(_, query_ref, *refs):
    count = len(refs) // 2
    keys, values, out_ref = refs[:count], refs[count:-1], refs[-1]
    queries = query_ref[...]
    rows, share = queries.shape
    head_of = lax.broadcasted_iota(jnp.int32, (rows, share), 1) // HEAD_DIM
    out = jnp.zeros((rows, share), F32)
    for head in range(share // HEAD_DIM):
        query = jnp.where(head_of == head, queries.astype(F32) * HEAD_DIM**-0.5, 0.0).astype(BF16)
        numer = jnp.zeros((rows, share), F32)
        denom = jnp.zeros((rows, 1), F32)
        for key, value in zip(keys, values):
            scores = lax.dot_general(
                query, key[...], (((1,), (1,)), ((), ())), preferred_element_type=F32
            )
            expw = jnp.exp(scores).astype(BF16)
            denom += jnp.sum(expw.astype(F32), axis=1, keepdims=True)
            numer += jnp.dot(expw, value[...], preferred_element_type=F32)
        out = jnp.where(head_of == head, numer / denom, out)
    out_ref[...] = out.astype(BF16)


def attend_call(me, queries, pieces):
    rows, share = queries.shape
    some = rows // 2
    part = spec((some, share), lambda i, _: (i, 0))
    return call(
        attend_kernel,
        me,
        (queries, *pieces),
        [part] + [whole(piece.shape) for piece in pieces],
        array((rows, share), BF16),
        part,
        grid=(2,),
    )


def first_kernel(me_ref, turn_ref, own, near, far, rest, w_out_ref, masked_ref, wf_ref, *refs):
    hidden_ref, outs, gathered, held = refs[0], refs[1:-2], refs[-2], refs[-1]
    step = pl.program_id(0)
    share = own.shape[1]
    group, size, _ = wf_ref.shape
    steps = TILE // group

    @pl.when(step == 0)
    def _():
        for bits, piece in enumerate((own, near, far, rest)):
            place = pl.multiple_of((me_ref[0] ^ bits) * share, share)
            gathered[:, pl.ds(place, share)] = piece[...]

    added = jnp.dot(gathered[...], w_out_ref[...], preferred_element_type=F32)
    hidden = (masked_ref[...].astype(F32) + added).astype(BF16)
    hidden_ref[...] = hidden
    for g in range(group):
        held[step % steps * group + g] = lax.dot_general(
            wf_ref[g],
            hidden[:, g * size : (g + 1) * size],
            (((1,), (1,)), ((), ())),
            preferred_element_type=F32,
        ).astype(BF16)

    @pl.when(step % steps == steps - 1)
    def _():
        chunks = []
        rest = list(outs)
        while rest:
            swapped = len(rest[0].shape) == 4
            refs = rest[: 1 if swapped else 4]
            rest = rest[len(refs) :]
            chunks.append((refs, refs[0].shape[1 if swapped else 0]))
        deep = sum(count for _, count in chunks)
        for bits in range(4):
            there = me_ref[0] ^ bits
            for low in range(0, deep, TILE):
                start = pl.multiple_of(there * deep + low, TILE)
                tile = turn(turn_ref[...], held[:, pl.ds(start, TILE), :])
                begin = 0
                for refs, count in chunks:
                    least, most = max(begin, low), min(begin + count, low + TILE)
                    if least < most:
                        target = refs[0].at[there] if len(refs) == 1 else refs[bits]
                        target[least - begin : most - begin] = tile[least - low : most - low]
                    begin += count


def first_call(me, matrix, attended, w_out, masked, w_first_t, chunks):
    blocks, size, _ = w_first_t.shape
    rows, genes = masked.shape
    width = w_out.shape[0]
    group = several(TILE)
    steps = TILE // group
    wide = spec((rows, group * size), lambda b, _: (0, b))
    outs, places = [array((rows, genes), BF16)], [wide]
    for deep, swapped in chunks:
        if swapped:
            outs.append(array((4, deep, blocks, rows), BF16))
            places.append(spec((4, deep, TILE, rows), lambda b, _: (0, 0, b // steps, 0)))
        else:
            outs += [array((deep, blocks, rows), BF16)] * 4
            places += [spec((deep, TILE, rows), lambda b, _: (0, b // steps, 0))] * 4
    hidden, *first = call(
        first_kernel,
        me,
        (matrix, *attended, w_out, masked, w_first_t),
        [whole(matrix.shape)]
        + [whole(part.shape) for part in attended]
        + [
            spec((width, group * size), lambda b, _: (0, b)),
            wide,
            spec((group, size, size), lambda b, _: (b, 0, 0)),
        ],
        outs,
        places,
        grid=(blocks // group,),
        scratch=[pltpu.VMEM((rows, width), BF16), pltpu.VMEM((TILE, size, rows), BF16)],
    )
    taken = []
    for _, swapped in chunks:
        wanted = 1 if swapped else 4
        taken.append(first[:wanted])
        first = first[wanted:]
    return hidden, taken


def second_kernel(me_ref, *refs):
    pieces = refs[: 1 if len(refs[0].shape) == 4 else 4]
    w_ref, cot_ref, hidden_ref = refs[len(pieces) : len(pieces) + 3]
    out_ref, *send_ref, keep_ref, square, held = refs[-6:]
    group, size, _ = w_ref.shape
    pair = held.shape[1]
    for g in range(group):
        at = slice(g * size, (g + 1) * size)
        mine = slice(g * pair, (g + 1) * pair)
        if len(pieces) == 1:
            for source in range(4):
                held[g, :, source] = pieces[0][source, mine]
        else:
            for bits in range(4):
                held[g, :, me_ref[0] ^ bits] = pieces[bits][mine]
        permuted = held[g].reshape(size, held.shape[4])
        square[g] = jnp.dot(permuted, cot_ref[:, at], preferred_element_type=F32)
        store_quarters(me_ref[1], g, square.at[g], send_ref, keep_ref)
        mixed = lax.dot_general(
            permuted, w_ref[g], (((0,), (0,)), ((), ())), preferred_element_type=F32
        )
        out_ref[:, at] = (hidden_ref[:, at].astype(F32) + mixed).astype(BF16)


def second_call(me, pieces, w_second, cotangent, hidden, denoised, start, low, count):
    blocks, size, _ = w_second.shape
    rows = hidden.shape[0]
    pair = size // (4 * blocks)
    group = several(math.gcd(count, start, low))
    begin, low = start // group, low // group
    wide = spec((rows, group * size), lambda j, _: (0, begin + j))
    square = spec((group, size, size), lambda j, _: (begin + j, 0, 0))
    args = [*pieces, w_second, cotangent, hidden]
    part = (group * pair, blocks, rows)
    if len(pieces) == 1:
        in_specs = [spec((4, *part), lambda j, _: (0, low + j, 0, 0))]
    else:
        in_specs = [spec(part, lambda j, _: (low + j, 0, 0))] * 4
    in_specs += [square, wide, wide]
    quarters = quarter_outs(count, group, size)
    aliases = {}
    if denoised is not None:
        args.append(denoised)
        in_specs.append(pl.BlockSpec(memory_space=pl.ANY))
        aliases = {len(args): 0}
    return call(
        second_kernel,
        me,
        args,
        in_specs,
        [array(hidden.shape, BF16), *quarters[0]],
        [wide, *quarters[1]],
        grid=(count // group,),
        scratch=[
            pltpu.VMEM((group, size, size), F32),
            pltpu.VMEM((group, pair, 4, blocks, rows), BF16),
        ],
        aliases=aliases,
    )


def grad_first_kernel(me_ref, *refs):
    pieces, (hidden_ref, *send_ref, keep_ref, held, square) = refs[:-6], refs[-6:]
    group, size, _ = square.shape
    for g in range(group):
        low = 0
        for part in range(0, len(pieces), 4):
            deep = pieces[part].shape[1]
            for bits in range(4):
                held[g, me_ref[0] ^ bits, low : low + deep] = pieces[part + bits][g]
            low += deep
        back = held[g].reshape(size, held.shape[3])
        hidden = hidden_ref[:, g * size : (g + 1) * size]
        square[g] = jnp.dot(back, hidden, preferred_element_type=F32).T
        store_quarters(me_ref[1], g, square.at[g], send_ref, keep_ref)


def grad_first_call(me, pieces, hidden, size, start, count):
    rows = hidden.shape[0]
    group = several(math.gcd(count, start) if start else count)
    begin = start // group
    return call(
        grad_first_kernel,
        me,
        (*pieces, hidden),
        [spec((group, *piece.shape[1:]), lambda b, _: (begin + b, 0, 0)) for piece in pieces]
        + [spec((rows, group * size), lambda b, _: (0, begin + b))],
        *quarter_outs(count, group, size),
        grid=(count // group,),
        scratch=[
            pltpu.VMEM((group, 4, size // 4, rows), BF16),
            pltpu.VMEM((group, size, size), F32),
        ],
        flops=200 * 2 * count * size * size * rows,
    )


def on_device_four(expression, gene_mask, mask_value, w_qkv, w_out, w_first, w_second, cotangent):
    me = jnp.stack([lax.axis_index("gene"), lax.axis_index("cell")]).astype(jnp.int32)
    blocks, size, _ = w_first.shape
    deep = size // 4
    counts = [blocks // 4, blocks // 2, blocks // 4]
    chunks = [(3 * deep // 4, True), (deep // 4, True)]
    matrix = grid_turn()
    sends, back = [None] * 3, [[None] * 4 for _ in range(3)]

    def prepare(part, *earlier):
        sends[part] = back_call(
            me, matrix, w_second, after(cotangent, *earlier), sum(counts[:part]), counts[part]
        )
        back[part][0] = sends[part][0]

    def begin(part, bits, *earlier):
        back[part][bits] = flip(after(sends[part][bits], *earlier), "gene", bits)
        return back[part][bits]

    prepare(0)
    beside_qkv = [begin(0, bits) for bits in (3, 2, 1)]
    prepare(1, sends[0][0])
    masked, send, keep = project_call(
        me, after(expression, sends[1][0]), gene_mask, mask_value, w_qkv
    )
    came = flip(after(send, *beside_qkv), "gene", 1)
    beside_sum = begin(1, 3, send, *beside_qkv)
    prepare(2, send)
    w_first_t = jnp.swapaxes(after(w_first, send), 1, 2)
    mine, other = add_call(me, keep, after(came, sends[2][0], w_first_t))
    last = flip(other, "gene", 2)
    queries, *own = split_call(me, mine, after(last, beside_sum))
    across = [flip(piece, "cell", 2) for piece in own]
    beside = [flip(piece, "cell", 1) for piece in own]
    corner = [flip(piece, "cell", 1) for piece in across]
    beside_keys = [begin(1, bits, last, beside_sum) for bits in (2, 1)]
    gathered = [piece for kind in zip(own, beside, across, corner) for piece in kind]
    attended = attend_call(me, queries, gathered)
    near = flip(attended, "gene", 1)
    far = flip(attended, "gene", 2)
    rest = flip(after(far, near, *beside_keys), "gene", 1)
    begin(2, 2, attended)
    hidden, first = first_call(
        me, matrix, (attended, near, far, rest), w_out, masked, w_first_t, chunks
    )
    begin(2, 3, rest)
    begin(2, 1, rest)

    got = []

    def launch(t, *earlier):
        pieces = after(first[t], *earlier)
        if chunks[t][1]:
            got.append([lax.all_to_all(pieces[0], "gene", split_axis=0, concat_axis=0, tiled=True)])
        else:
            got.append([pieces[0]] + [flip(pieces[bits], "gene", bits) for bits in (1, 2, 3)])

    launch(0)
    denoised, shares = None, [None, None]
    back = sum(back, [])

    def sum_cells(which, start, send, keep):
        came = [flip(piece, "cell", 1) for piece in send]
        mine, other = pair_call(me, keep, came)
        last = flip(other, "cell", 2)
        shares[which] = finish_call(me, mine, last, shares[which], start, blocks)

    *send, keep = grad_first_call(me, back, hidden, size, 0, blocks // 2)
    *send_next, keep_next = grad_first_call(me, back, hidden, size, blocks // 2, blocks // 2)
    sum_cells(0, 0, send, keep)
    sum_cells(0, blocks // 2, send_next, keep_next)
    pin = shares[0]
    for t in range(len(chunks)):
        if t + 1 < len(chunks):
            launch(t + 1, *got[t], pin)
        start, count = (n * blocks // deep for n in (sum(n for n, _ in chunks[:t]), chunks[t][0]))
        calls = 2 if t == len(chunks) - 1 else 1
        count //= calls
        for low in range(0, calls * count, count):
            denoised, *send, keep = second_call(
                me, got[t], w_second, cotangent, hidden, denoised, start + low, low, count
            )
            sum_cells(1, start + low, send, keep)
        pin = shares[1]
    return (denoised, *shares)


def solution(mesh):
    placed = (
        P(("grp", "cell"), "gene"),
        P(("grp", "cell"), "gene"),
        P("gene"),
        P("gene", None),
        P(None, "gene"),
        P("gene", None, None),
        P("gene", None, None),
        P(("grp", "cell"), "gene"),
    )
    four = mesh.shape["gene"] == 4 and mesh.shape["cell"] == 4
    return jax.shard_map(
        on_device_four if four else on_device_general,
        mesh=mesh,
        in_specs=placed,
        out_specs=(
            P(("grp", "cell"), "gene"),
            P(("grp", "gene"), "cell", None),
            P(("grp", "gene"), "cell", None),
        ),
        check_vma=False,
    )
```

```python
import math

import jax
import jax.numpy as jnp
from jax import lax
from jax.experimental import pallas as pl
from jax.experimental.pallas import tpu as pltpu
from jax.sharding import PartitionSpec as P

HEADS = 16
HEAD_DIM = 64
TILE = 16
BF16 = jnp.bfloat16
F32 = jnp.float32


def normalize(part):
    count, columns = part.shape
    shaped = part.reshape(count, columns // HEAD_DIM, HEAD_DIM)
    meansq = jnp.mean(shaped * shaped, axis=-1, keepdims=True)
    return (shaped * lax.rsqrt(meansq + 1e-06)).astype(BF16).reshape(count, columns)


def attend(queries, key_piece, value_piece):
    query_count, columns = queries.shape
    key_count = key_piece.shape[0]
    heads = columns // HEAD_DIM
    query_heads = queries.reshape(query_count, heads, HEAD_DIM)
    key_heads = key_piece.reshape(key_count, heads, HEAD_DIM)
    value_heads = value_piece.reshape(key_count, heads, HEAD_DIM)
    scores = jnp.einsum(
        "qhd,khd->hqk", query_heads, key_heads, preferred_element_type=F32
    ) * HEAD_DIM ** (-0.5)
    expw = jnp.exp(scores).astype(BF16)
    denom = jnp.sum(expw, axis=2, dtype=F32)
    numer = jnp.einsum("hqk,khd->qhd", expw, value_heads, preferred_element_type=F32)
    return (numer / denom.T[:, :, None]).astype(BF16).reshape(query_count, columns)


def on_device_general(
    expression, gene_mask, mask_value, w_qkv, w_out, w_first, w_second, cotangent
):
    groups = lax.axis_size("gene")
    local_blocks = w_first.shape[0]
    block_size = w_first.shape[1]
    block_total = local_blocks * groups
    cell_rows = expression.shape[0]
    masked_in = jnp.where(gene_mask == 1, mask_value[None, :], expression)
    qkv_part = jnp.dot(masked_in, w_qkv, preferred_element_type=F32)
    qkv_full = lax.psum(qkv_part.astype(BF16), "gene").astype(F32)
    columns = qkv_full.shape[1] // 3
    queries = normalize(qkv_full[:, :columns])
    keys_normed = normalize(qkv_full[:, columns : 2 * columns])
    values_b = qkv_full[:, 2 * columns :].astype(BF16)
    attended = attend(
        queries,
        lax.all_gather(keys_normed, "cell", axis=0, tiled=True),
        lax.all_gather(values_b, "cell", axis=0, tiled=True),
    )
    added = jnp.dot(attended, w_out, preferred_element_type=F32)
    hidden = (masked_in.astype(F32) + added).astype(BF16)
    blocks = hidden.reshape(cell_rows, local_blocks, block_size)
    first = jnp.einsum("cbi,bio->cbo", blocks, w_first, preferred_element_type=F32).astype(BF16)
    cot_blocks = cotangent.reshape(cell_rows, local_blocks, block_size)
    back_perm = jnp.einsum(
        "cjo,jko->cjk", cot_blocks, w_second, preferred_element_type=F32
    ).astype(BF16)
    back_send = back_perm.reshape(cell_rows, block_size // groups, block_total)
    received = lax.all_to_all(first, "gene", split_axis=2, concat_axis=1, tiled=True)
    permuted = jnp.swapaxes(received, 1, 2).reshape(cell_rows, local_blocks, block_size)
    mixed = jnp.einsum("cjk,jko->cjo", permuted, w_second, preferred_element_type=F32)
    denoised = (
        (blocks.astype(F32) + mixed).astype(BF16).reshape(cell_rows, local_blocks * block_size)
    )
    grad_second = jnp.einsum("cjk,cjo->jko", permuted, cot_blocks, preferred_element_type=F32)
    back_recv = lax.all_to_all(back_send, "gene", split_axis=2, concat_axis=1, tiled=True)
    back_first = jnp.swapaxes(back_recv, 1, 2)
    grad_first = jnp.einsum("cbi,cbo->bio", blocks, back_first, preferred_element_type=F32)
    first_share, second_share = (
        lax.psum_scatter(
            grad_first.astype(BF16), "cell", scatter_dimension=1, tiled=True
        ).astype(F32),
        lax.psum_scatter(
            grad_second.astype(BF16), "cell", scatter_dimension=1, tiled=True
        ).astype(F32),
    )
    return (denoised, first_share, second_share)


def after(value, *earlier):
    return lax.optimization_barrier((value, *earlier))[0]


def flip(value, axis, bit):
    pairs = [(i, i ^ bit) for i in range(lax.axis_size(axis))]
    return lax.ppermute(value, axis, pairs)


def call(
    body, me, args, in_specs, outs, out_specs, grid=(1,), scratch=(), aliases=None, flops=1
):
    return pl.pallas_call(
        body,
        out_shape=outs,
        grid_spec=pltpu.PrefetchScalarGridSpec(
            num_scalar_prefetch=1,
            grid=grid,
            in_specs=in_specs,
            out_specs=out_specs,
            scratch_shapes=list(scratch),
        ),
        input_output_aliases=aliases or {},
        compiler_params=pltpu.CompilerParams(vmem_limit_bytes=52 * 2**20),
        cost_estimate=pl.CostEstimate(flops=flops, bytes_accessed=1, transcendentals=0),
    )(me, *args)


def spec(shape, place):
    return pl.BlockSpec(shape, place)


def whole(shape):
    return pl.BlockSpec(shape, lambda *_: (0,) * len(shape))


def several(count):
    return next(group for group in (4, 2, 1) if count % group == 0)


def array(shape, dtype):
    return jax.ShapeDtypeStruct(shape, dtype)


def grid_turn():
    rows = lax.broadcasted_iota(jnp.int32, (TILE * TILE, TILE * TILE), 0)
    columns = lax.broadcasted_iota(jnp.int32, (TILE * TILE, TILE * TILE), 1)
    return ((rows % TILE) * TILE + rows // TILE == columns).astype(BF16)


def turn(matrix, tile):
    rows = tile.shape[-1]
    flat = tile.reshape(TILE * TILE, rows)
    return jnp.dot(matrix, flat, preferred_element_type=F32).astype(BF16).reshape(TILE, TILE, rows)


def back_kernel(me_ref, turn_ref, second_ref, cot_ref, *refs):
    outs, held = refs[:4], refs[4]
    blocks, rows = held.shape[2], held.shape[3]
    group, size, _ = second_ref.shape
    pair = size // (4 * blocks)
    steps = TILE // (pair * group)
    at = pl.program_id(0) % steps
    for g in range(group):
        back = lax.dot_general(
            second_ref[g],
            cot_ref[:, g * size : (g + 1) * size],
            (((1,), (1,)), ((), ())),
            preferred_element_type=F32,
        ).astype(BF16)
        held[pl.ds((at * group + g) * pair, pair)] = back.reshape(pair, 4, blocks, rows)

    @pl.when(at == steps - 1)
    def _():
        for bits in range(4):
            there = me_ref[0] ^ bits
            for low in range(0, blocks, TILE):
                outs[bits][low : low + TILE] = turn(
                    turn_ref[...], held[:, there, low : low + TILE, :]
                )


def back_call(me, matrix, w_second, cotangent, start, count):
    blocks, size, _ = w_second.shape
    rows = cotangent.shape[0]
    pair = size // (4 * blocks)
    group = several(math.gcd(count, TILE // pair))
    steps = TILE // (pair * group)
    first = start // group
    piece = array((blocks, count * pair, rows), BF16)
    return call(
        back_kernel,
        me,
        (matrix, w_second, cotangent),
        [
            whole(matrix.shape),
            spec((group, size, size), lambda j, _: (first + j, 0, 0)),
            spec((rows, group * size), lambda j, _: (0, first + j)),
        ],
        [piece] * 4,
        [spec((blocks, TILE, rows), lambda j, _: (0, j // steps, 0))] * 4,
        grid=(count // group,),
        scratch=[pltpu.VMEM((TILE, 4, blocks, rows), BF16)],
    )


def project_kernel(me_ref, value_ref, mask_ref, fill_ref, weight_ref, *refs):
    masked_ref, send_ref, keep_ref, total = refs
    step = pl.program_id(0)
    masked = jnp.where(
        mask_ref[...] == 1, fill_ref[...].astype(F32), value_ref[...].astype(F32)
    ).astype(BF16)
    masked_ref[...] = masked
    width = total.shape[1] // 3

    @pl.when(step == 0)
    def _():
        total[...] = jnp.dot(masked, weight_ref[...], preferred_element_type=F32)

    @pl.when(step > 0)
    def _():
        total[...] += jnp.dot(masked, weight_ref[...], preferred_element_type=F32)

    @pl.when(step == pl.num_programs(0) - 1)
    def _():
        share = width // 4
        for out, flips in ((send_ref, (1, 3)), (keep_ref, (0, 2))):
            for slot, bits in enumerate(flips):
                for kind in range(3):
                    place = pl.multiple_of(kind * width + (me_ref[0] ^ bits) * share, share)
                    out[slot, :, kind * share : (kind + 1) * share] = total[
                        :, pl.ds(place, share)
                    ].astype(out.dtype)


def project_call(me, expression, gene_mask, mask_value, w_qkv):
    rows, genes = expression.shape
    width = w_qkv.shape[1]
    depth = min(genes, 1024)
    wide = spec((rows, depth), lambda i, _: (0, i))
    shape = (2, rows, width // 4)
    return call(
        project_kernel,
        me,
        (expression, gene_mask, mask_value.reshape(1, genes), w_qkv),
        [
            wide,
            wide,
            spec((1, depth), lambda i, _: (0, i)),
            spec((depth, width), lambda i, _: (i, 0)),
        ],
        [array((rows, genes), BF16), array(shape, BF16), array(shape, F32)],
        [wide, whole(shape), whole(shape)],
        grid=(genes // depth,),
        scratch=[pltpu.VMEM((rows, width), F32)],
    )


def store_quarters(me, at, held, send_ref, keep_ref):
    quarter = held.shape[0] // 4
    for bits in range(4):
        start = pl.multiple_of((me ^ bits) * quarter, quarter)
        part = held[pl.ds(start, quarter), :]
        if bits % 2:
            send_ref[bits // 2][at] = part.astype(BF16)
        else:
            keep_ref[bits // 2, at] = part


def quarter_outs(count, group, size):
    shape = (count, size // 4, size)
    one = spec((group, *shape[1:]), lambda j, _: (j, 0, 0))
    two = spec((2, group, *shape[1:]), lambda j, _: (0, j, 0, 0))
    return [array(shape, BF16)] * 2 + [array((2, *shape), F32)], [one, one, two]


def add_kernel(_, keep_ref, came_ref, mine_ref, other_ref):
    mine_ref[...] = keep_ref[0] + came_ref[0].astype(F32)
    other_ref[...] = (keep_ref[1] + came_ref[1].astype(F32)).astype(BF16)


def add_call(me, keep, came):
    shape = keep.shape
    return call(
        add_kernel,
        me,
        (keep, came),
        [whole(shape), whole(shape)],
        [array(shape[1:], F32), array(shape[1:], BF16)],
        [whole(shape[1:])] * 2,
    )


def normalize_heads(part):
    columns = part.shape[1]
    heads = [lax.broadcasted_iota(jnp.int32, (columns, columns), d) // HEAD_DIM for d in (0, 1)]
    same = (heads[0] == heads[1]).astype(F32)
    sums = jnp.dot(
        part * part, same, precision=lax.Precision.HIGHEST, preferred_element_type=F32
    )
    return (part * lax.rsqrt(sums * (1.0 / HEAD_DIM) + 1e-06)).astype(BF16)


def pair_kernel(_, keep_ref, came_ref, next_ref, mine_ref, other_ref):
    mine_ref[...] = keep_ref[0] + came_ref[...].astype(F32)
    other_ref[...] = (keep_ref[1] + next_ref[...].astype(F32)).astype(BF16)


def pair_call(me, keep, came):
    shape = keep.shape[1:]
    return call(
        pair_kernel,
        me,
        (keep, *came),
        [whole(keep.shape), whole(shape), whole(shape)],
        [array(shape, F32), array(shape, BF16)],
        [whole(shape)] * 2,
    )


def finish_kernel(_, mine_ref, came_ref, *refs):
    refs[-1][...] = mine_ref[...] + came_ref[...].astype(F32)


def finish_call(me, mine, came, total, start, blocks):
    count, quarter, size = mine.shape
    step = math.gcd(count, start) if start else count
    args = [mine, came]
    in_specs = [spec((step, quarter, size), lambda i, _: (i, 0, 0))] * 2
    aliases = {}
    if total is not None:
        args.append(total)
        in_specs.append(pl.BlockSpec(memory_space=pl.ANY))
        aliases = {len(args): 0}
    return call(
        finish_kernel,
        me,
        args,
        in_specs,
        array((blocks, quarter, size), F32),
        spec((step, quarter, size), lambda i, _: (start // step + i, 0, 0)),
        grid=(count // step,),
        aliases=aliases,
    )


def split_kernel(_, mine_ref, came_ref, query_ref, key_ref, value_ref):
    total = mine_ref[...] + came_ref[...].astype(F32)
    share = total.shape[1] // 3
    query_ref[...] = normalize_heads(total[:, :share])
    key_ref[...] = normalize_heads(total[:, share : 2 * share])
    value_ref[...] = total[:, 2 * share :].astype(BF16)


def split_call(me, mine, came):
    rows, columns = mine.shape
    shapes = ((rows, columns // 3),) * 3
    return call(
        split_kernel,
        me,
        (mine, came),
        [whole(mine.shape)] * 2,
        [array(shape, BF16) for shape in shapes],
        [whole(shape) for shape in shapes],
    )


def attend_kernel(_, query_ref, *refs):
    count = len(refs) // 2
    keys, values, out_ref = refs[:count], refs[count:-1], refs[-1]
    queries = query_ref[...]
    rows, share = queries.shape
    head_of = lax.broadcasted_iota(jnp.int32, (rows, share), 1) // HEAD_DIM
    out = jnp.zeros((rows, share), F32)
    for head in range(share // HEAD_DIM):
        query = jnp.where(head_of == head, queries.astype(F32) * HEAD_DIM**-0.5, 0.0).astype(BF16)
        numer = jnp.zeros((rows, share), F32)
        denom = jnp.zeros((rows, 1), F32)
        for key, value in zip(keys, values):
            scores = lax.dot_general(
                query, key[...], (((1,), (1,)), ((), ())), preferred_element_type=F32
            )
            expw = jnp.exp(scores).astype(BF16)
            denom += jnp.sum(expw.astype(F32), axis=1, keepdims=True)
            numer += jnp.dot(expw, value[...], preferred_element_type=F32)
        out = jnp.where(head_of == head, numer / denom, out)
    out_ref[...] = out.astype(BF16)


def attend_call(me, queries, pieces):
    rows, share = queries.shape
    some = rows // 2
    part = spec((some, share), lambda i, _: (i, 0))
    return call(
        attend_kernel,
        me,
        (queries, *pieces),
        [part] + [whole(piece.shape) for piece in pieces],
        array((rows, share), BF16),
        part,
        grid=(2,),
    )


def first_kernel(me_ref, turn_ref, own, near, far, rest, w_out_ref, masked_ref, wf_ref, *refs):
    hidden_ref, outs, gathered, held = refs[0], refs[1:-2], refs[-2], refs[-1]
    step = pl.program_id(0)
    share = own.shape[1]
    group, size, _ = wf_ref.shape
    steps = TILE // group

    @pl.when(step == 0)
    def _():
        for bits, piece in enumerate((own, near, far, rest)):
            place = pl.multiple_of((me_ref[0] ^ bits) * share, share)
            gathered[:, pl.ds(place, share)] = piece[...]

    added = jnp.dot(gathered[...], w_out_ref[...], preferred_element_type=F32)
    hidden = (masked_ref[...].astype(F32) + added).astype(BF16)
    hidden_ref[...] = hidden
    for g in range(group):
        held[step % steps * group + g] = lax.dot_general(
            wf_ref[g],
            hidden[:, g * size : (g + 1) * size],
            (((1,), (1,)), ((), ())),
            preferred_element_type=F32,
        ).astype(BF16)

    @pl.when(step % steps == steps - 1)
    def _():
        chunks = []
        rest = list(outs)
        while rest:
            swapped = len(rest[0].shape) == 4
            refs = rest[: 1 if swapped else 4]
            rest = rest[len(refs) :]
            chunks.append((refs, refs[0].shape[1 if swapped else 0]))
        deep = sum(count for _, count in chunks)
        for bits in range(4):
            there = me_ref[0] ^ bits
            for low in range(0, deep, TILE):
                start = pl.multiple_of(there * deep + low, TILE)
                tile = turn(turn_ref[...], held[:, pl.ds(start, TILE), :])
                begin = 0
                for refs, count in chunks:
                    least, most = max(begin, low), min(begin + count, low + TILE)
                    if least < most:
                        target = refs[0].at[there] if len(refs) == 1 else refs[bits]
                        target[least - begin : most - begin] = tile[least - low : most - low]
                    begin += count


def first_call(me, matrix, attended, w_out, masked, w_first_t, chunks):
    blocks, size, _ = w_first_t.shape
    rows, genes = masked.shape
    width = w_out.shape[0]
    group = several(TILE)
    steps = TILE // group
    wide = spec((rows, group * size), lambda b, _: (0, b))
    outs, places = [array((rows, genes), BF16)], [wide]
    for deep, swapped in chunks:
        if swapped:
            outs.append(array((4, deep, blocks, rows), BF16))
            places.append(spec((4, deep, TILE, rows), lambda b, _: (0, 0, b // steps, 0)))
        else:
            outs += [array((deep, blocks, rows), BF16)] * 4
            places += [spec((deep, TILE, rows), lambda b, _: (0, b // steps, 0))] * 4
    hidden, *first = call(
        first_kernel,
        me,
        (matrix, *attended, w_out, masked, w_first_t),
        [whole(matrix.shape)]
        + [whole(part.shape) for part in attended]
        + [
            spec((width, group * size), lambda b, _: (0, b)),
            wide,
            spec((group, size, size), lambda b, _: (b, 0, 0)),
        ],
        outs,
        places,
        grid=(blocks // group,),
        scratch=[pltpu.VMEM((rows, width), BF16), pltpu.VMEM((TILE, size, rows), BF16)],
    )
    taken = []
    for _, swapped in chunks:
        wanted = 1 if swapped else 4
        taken.append(first[:wanted])
        first = first[wanted:]
    return hidden, taken


def second_kernel(me_ref, *refs):
    pieces = refs[: 1 if len(refs[0].shape) == 4 else 4]
    w_ref, cot_ref, hidden_ref = refs[len(pieces) : len(pieces) + 3]
    out_ref, *send_ref, keep_ref, square, held = refs[-6:]
    group, size, _ = w_ref.shape
    pair = held.shape[1]
    for g in range(group):
        at = slice(g * size, (g + 1) * size)
        mine = slice(g * pair, (g + 1) * pair)
        if len(pieces) == 1:
            for source in range(4):
                held[g, :, source] = pieces[0][source, mine]
        else:
            for bits in range(4):
                held[g, :, me_ref[0] ^ bits] = pieces[bits][mine]
        permuted = held[g].reshape(size, held.shape[4])
        square[g] = jnp.dot(permuted, cot_ref[:, at], preferred_element_type=F32)
        store_quarters(me_ref[1], g, square.at[g], send_ref, keep_ref)
        mixed = lax.dot_general(
            permuted, w_ref[g], (((0,), (0,)), ((), ())), preferred_element_type=F32
        )
        out_ref[:, at] = (hidden_ref[:, at].astype(F32) + mixed).astype(BF16)


def second_call(me, pieces, w_second, cotangent, hidden, denoised, start, low, count):
    blocks, size, _ = w_second.shape
    rows = hidden.shape[0]
    pair = size // (4 * blocks)
    group = several(math.gcd(count, start, low))
    begin, low = start // group, low // group
    wide = spec((rows, group * size), lambda j, _: (0, begin + j))
    square = spec((group, size, size), lambda j, _: (begin + j, 0, 0))
    args = [*pieces, w_second, cotangent, hidden]
    part = (group * pair, blocks, rows)
    if len(pieces) == 1:
        in_specs = [spec((4, *part), lambda j, _: (0, low + j, 0, 0))]
    else:
        in_specs = [spec(part, lambda j, _: (low + j, 0, 0))] * 4
    in_specs += [square, wide, wide]
    quarters = quarter_outs(count, group, size)
    aliases = {}
    if denoised is not None:
        args.append(denoised)
        in_specs.append(pl.BlockSpec(memory_space=pl.ANY))
        aliases = {len(args): 0}
    return call(
        second_kernel,
        me,
        args,
        in_specs,
        [array(hidden.shape, BF16), *quarters[0]],
        [wide, *quarters[1]],
        grid=(count // group,),
        scratch=[
            pltpu.VMEM((group, size, size), F32),
            pltpu.VMEM((group, pair, 4, blocks, rows), BF16),
        ],
        aliases=aliases,
    )


def grad_first_kernel(me_ref, *refs):
    pieces, (hidden_ref, *send_ref, keep_ref, held, square) = refs[:-6], refs[-6:]
    group, size, _ = square.shape
    for g in range(group):
        low = 0
        for part in range(0, len(pieces), 4):
            deep = pieces[part].shape[1]
            for bits in range(4):
                held[g, me_ref[0] ^ bits, low : low + deep] = pieces[part + bits][g]
            low += deep
        back = held[g].reshape(size, held.shape[3])
        hidden = hidden_ref[:, g * size : (g + 1) * size]
        square[g] = jnp.dot(back, hidden, preferred_element_type=F32).T
        store_quarters(me_ref[1], g, square.at[g], send_ref, keep_ref)


def grad_first_call(me, pieces, hidden, size, start, count):
    rows = hidden.shape[0]
    group = several(math.gcd(count, start) if start else count)
    begin = start // group
    return call(
        grad_first_kernel,
        me,
        (*pieces, hidden),
        [spec((group, *piece.shape[1:]), lambda b, _: (begin + b, 0, 0)) for piece in pieces]
        + [spec((rows, group * size), lambda b, _: (0, begin + b))],
        *quarter_outs(count, group, size),
        grid=(count // group,),
        scratch=[
            pltpu.VMEM((group, 4, size // 4, rows), BF16),
            pltpu.VMEM((group, size, size), F32),
        ],
        flops=200 * 2 * count * size * size * rows,
    )


def on_device_four(expression, gene_mask, mask_value, w_qkv, w_out, w_first, w_second, cotangent):
    me = jnp.stack([lax.axis_index("gene"), lax.axis_index("cell")]).astype(jnp.int32)
    blocks, size, _ = w_first.shape
    deep = size // 4
    counts = [blocks // 4, blocks // 2, blocks // 4]
    chunks = [(13 * deep // 16, True), (3 * deep // 16, True)]
    matrix = grid_turn()
    sends, back = [None] * 3, [[None] * 4 for _ in range(3)]

    def prepare(part, *earlier):
        sends[part] = back_call(
            me, matrix, w_second, after(cotangent, *earlier), sum(counts[:part]), counts[part]
        )
        back[part][0] = sends[part][0]

    def begin(part, bits, *earlier):
        back[part][bits] = flip(after(sends[part][bits], *earlier), "gene", bits)
        return back[part][bits]

    prepare(0)
    beside_qkv = [begin(0, bits) for bits in (3, 2, 1)]
    prepare(1, sends[0][0])
    masked, send, keep = project_call(
        me, after(expression, sends[1][0]), gene_mask, mask_value, w_qkv
    )
    came = flip(after(send, *beside_qkv), "gene", 1)
    beside_sum = begin(1, 3, send, *beside_qkv)
    prepare(2, send)
    w_first_t = jnp.swapaxes(after(w_first, send), 1, 2)
    mine, other = add_call(me, keep, after(came, sends[2][0], w_first_t))
    last = flip(other, "gene", 2)
    queries, *own = split_call(me, mine, after(last, beside_sum))
    across = [flip(piece, "cell", 2) for piece in own]
    beside = [flip(piece, "cell", 1) for piece in own]
    corner = [flip(piece, "cell", 1) for piece in across]
    beside_keys = [begin(1, bits, last, beside_sum) for bits in (2, 1)]
    gathered = [piece for kind in zip(own, beside, across, corner) for piece in kind]
    attended = attend_call(me, queries, gathered)
    near = flip(attended, "gene", 1)
    far = flip(attended, "gene", 2)
    rest = flip(after(far, near, *beside_keys), "gene", 1)
    begin(2, 2, attended)
    hidden, first = first_call(
        me, matrix, (attended, near, far, rest), w_out, masked, w_first_t, chunks
    )
    begin(2, 3, rest)
    begin(2, 1, rest)

    got = []

    def launch(t, *earlier):
        pieces = after(first[t], *earlier)
        if chunks[t][1]:
            got.append([lax.all_to_all(pieces[0], "gene", split_axis=0, concat_axis=0, tiled=True)])
        else:
            got.append([pieces[0]] + [flip(pieces[bits], "gene", bits) for bits in (1, 2, 3)])

    launch(0)
    denoised, shares = None, [None, None]
    back = sum(back, [])

    def sum_cells(which, start, send, keep):
        came = [flip(piece, "cell", 1) for piece in send]
        mine, other = pair_call(me, keep, came)
        last = flip(other, "cell", 2)
        shares[which] = finish_call(me, mine, last, shares[which], start, blocks)

    *send, keep = grad_first_call(me, back, hidden, size, 0, blocks // 2)
    *send_next, keep_next = grad_first_call(me, back, hidden, size, blocks // 2, blocks // 2)
    sum_cells(0, 0, send, keep)
    sum_cells(0, blocks // 2, send_next, keep_next)
    pin = shares[0]
    for t in range(len(chunks)):
        if t + 1 < len(chunks):
            launch(t + 1, *got[t], pin)
        start, count = (n * blocks // deep for n in (sum(n for n, _ in chunks[:t]), chunks[t][0]))
        rest = count % 4
        low = 0
        for part in (count - rest, rest) if rest else (count,):
            denoised, *send, keep = second_call(
                me, got[t], w_second, cotangent, hidden, denoised, start + low, low, part
            )
            sum_cells(1, start + low, send, keep)
            low += part
        pin = shares[1]
    return (denoised, *shares)


def solution(mesh):
    placed = (
        P(("grp", "cell"), "gene"),
        P(("grp", "cell"), "gene"),
        P("gene"),
        P("gene", None),
        P(None, "gene"),
        P("gene", None, None),
        P("gene", None, None),
        P(("grp", "cell"), "gene"),
    )
    four = mesh.shape["gene"] == 4 and mesh.shape["cell"] == 4
    return jax.shard_map(
        on_device_four if four else on_device_general,
        mesh=mesh,
        in_specs=placed,
        out_specs=(
            P(("grp", "cell"), "gene"),
            P(("grp", "gene"), "cell", None),
            P(("grp", "gene"), "cell", None),
        ),
        check_vma=False,
    )
```
